128 devices in a mesh: dp: 4 (over x_hi, core), section: 2 (over x_lo), seq: 16 (over z, y).
Axes of the slice: x: 4 (x_hi: 2, x_lo: 2; x = x_hi * 2 + x_lo), y: 4, z: 4, core: 2. Of those that a mesh axis runs over, the one named last changes fastest.
Arguments:
- streams: bfloat16 [2, 4, 2048, 1152], P('section', 'dp', 'seq'), may hold values from -30 to 30
- modulation: float32 [2, 2, 3, 1152], P('section'), may hold values from -2 to 2, as said below
- w_qkv: bfloat16 [2, 2, 16, 3, 72, 1152], P('section', None, 'seq'), may hold values from -2 to 2
- w_out: bfloat16 [2, 2, 16, 72, 1152], P('section', None, 'seq'), may hold values from -0.1875 to 0.1875
- w_zero: bfloat16 [2, 1152, 1152], replicated, may hold values from -0.1875 to 0.1875
- pairing: int32 [4, 2], P('dp'), may hold values from 0 to 1, as said below
- positions: int32 [2048], P('seq'), may hold values from 0 to 2047, each once
- cotangent: bfloat16 [4, 2048, 1152], P('dp', 'seq'), may hold values from -0.59765625 to 0.59765625
Outputs:
- final: bfloat16 [2, 4, 2048, 1152], P('section', 'dp', 'seq')
- stream_grads: float32 [2, 4, 2048, 1152], P('section', 'dp', 'seq')
- grad_qkv: float32 [2, 2, 16, 3, 72, 1152], P('section', None, 'seq')
- grad_out: float32 [2, 2, 16, 72, 1152], P('section', None, 'seq')
The draws below stay inside these ranges and needn't reach their ends.
Inputs may be any that keep to these rules, and one draw needn't show every extreme that they name: `modulation`: entries 0, 1, 2 of the third dimension are shift, scale and gate; gates are positive. pairing[b, j] >= j for every sequence b and control block j.
All inputs are finite; a program needn't handle non-finite values.
Results may differ from the reference program's by a relative error of at most 0.03.
Values may be sent and summed in bfloat16 or wider, within the bound.
No kernel may reach another device: no remote copies, remote signals or barrier semaphores. Data moves between devices by JAX's collectives and lax.ppermute only.
A program may use at most 192 MiB of HBM per device.

```python
import math
import jax
import jax.numpy as jnp
from jax import lax

D = 1152
HEADS = 16
HS = 72
NB = 2
GRID_W = 128
LENGTH = 2048
BATCH = 4
N_SEQ = 16


def draw_streams(key, part):
    key = jax.random.fold_in(key, 11)
    base_key = jax.random.fold_in(key, 0)
    dims_out = (2, BATCH, LENGTH, D)
    values = jnp.clip(jax.random.normal(base_key, dims_out, jnp.float32), -6.0, 6.0)
    return values.astype(jnp.bfloat16)


def draw_modulation(key, part):
    key = jax.random.fold_in(key, 12)
    shift_key, scale_key, gate_key = jax.random.split(key, 3)
    dims_out = (2, NB, 1, D)
    shift_part = 0.4 * jnp.clip(jax.random.normal(shift_key, dims_out, jnp.float32), -2.0, 2.0)
    scale_part = jax.random.uniform(scale_key, dims_out, jnp.float32, -0.5, 0.5)
    gate_part = jax.random.uniform(gate_key, dims_out, jnp.float32, 0.5, 1.5)
    return jnp.concatenate([shift_part, scale_part, gate_part], axis=2)


def draw_w_qkv(key, part):
    key = jax.random.fold_in(key, 13)
    base_key = jax.random.fold_in(key, 0)
    dims_out = (2, NB, HEADS, 3, HS, D)
    values = jnp.clip(jax.random.normal(base_key, dims_out, jnp.float32), -6.0, 6.0) / math.sqrt(D)
    return values.astype(jnp.bfloat16)


def draw_pairing(key, part):
    key = jax.random.fold_in(key, 14)
    spans = NB - jnp.arange(NB, dtype=jnp.int32)
    picks = jax.random.randint(key, (BATCH, NB), 0, 1 << 20, dtype=jnp.int32) % spans[None, :]
    return (jnp.arange(NB, dtype=jnp.int32)[None, :] + picks).astype(jnp.int32)


def levels(own_key, shape, pieces, smallest, top_value):
    level = 1.0
    for axis_at, shards_of in pieces:
        steps = jax.random.uniform(jax.random.fold_in(jax.random.fold_in(own_key, 6), axis_at), (shards_of,), jnp.float32, smallest / len(pieces), top_value / len(pieces))
        level = level * jnp.repeat(jnp.exp(steps), shape[axis_at] // shards_of).reshape((-1,) + (1,) * (len(shape) - 1 - axis_at))
    return level


def bell_draw(own_key, shape, scale, most, cuts=(), held_as=jnp.bfloat16):
    array = jax.random.normal(own_key, shape, jnp.float32) * scale
    if len(cuts) > 0:
        array = levels(own_key, shape, cuts, -0.22, 0.18) * array
    return jnp.clip(array, min=-most, max=most).astype(held_as)


def setup_inputs(seed: int = 0) -> dict:
    keys = jax.random.split(jax.random.key(seed), 9)
    return {
        "streams": draw_streams(jax.random.fold_in(keys[8], 71), 0),
        "modulation": draw_modulation(jax.random.fold_in(keys[8], 71), 0),
        "w_qkv": draw_w_qkv(jax.random.fold_in(keys[8], 71), 0),
        "w_out": bell_draw(keys[3], (2, NB, HEADS, HS, D), D ** -0.5, 0.1875, ((0, 2), (2, 16))),
        "w_zero": bell_draw(keys[4], (NB, D, D), D ** -0.5, 0.1875),
        "pairing": draw_pairing(jax.random.fold_in(keys[8], 71), 0),
        "positions": jax.random.permutation(keys[6], LENGTH).astype(jnp.int32),
        "cotangent": bell_draw(keys[7], (BATCH, LENGTH, D), 0.1, 0.59765625, ((0, 4), (1, 16))),
    }


norm_eps = 1e-06

def angle_tables(places, head_size):
    quarter = head_size // 4
    grid_rows = (places // GRID_W).astype(jnp.float32)
    grid_cols = (places % GRID_W).astype(jnp.float32)
    freqs = jnp.exp(-math.log(10000.0) * jnp.arange(quarter, dtype=jnp.float32) / quarter)
    row_angle = grid_rows[:, None] * freqs[None, :]
    col_angle = grid_cols[:, None] * freqs[None, :]
    return (jnp.cos(row_angle), jnp.sin(row_angle), jnp.cos(col_angle), jnp.sin(col_angle))

def expand(table_in, rank_count):
    return table_in.reshape(table_in.shape[:1] + (1,) * (rank_count - 2) + table_in.shape[1:])

def turn_half(part_vals, cosine, sine_tab):
    quarter = cosine.shape[1]
    cosine = expand(cosine, part_vals.ndim)
    sine_tab = expand(sine_tab, part_vals.ndim)
    first_half = part_vals[..., :quarter]
    second_half = part_vals[..., quarter:]
    return jnp.concatenate([first_half * cosine - second_half * sine_tab, first_half * sine_tab + second_half * cosine], axis=-1)

def rotate(values, tables):
    middle = values.shape[-1] // 2
    return jnp.concatenate([turn_half(values[..., :middle], tables[0], tables[1]), turn_half(values[..., middle:], tables[2], tables[3])], axis=-1)

def unrotate(values, tables):
    return rotate(values, (tables[0], -tables[1], tables[2], -tables[3]))

def rope_qkv(raw_proj, tables):
    turned = rotate(raw_proj[:, :, :2], tables)
    return jnp.concatenate([turned, raw_proj[:, :, 2:]], axis=2).astype(jnp.bfloat16)

def attend_head(head_qkv):
    head_size = head_qkv.shape[2]
    scores = lax.dot_general(head_qkv[:, 0], head_qkv[:, 1], (((1,), (1,)), ((), ())), preferred_element_type=jnp.float32) / math.sqrt(head_size)
    weights = jax.nn.softmax(scores, axis=-1).astype(jnp.bfloat16)
    return jnp.dot(weights, head_qkv[:, 2], preferred_element_type=jnp.float32).astype(jnp.bfloat16)

def back_head(head_qkv, grad_heads, tables):
    head_size = head_qkv.shape[2]
    query = head_qkv[:, 0]
    keys_in = head_qkv[:, 1]
    values_in = head_qkv[:, 2]
    scores = lax.dot_general(query, keys_in, (((1,), (1,)), ((), ())), preferred_element_type=jnp.float32) / math.sqrt(head_size)
    probs = jax.nn.softmax(scores, axis=-1)
    grad_values = lax.dot_general(probs.astype(jnp.bfloat16), grad_heads, (((0,), (0,)), ((), ())), preferred_element_type=jnp.float32)
    grad_probs = lax.dot_general(grad_heads, values_in, (((1,), (1,)), ((), ())), preferred_element_type=jnp.float32)
    centred = grad_probs - lax.optimization_barrier(jnp.sum(probs * grad_probs, axis=-1, keepdims=True))
    grad_scores = (probs * centred / math.sqrt(head_size)).astype(jnp.bfloat16)
    grad_query = jnp.dot(grad_scores, keys_in, preferred_element_type=jnp.float32)
    grad_keys = lax.dot_general(grad_scores, query, (((0,), (0,)), ((), ())), preferred_element_type=jnp.float32)
    return jnp.stack([unrotate(grad_query, tables), unrotate(grad_keys, tables), grad_values], axis=1)

def modulated_norm(hidden, shift_vec, scale_vec):
    centre = hidden - lax.optimization_barrier(jnp.mean(hidden, axis=-1, keepdims=True))
    spread = lax.optimization_barrier(jnp.mean(centre * centre, axis=-1, keepdims=True))
    return centre * lax.rsqrt(spread + norm_eps) * (1.0 + scale_vec) + shift_vec

def grouped_sum(rows_in, weight, groups):
    count_rows = rows_in.shape[0]
    parts = jnp.einsum('ngc,gcd->ngd', rows_in.reshape(count_rows, groups, -1).astype(jnp.float32), weight.reshape(groups, -1, weight.shape[1]).astype(jnp.float32), precision=lax.Precision.HIGHEST)
    rounded = lax.optimization_barrier(parts.astype(jnp.bfloat16))
    return lax.optimization_barrier(jnp.sum(rounded.astype(jnp.float32), axis=1))

def block_forward(hidden, tables, mods, qkv_w, out_w, groups):
    length = hidden.shape[0]
    heads_all = qkv_w.shape[0]
    head_size = qkv_w.shape[2]
    width = qkv_w.shape[3]
    normed = modulated_norm(hidden, mods[0], mods[1]).astype(jnp.bfloat16)
    raw_proj = lax.dot_general(normed, qkv_w.reshape(heads_all * 3 * head_size, width), (((1,), (1,)), ((), ())), preferred_element_type=jnp.float32)
    qkv_rot = rope_qkv(raw_proj.reshape(length, heads_all, 3, head_size), tables)
    head_outs = lax.map(attend_head, jnp.moveaxis(qkv_rot, 1, 0))
    mixed_heads = jnp.moveaxis(head_outs, 0, 1).reshape(length, heads_all * head_size)
    attn_sum = grouped_sum(mixed_heads, out_w.reshape(heads_all * head_size, width), groups)
    return (hidden + mods[2] * attn_sum, (normed, qkv_rot, mixed_heads))

def block_backward(grad_flow, hidden, kept, tables, mods, qkv_w, out_w, groups):
    normed, qkv_rot, mixed_heads = kept
    length = hidden.shape[0]
    heads_all = qkv_w.shape[0]
    head_size = qkv_w.shape[2]
    width = qkv_w.shape[3]
    d_attn = (mods[2] * grad_flow).astype(jnp.bfloat16)
    d_mixed = lax.dot_general(d_attn, out_w.reshape(heads_all * head_size, width), (((1,), (1,)), ((), ())), preferred_element_type=jnp.float32).astype(jnp.bfloat16)
    head_grads = lax.map(lambda pair_in: back_head(pair_in[0], pair_in[1], tables), (jnp.moveaxis(qkv_rot, 1, 0), jnp.moveaxis(d_mixed.reshape(length, heads_all, head_size), 1, 0)))
    d_raw = jnp.moveaxis(head_grads, 0, 1).reshape(length, heads_all * 3 * head_size).astype(jnp.bfloat16)
    qkv_rows = qkv_w.reshape(heads_all * 3 * head_size, width)
    grad_qkv_w = lax.dot_general(d_raw, normed, (((0,), (0,)), ((), ())), preferred_element_type=jnp.float32)
    grad_out_w = lax.dot_general(mixed_heads, d_attn, (((0,), (0,)), ((), ())), preferred_element_type=jnp.float32)
    d_normed = grouped_sum(d_raw, qkv_rows, groups)
    norm_back = jax.vjp(lambda inner: modulated_norm(inner, mods[0], mods[1]), hidden)[1](d_normed)[0]
    return (grad_flow + norm_back, grad_qkv_w, grad_out_w)

def reference(streams, modulation, w_qkv, w_out, w_zero, pairing, positions, cotangent):
    tables = angle_tables(positions, HS)
    groups = N_SEQ
    qkv_total = jnp.zeros((2, NB, HEADS * 3 * HS, D), jnp.float32)
    out_total = jnp.zeros((2, NB, HEADS * HS, D), jnp.float32)
    finals_ctrl = []
    finals_main = []
    grads_ctrl = []
    grads_main = []
    for batch_index in range(BATCH):
        hidden = streams[0, batch_index].astype(jnp.float32)
        ctrl_kept = []
        zero_outs = []
        for block_index in range(NB):
            new_state, kept = block_forward(hidden, tables, modulation[0, block_index], w_qkv[0, block_index], w_out[0, block_index], groups)
            ctrl_kept.append((hidden, kept))
            hidden = new_state
            zero_outs.append(jnp.dot(hidden.astype(jnp.bfloat16), w_zero[block_index], preferred_element_type=jnp.float32).astype(jnp.bfloat16))
        finals_ctrl.append(hidden.astype(jnp.bfloat16))
        hidden = streams[1, batch_index].astype(jnp.float32)
        main_kept = []
        for block_index in range(NB):
            new_state, kept = block_forward(hidden, tables, modulation[1, block_index], w_qkv[1, block_index], w_out[1, block_index], groups)
            main_kept.append((hidden, kept))
            for source in range(NB):
                new_state = new_state + jnp.where(pairing[batch_index, source] == block_index, zero_outs[source].astype(jnp.float32), 0.0)
            hidden = new_state
        finals_main.append(hidden.astype(jnp.bfloat16))
        grad_flow = cotangent[batch_index].astype(jnp.float32)
        sends = [None] * NB
        for block_index in reversed(range(NB)):
            sends[block_index] = grad_flow.astype(jnp.bfloat16)
            hidden_in, kept = main_kept[block_index]
            grad_flow, grad_qkv_w, grad_out_w = block_backward(grad_flow, hidden_in, kept, tables, modulation[1, block_index], w_qkv[1, block_index], w_out[1, block_index], groups)
            qkv_total = qkv_total.at[1, block_index].add(grad_qkv_w)
            out_total = out_total.at[1, block_index].add(grad_out_w)
        grads_main.append(grad_flow)
        grad_flow = jnp.zeros((LENGTH, D), jnp.float32)
        for block_index in reversed(range(NB)):
            picked = jnp.zeros((LENGTH, D), jnp.float32)
            for target in range(NB):
                picked = picked + jnp.where(pairing[batch_index, block_index] == target, sends[target].astype(jnp.float32), 0.0)
            grad_flow = grad_flow + lax.dot_general(picked.astype(jnp.bfloat16), w_zero[block_index], (((1,), (1,)), ((), ())), preferred_element_type=jnp.float32)
            hidden_in, kept = ctrl_kept[block_index]
            grad_flow, grad_qkv_w, grad_out_w = block_backward(grad_flow, hidden_in, kept, tables, modulation[0, block_index], w_qkv[0, block_index], w_out[0, block_index], groups)
            qkv_total = qkv_total.at[0, block_index].add(grad_qkv_w)
            out_total = out_total.at[0, block_index].add(grad_out_w)
        grads_ctrl.append(grad_flow)
    final = jnp.stack([jnp.stack(finals_ctrl), jnp.stack(finals_main)])
    stream_grads = jnp.stack([jnp.stack(grads_ctrl), jnp.stack(grads_main)])
    return (final, stream_grads, qkv_total.reshape(2, NB, HEADS, 3, HS, D), out_total.reshape(2, NB, HEADS, HS, D))
```

```python
import math

import jax
import jax.numpy as jnp
from jax import lax
from jax.experimental import pallas as pl
from jax.experimental.pallas import tpu as pltpu
from jax.sharding import PartitionSpec as P

GRID_W = 128
HS = 72
HP = 80
HALF = 40
QB = 256
TB = 128
SCALE = 1.0 / math.sqrt(HS)
EXP_SCALE = math.log2(math.e) / math.sqrt(HS)

norm_eps = 1e-06
bf = jnp.bfloat16
f32 = jnp.float32


def nn(a, b):
    return lax.dot_general(a, b, (((1,), (0,)), ((), ())), preferred_element_type=f32)


def nt(a, b):
    return lax.dot_general(a, b, (((1,), (1,)), ((), ())), preferred_element_type=f32)


def tn(a, b):
    return lax.dot_general(a, b, (((0,), (0,)), ((), ())), preferred_element_type=f32)


def flat(ref, to_ref):
    for j in range(ref.shape[0]):
        to_ref[:, j * TB : (j + 1) * TB] = ref[j]


def put(ref, i, value):
    for j in range(QB // TB):
        ref[i * (QB // TB) + j] = value[:, j * TB : (j + 1) * TB]


def turn_back(x, c, s):
    a, b = x[:HALF], x[HALF:]
    return jnp.concatenate([a * c + b * s, b * c - a * s], axis=0)


def with_ones(v):
    rows = lax.broadcasted_iota(jnp.int32, v.shape, 0)
    return jnp.where(rows == HS, 1.0, v.astype(f32)).astype(bf)


def fwd_kernel(x_ref, o_ref, l_ref, kt_ref, vo_ref):
    i = pl.program_id(0)

    @pl.when(i == 0)
    def _():
        kt_ref[...] = x_ref[HP : 2 * HP].astype(f32).T.astype(bf)
        vo_ref[...] = with_ones(x_ref[2 * HP :])

    s = nn(kt_ref[...], x_ref[:HP, pl.ds(pl.multiple_of(i * QB, QB), QB)])
    m = jnp.max(s, axis=0, keepdims=True)
    e = jnp.exp2((s - m) * EXP_SCALE).astype(bf)
    o = nn(vo_ref[...], e)
    total = o[HS : HS + 1]
    rows = lax.broadcasted_iota(jnp.int32, o.shape, 0)
    put(o_ref, i, jnp.where(rows < HS, o * (1.0 / total), 0.0).astype(bf))
    l_ref[...] = m * EXP_SCALE + jnp.log2(total)


def attn_fwd(x):
    n = x.shape[1]
    return pl.pallas_call(
        fwd_kernel,
        grid=(n // QB,),
        in_specs=[pl.BlockSpec((3 * HP, n), lambda i: (0, 0))],
        out_specs=[
            pl.BlockSpec((n // TB, HP, TB), lambda i: (0, 0, 0)),
            pl.BlockSpec((1, QB), lambda i: (0, i)),
        ],
        out_shape=[jax.ShapeDtypeStruct((n // TB, HP, TB), bf), jax.ShapeDtypeStruct((1, n), f32)],
        scratch_shapes=[pltpu.VMEM((n, HP), bf), pltpu.VMEM((HP, n), bf)],
        compiler_params=pltpu.CompilerParams(vmem_limit_bytes=40 * 2**20),
        cost_estimate=pl.CostEstimate(flops=4 * n * n * 256, bytes_accessed=2 * 4 * HP * n, transcendentals=n * n),
        name="attn_fwd",
    )(x)


def prep(x_ref, kt_ref, vt_ref, dk_ref, dv_ref):
    kt_ref[...] = x_ref[HP : 2 * HP].astype(f32).T.astype(bf)
    vt_ref[...] = x_ref[2 * HP :].astype(f32).T.astype(bf)
    dk_ref[...] = jnp.zeros_like(dk_ref)
    dv_ref[...] = jnp.zeros_like(dv_ref)


def finish(i, dq, c_ref, s_ref, d_ref, db_ref, dk_ref, dv_ref):
    at = pl.ds(pl.multiple_of(i * QB, QB), QB)
    d_ref[:HP, at] = turn_back(dq * SCALE, c_ref[:, at], s_ref[:, at]).astype(bf)

    @pl.when(i == pl.num_programs(0) - 1)
    def _():
        d_ref[HP : 2 * HP, :] = turn_back(dk_ref[...].T * SCALE, c_ref[...], s_ref[...]).astype(bf)
        d_ref[2 * HP :, :] = dv_ref[...].T.astype(bf)
        for j in range(db_ref.shape[0]):
            db_ref[j] = d_ref[:, j * TB : (j + 1) * TB]


def bwd_kernel(x_ref, g_ref, o_ref, l_ref, c_ref, s_ref, d_ref, db_ref, kt_ref, vt_ref, dk_ref, dv_ref, gx_ref, ox_ref):
    i = pl.program_id(0)

    @pl.when(i == 0)
    def _():
        prep(x_ref, kt_ref, vt_ref, dk_ref, dv_ref)
        flat(g_ref, gx_ref)
        flat(o_ref, ox_ref)

    at = pl.ds(pl.multiple_of(i * QB, QB), QB)
    q = x_ref[:HP, at]
    g = gx_ref[:, at]
    p = jnp.exp2(nn(kt_ref[...], q) * EXP_SCALE - l_ref[...])
    delta = jnp.sum(g.astype(f32) * ox_ref[:, at].astype(f32), axis=0, keepdims=True)
    ds = (p * (nn(vt_ref[...], g) - delta)).astype(bf)
    dv_ref[...] += nt(p.astype(bf), g)
    dk_ref[...] += nt(ds, q)
    finish(i, nn(x_ref[HP : 2 * HP], ds), c_ref, s_ref, d_ref, db_ref, dk_ref, dv_ref)


def both_kernel(xb_ref, gb_ref, c_ref, s_ref, o_ref, d_ref, db_ref, kt_ref, vt_ref, dk_ref, dv_ref, x_ref, g_ref, vo_ref):
    i = pl.program_id(0)

    @pl.when(i == 0)
    def _():
        flat(xb_ref, x_ref)
        flat(gb_ref, g_ref)
        prep(x_ref, kt_ref, vt_ref, dk_ref, dv_ref)
        vo_ref[...] = with_ones(x_ref[2 * HP :])

    at = pl.ds(pl.multiple_of(i * QB, QB), QB)
    q = x_ref[:HP, at]
    s = nn(kt_ref[...], q)
    m = jnp.max(s, axis=0, keepdims=True)
    e = jnp.exp2((s - m) * EXP_SCALE)
    eb = e.astype(bf)
    o = nn(vo_ref[...], eb)
    inv = 1.0 / o[HS : HS + 1]
    rows = lax.broadcasted_iota(jnp.int32, o.shape, 0)
    o = jnp.where(rows < HS, o * inv, 0.0)
    put(o_ref, i, o.astype(bf))
    g = g_ref[:, at].astype(f32) * inv
    delta = jnp.sum(g * o, axis=0, keepdims=True)
    g = g.astype(bf)
    ds = (e * (nn(vt_ref[...], g) - delta)).astype(bf)
    dv_ref[...] += nt(eb, g)
    dk_ref[...] += nt(ds, q)
    finish(i, nn(x_ref[HP : 2 * HP], ds), c_ref, s_ref, d_ref, db_ref, dk_ref, dv_ref)


def whole(x):
    zeros = (0,) * x.ndim
    return pl.BlockSpec(x.shape, lambda i: zeros)


def back_call(kernel, ins, in_specs, n, extra_out, extra_scratch, name):
    d_shapes = [jax.ShapeDtypeStruct((3 * HP, n), bf), jax.ShapeDtypeStruct((n // TB, 3 * HP, TB), bf)]
    out_shape = extra_out + d_shapes
    scratch = [pltpu.VMEM((n, HP), bf), pltpu.VMEM((n, HP), bf), pltpu.VMEM((n, HP), f32), pltpu.VMEM((n, HP), f32)]
    return pl.pallas_call(
        kernel,
        grid=(n // QB,),
        in_specs=in_specs,
        out_specs=[whole(x) for x in out_shape],
        out_shape=out_shape,
        scratch_shapes=scratch + extra_scratch,
        compiler_params=pltpu.CompilerParams(vmem_limit_bytes=48 * 2**20),
        cost_estimate=pl.CostEstimate(flops=10 * n * n * 256, bytes_accessed=2 * 12 * HP * n, transcendentals=n * n),
        name=name,
    )(*ins)


def attn_bwd(x, g, o, l, c, s):
    n = x.shape[1]
    specs = [whole(x), whole(g), whole(o), pl.BlockSpec((1, QB), lambda i: (0, i)), whole(c), whole(s)]
    extra = [pltpu.VMEM((HP, n), bf), pltpu.VMEM((HP, n), bf)]
    return back_call(bwd_kernel, (x, g, o, l, c, s), specs, n, [], extra, "attn_bwd")


def attn_both(x, g, c, s):
    n = x.shape[0] * TB
    extra = [pltpu.VMEM((3 * HP, n), bf), pltpu.VMEM((HP, n), bf), pltpu.VMEM((HP, n), bf)]
    out = [jax.ShapeDtypeStruct((n // TB, HP, TB), bf)]
    return back_call(both_kernel, (x, g, c, s), [whole(x), whole(g), whole(c), whole(s)], n, out, extra, "attn_both")


def swap(value, axis, bit):
    count = lax.axis_size(axis)
    return lax.ppermute(value, axis, [(i, i ^ bit) for i in range(count)])


def shifted(value, axis, by):
    count = lax.axis_size(axis)
    pairs = [(i, i + by) for i in range(count) if 0 <= i + by < count]
    return lax.ppermute(value, axis, pairs)


def scatter_heads(value):
    return lax.all_to_all(value, "seq", split_axis=0, concat_axis=0, tiled=True)


def angle_tables(places):
    quarter = HS // 4
    freqs = jnp.exp(-math.log(10000.0) * jnp.arange(quarter, dtype=f32) / quarter)
    grid_rows = (places // GRID_W).astype(f32)
    grid_cols = (places % GRID_W).astype(f32)
    angles = jnp.concatenate(
        [
            freqs[:, None] * grid_rows[None, :],
            freqs[:, None] * grid_cols[None, :],
            jnp.zeros((HALF - 2 * quarter, places.shape[0]), f32),
        ],
        axis=0,
    )
    return jnp.cos(angles), jnp.sin(angles)


def pad_rows(x, count):
    return jnp.pad(x, ((0, count - x.shape[0]), (0, 0)))


def arrange(w):
    qt = HS // 4
    parts = []
    for part in (w[0], w[1]):
        parts += [pad_rows(jnp.concatenate([part[0:qt], part[2 * qt : 3 * qt]]), HALF)]
        parts += [pad_rows(jnp.concatenate([part[qt : 2 * qt], part[3 * qt :]]), HALF)]
    return jnp.concatenate(parts + [pad_rows(w[2], HP)], axis=0)


def disarrange(g):
    qt = HS // 4
    parts = []
    for at in (0, HP):
        a, b = g[at : at + HALF], g[at + HALF : at + HP]
        parts += [a[:qt], b[:qt], a[qt : 2 * qt], b[qt : 2 * qt]]
    return jnp.concatenate(parts + [g[2 * HP : 2 * HP + HS]], axis=0).reshape(3, HS, g.shape[1])


def rope(qa, qb, ka, kb, v, c, s):
    return jnp.concatenate([qa * c - qb * s, qa * s + qb * c, ka * c - kb * s, ka * s + kb * c, v], axis=-2).astype(bf)


def modulated_norm(hidden, shift_vec, scale_vec):
    centre = hidden - jnp.mean(hidden, axis=-1, keepdims=True)
    spread = jnp.mean(centre * centre, axis=-1, keepdims=True)
    return centre * lax.rsqrt(spread + norm_eps) * (1.0 + scale_vec) + shift_vec


def norm_back(hidden, scale_vec, grad):
    centre = hidden - jnp.mean(hidden, axis=-1, keepdims=True)
    inv = lax.rsqrt(jnp.mean(centre * centre, axis=-1, keepdims=True) + norm_eps)
    unit = centre * inv
    grad = grad * (1.0 + scale_vec)
    return inv * (grad - jnp.mean(grad, axis=-1, keepdims=True) - unit * jnp.mean(grad * unit, axis=-1, keepdims=True))


def dp_sum(value):
    own = value.astype(bf)
    both = (own.astype(f32) + swap(own, "dp", 1).astype(f32)).astype(bf)
    return both.astype(f32) + swap(both, "dp", 2).astype(f32)


def local(streams, modulation, w_qkv, w_out, w_zero, pairing, positions, cotangent):
    on_main = lax.axis_index("section") == 1
    core = lax.axis_index("dp") % 2
    first = core == 0
    mods = modulation[0]
    pair_row = pairing[0]
    width = streams.shape[-1]
    seqs = lax.axis_size("seq")
    qkv_w = [arrange(w_qkv[0, k, 0]) for k in range(2)]
    out_w = [pad_rows(w_out[0, k, 0], HP) for k in range(2)]

    def own_half(w):
        rows = w.shape[0] // 2
        return lax.dynamic_slice_in_dim(w, core * rows, rows, axis=0)

    def gather(x):
        return lax.all_gather(x, "seq", axis=0, tiled=False)

    def rows_of(w):
        return w.reshape(-1, width)

    def halves_of(x):
        rows = x.shape[1] // 2
        low, high = x[:, :rows], x[:, rows:]
        mine = jnp.where(first, low, high)
        theirs = jnp.where(first, high, low)
        return mine.reshape(-1, x.shape[2]), theirs.reshape(-1, x.shape[2])

    def to_heads(w_pair, x):
        mine, theirs = [nt(rows_of(w), x).reshape(seqs, -1, x.shape[0]) for w in w_pair]
        return jnp.where(first, mine, theirs), jnp.where(first, theirs, mine)

    def from_heads(w_pair, x):
        mine, theirs = halves_of(x)
        return tn(mine, rows_of(w_pair[0])) + tn(theirs, rows_of(w_pair[1]))

    hidden0 = streams[0, 0].astype(f32)
    normed0 = modulated_norm(hidden0, mods[0, 0], mods[0, 1]).astype(bf)
    normed0_all = gather(normed0).reshape(-1, width)
    piece_1 = gather(jnp.concatenate([own_half(out_w[0]), own_half(out_w[1]), own_half(qkv_w[1])], axis=0))
    cuts = (HP // 2, HP, HP + 3 * HP // 2)

    def with_other(x):
        return (x, swap(x, "dp", 1))

    out_full0 = with_other(piece_1[:, : cuts[0]])
    out_full1 = with_other(piece_1[:, cuts[0] : cuts[1]])
    qkv_full1 = with_other(piece_1[:, cuts[1] :])

    everywhere = scatter_heads(jnp.broadcast_to(positions[None, None, :], (seqs, 1, positions.shape[0])))
    cos_all, sin_all = angle_tables(everywhere.reshape(-1))
    cos_own, sin_own = angle_tables(positions)

    cot = cotangent[0]
    through = nt(cot, w_zero[1])
    grad2 = jnp.where(on_main, cot.astype(f32), jnp.where(pair_row[1] == 1, through, 0.0))
    d_attn1 = (mods[1, 2] * grad2).astype(bf)
    low, high = to_heads(out_full1, d_attn1)
    d_mixed1 = scatter_heads(jnp.concatenate([low, high], axis=1).astype(bf))

    raw = nt(qkv_w[0], normed0_all)
    qkv0 = rope(raw[:HALF], raw[HALF:HP], raw[HP : HP + HALF], raw[HP + HALF : 2 * HP], raw[2 * HP :], cos_all, sin_all)
    mixed0, log_sums0 = attn_fwd(qkv0)
    attn0 = from_heads(out_full0, scatter_heads(mixed0))
    hidden1 = hidden0 + mods[0, 2] * attn0
    zero0 = shifted(nn(hidden1.astype(bf), w_zero[0]).astype(bf), "section", 1).astype(f32)
    hidden1 = hidden1 + jnp.where(pair_row[0] == 0, zero0, 0.0)

    normed1 = modulated_norm(hidden1, mods[1, 0], mods[1, 1]).astype(bf)
    low, high = to_heads(qkv_full1, normed1)
    qkv1 = rope(low[:, :HALF], low[:, HALF:HP], low[:, HP:], high[:, :HALF], high[:, HALF:], cos_own, sin_own)
    mixed1, d_raw1, d_raw1_blocks = attn_both(scatter_heads(qkv1), d_mixed1, cos_all, sin_all)
    d_normed1 = from_heads(qkv_full1, scatter_heads(d_raw1_blocks))
    grad1 = grad2 + norm_back(hidden1, mods[1, 1], d_normed1)

    attn1 = from_heads(out_full1, scatter_heads(mixed1))
    hidden2 = hidden1 + mods[1, 2] * attn1
    zero1 = shifted(nn(hidden2.astype(bf), w_zero[1]).astype(bf), "section", 1).astype(f32)
    hidden2 = hidden2 + jnp.where(pair_row[0] == 1, zero0, 0.0) + jnp.where(pair_row[1] == 1, zero1, 0.0)
    final_out = hidden2.astype(bf)[None, None]

    sent = shifted(grad1.astype(bf), "section", -1)
    picked = jnp.where(pair_row[0] == 0, sent, cot)
    picked = jnp.where(on_main, jnp.zeros_like(picked), picked)
    grad1 = grad1 + nt(picked, w_zero[0])
    d_attn0 = (mods[0, 2] * grad1).astype(bf)
    low, high = to_heads(out_full0, d_attn0)
    d_mixed0 = scatter_heads(jnp.concatenate([low, high], axis=1).astype(bf))
    d_raw0, d_raw0_blocks = attn_bwd(qkv0, d_mixed0, mixed0, log_sums0, cos_all, sin_all)
    later = gather(jnp.concatenate([d_attn1, normed1, own_half(qkv_w[0])], axis=0))
    qkv_full0 = with_other(later[:, 2 * TB :])
    d_normed0 = from_heads(qkv_full0, scatter_heads(d_raw0_blocks))
    grad0 = grad1 + norm_back(hidden0, mods[0, 1], d_normed0)

    d_attn1_all = later[:, :TB].reshape(-1, width)
    normed1_all = later[:, TB : 2 * TB].reshape(-1, width)
    d_attn0_all = gather(d_attn0).reshape(-1, width)

    def tokens_last(x):
        return jnp.moveaxis(x, 0, 1).reshape(x.shape[1], -1)

    block_1 = dp_sum(jnp.concatenate([nn(d_raw1, normed1_all), nn(tokens_last(mixed1), d_attn1_all)], axis=0))
    qkv_grad0 = dp_sum(nn(d_raw0, normed0_all))
    out_grad0 = dp_sum(nn(tokens_last(mixed0), d_attn0_all))
    grad_qkv = jnp.stack([disarrange(qkv_grad0), disarrange(block_1[: 3 * HP])])[None, :, None]
    grad_out = jnp.stack([out_grad0[:HS], block_1[3 * HP : 3 * HP + HS]])[None, :, None]
    return (final_out, grad0[None, None], grad_qkv, grad_out)


def solution(mesh):
    in_specs = (
        P("section", "dp", "seq", None),
        P("section", None, None, None),
        P("section", None, "seq", None, None, None),
        P("section", None, "seq", None, None),
        P(),
        P("dp", None),
        P("seq"),
        P("dp", "seq", None),
    )
    out_specs = (
        P("section", "dp", "seq", None),
        P("section", "dp", "seq", None),
        P("section", None, "seq", None, None, None),
        P("section", None, "seq", None, None),
    )
    return jax.shard_map(local, mesh=mesh, in_specs=in_specs, out_specs=out_specs, check_vma=False)
```

```python
import math

import jax
import jax.numpy as jnp
from jax import lax
from jax.experimental import pallas as pl
from jax.experimental.pallas import tpu as pltpu
from jax.sharding import PartitionSpec as P

GRID_W = 128
HS = 72
HP = 80
HALF = 40
QB = 256
TB = 128
SCALE = 1.0 / math.sqrt(HS)
EXP_SCALE = math.log2(math.e) / math.sqrt(HS)

norm_eps = 1e-06
bf = jnp.bfloat16
f32 = jnp.float32


def nn(a, b):
    return lax.dot_general(a, b, (((1,), (0,)), ((), ())), preferred_element_type=f32)


def nt(a, b):
    return lax.dot_general(a, b, (((1,), (1,)), ((), ())), preferred_element_type=f32)


def tn(a, b):
    return lax.dot_general(a, b, (((0,), (0,)), ((), ())), preferred_element_type=f32)


def flat(ref, to_ref):
    for j in range(ref.shape[0]):
        to_ref[:, j * TB : (j + 1) * TB] = ref[j]


def put(ref, i, value):
    for j in range(QB // TB):
        ref[i * (QB // TB) + j] = value[:, j * TB : (j + 1) * TB]


def turn_back(x, c, s):
    a, b = x[:HALF], x[HALF:]
    return jnp.concatenate([a * c + b * s, b * c - a * s], axis=0)


def with_ones(v):
    rows = lax.broadcasted_iota(jnp.int32, v.shape, 0)
    return jnp.where(rows == HS, 1.0, v.astype(f32)).astype(bf)


def whole(x):
    zeros = (0,) * x.ndim
    return pl.BlockSpec(x.shape, lambda i: zeros)


def fwd_kernel(to_ref, p0_ref, p1_ref, p2_ref, p3_ref, x_ref, o_ref, l_ref, kt_ref, vo_ref):
    i = pl.program_id(0)

    @pl.when(i == 0)
    def _():
        for at, piece in enumerate((p0_ref, p1_ref, p2_ref, p3_ref)):
            for j in range(piece.shape[1] // TB):
                place = pl.multiple_of(to_ref[at * (piece.shape[1] // TB) + j] * TB, TB)
                x_ref[:, pl.ds(place, TB)] = piece[:, j * TB : (j + 1) * TB]
        kt_ref[...] = x_ref[HP : 2 * HP].astype(f32).T.astype(bf)
        vo_ref[...] = with_ones(x_ref[2 * HP :])

    s = nn(kt_ref[...], x_ref[:HP, pl.ds(pl.multiple_of(i * QB, QB), QB)])
    m = jnp.max(s, axis=0, keepdims=True)
    e = jnp.exp2((s - m) * EXP_SCALE).astype(bf)
    o = nn(vo_ref[...], e)
    total = o[HS : HS + 1]
    rows = lax.broadcasted_iota(jnp.int32, o.shape, 0)
    put(o_ref, i, jnp.where(rows < HS, o * (1.0 / total), 0.0).astype(bf))
    l_ref[...] = m * EXP_SCALE + jnp.log2(total)


def attn_fwd(pieces, places):
    n = sum(p.shape[1] for p in pieces)
    return pl.pallas_call(
        fwd_kernel,
        grid=(n // QB,),
        in_specs=[pl.BlockSpec(memory_space=pltpu.SMEM)] + [whole(p) for p in pieces],
        out_specs=[
            pl.BlockSpec((3 * HP, n), lambda i: (0, 0)),
            pl.BlockSpec((n // TB, HP, TB), lambda i: (0, 0, 0)),
            pl.BlockSpec((1, QB), lambda i: (0, i)),
        ],
        out_shape=[
            jax.ShapeDtypeStruct((3 * HP, n), bf),
            jax.ShapeDtypeStruct((n // TB, HP, TB), bf),
            jax.ShapeDtypeStruct((1, n), f32),
        ],
        scratch_shapes=[pltpu.VMEM((n, HP), bf), pltpu.VMEM((HP, n), bf)],
        compiler_params=pltpu.CompilerParams(vmem_limit_bytes=40 * 2**20),
        cost_estimate=pl.CostEstimate(flops=4 * n * n * 256, bytes_accessed=2 * 4 * HP * n, transcendentals=n * n),
        name="attn_fwd",
    )(places, *pieces)


def prep(x_ref, kt_ref, vt_ref, dk_ref, dv_ref):
    kt_ref[...] = x_ref[HP : 2 * HP].astype(f32).T.astype(bf)
    vt_ref[...] = x_ref[2 * HP :].astype(f32).T.astype(bf)
    dk_ref[...] = jnp.zeros_like(dk_ref)
    dv_ref[...] = jnp.zeros_like(dv_ref)


def finish(i, dq, c_ref, s_ref, d_ref, db_ref, dk_ref, dv_ref):
    at = pl.ds(pl.multiple_of(i * QB, QB), QB)
    d_ref[:HP, at] = turn_back(dq * SCALE, c_ref[:, at], s_ref[:, at]).astype(bf)

    @pl.when(i == pl.num_programs(0) - 1)
    def _():
        d_ref[HP : 2 * HP, :] = turn_back(dk_ref[...].T * SCALE, c_ref[...], s_ref[...]).astype(bf)
        d_ref[2 * HP :, :] = dv_ref[...].T.astype(bf)
        for j in range(db_ref.shape[0]):
            db_ref[j] = d_ref[:, j * TB : (j + 1) * TB]


def bwd_kernel(x_ref, g_ref, o_ref, l_ref, c_ref, s_ref, d_ref, db_ref, kt_ref, vt_ref, dk_ref, dv_ref, gx_ref, ox_ref):
    i = pl.program_id(0)

    @pl.when(i == 0)
    def _():
        prep(x_ref, kt_ref, vt_ref, dk_ref, dv_ref)
        flat(g_ref, gx_ref)
        flat(o_ref, ox_ref)

    at = pl.ds(pl.multiple_of(i * QB, QB), QB)
    q = x_ref[:HP, at]
    g = gx_ref[:, at]
    p = jnp.exp2(nn(kt_ref[...], q) * EXP_SCALE - l_ref[...])
    delta = jnp.sum(g.astype(f32) * ox_ref[:, at].astype(f32), axis=0, keepdims=True)
    ds = (p * (nn(vt_ref[...], g) - delta)).astype(bf)
    dv_ref[...] += nt(p.astype(bf), g)
    dk_ref[...] += nt(ds, q)
    finish(i, nn(x_ref[HP : 2 * HP], ds), c_ref, s_ref, d_ref, db_ref, dk_ref, dv_ref)


def both_kernel(xb_ref, gb_ref, c_ref, s_ref, o_ref, d_ref, db_ref, kt_ref, vt_ref, dk_ref, dv_ref, x_ref, g_ref, vo_ref):
    i = pl.program_id(0)

    @pl.when(i == 0)
    def _():
        flat(xb_ref, x_ref)
        flat(gb_ref, g_ref)
        prep(x_ref, kt_ref, vt_ref, dk_ref, dv_ref)
        vo_ref[...] = with_ones(x_ref[2 * HP :])

    at = pl.ds(pl.multiple_of(i * QB, QB), QB)
    q = x_ref[:HP, at]
    s = nn(kt_ref[...], q)
    m = jnp.max(s, axis=0, keepdims=True)
    e = jnp.exp2((s - m) * EXP_SCALE)
    eb = e.astype(bf)
    o = nn(vo_ref[...], eb)
    inv = 1.0 / o[HS : HS + 1]
    rows = lax.broadcasted_iota(jnp.int32, o.shape, 0)
    o = jnp.where(rows < HS, o * inv, 0.0)
    put(o_ref, i, o.astype(bf))
    g = g_ref[:, at].astype(f32) * inv
    delta = jnp.sum(g * o, axis=0, keepdims=True)
    g = g.astype(bf)
    ds = (e * (nn(vt_ref[...], g) - delta)).astype(bf)
    dv_ref[...] += nt(eb, g)
    dk_ref[...] += nt(ds, q)
    finish(i, nn(x_ref[HP : 2 * HP], ds), c_ref, s_ref, d_ref, db_ref, dk_ref, dv_ref)


def back_call(kernel, ins, in_specs, n, extra_out, extra_scratch, name):
    d_shapes = [jax.ShapeDtypeStruct((3 * HP, n), bf), jax.ShapeDtypeStruct((n // TB, 3 * HP, TB), bf)]
    out_shape = extra_out + d_shapes
    scratch = [pltpu.VMEM((n, HP), bf), pltpu.VMEM((n, HP), bf), pltpu.VMEM((n, HP), f32), pltpu.VMEM((n, HP), f32)]
    return pl.pallas_call(
        kernel,
        grid=(n // QB,),
        in_specs=in_specs,
        out_specs=[whole(x) for x in out_shape],
        out_shape=out_shape,
        scratch_shapes=scratch + extra_scratch,
        compiler_params=pltpu.CompilerParams(vmem_limit_bytes=48 * 2**20),
        cost_estimate=pl.CostEstimate(flops=10 * n * n * 256, bytes_accessed=2 * 12 * HP * n, transcendentals=n * n),
        name=name,
    )(*ins)


def attn_bwd(x, g, o, l, c, s):
    n = x.shape[1]
    specs = [whole(x), whole(g), whole(o), pl.BlockSpec((1, QB), lambda i: (0, i)), whole(c), whole(s)]
    extra = [pltpu.VMEM((HP, n), bf), pltpu.VMEM((HP, n), bf)]
    return back_call(bwd_kernel, (x, g, o, l, c, s), specs, n, [], extra, "attn_bwd")


def attn_both(x, g, c, s):
    n = x.shape[0] * TB
    extra = [pltpu.VMEM((3 * HP, n), bf), pltpu.VMEM((HP, n), bf), pltpu.VMEM((HP, n), bf)]
    out = [jax.ShapeDtypeStruct((n // TB, HP, TB), bf)]
    return back_call(both_kernel, (x, g, c, s), [whole(x), whole(g), whole(c), whole(s)], n, out, extra, "attn_both")


def swap(value, axis, bit):
    count = lax.axis_size(axis)
    return lax.ppermute(value, axis, [(i, i ^ bit) for i in range(count)])


def shifted(value, axis, by):
    count = lax.axis_size(axis)
    pairs = [(i, i + by) for i in range(count) if 0 <= i + by < count]
    return lax.ppermute(value, axis, pairs)


RINGS = 4
FROM = (0, -1, 1, 2)


def move(value, along_z, by):
    pairs = []
    for i in range(RINGS * RINGS):
        z, y = i // RINGS, i % RINGS
        to = (z + by) % RINGS * RINGS + y if along_z else z * RINGS + (y + by) % RINGS
        pairs.append((i, to))
    return lax.ppermute(value, "seq", pairs)


def around(x, along_z):
    behind, ahead = move(x, along_z, 1), move(x, along_z, -1)
    half = x.shape[0] // 2
    far = [move(behind[:half], along_z, 1), move(ahead[half:], along_z, -1)]
    return [x, behind, ahead, jnp.concatenate(far, axis=0)]


def scatter_heads(value):
    return lax.all_to_all(value, "seq", split_axis=0, concat_axis=0, tiled=True)


def angle_tables(places):
    quarter = HS // 4
    freqs = jnp.exp(-math.log(10000.0) * jnp.arange(quarter, dtype=f32) / quarter)
    grid_rows = (places // GRID_W).astype(f32)
    grid_cols = (places % GRID_W).astype(f32)
    angles = jnp.concatenate(
        [
            freqs[:, None] * grid_rows[None, :],
            freqs[:, None] * grid_cols[None, :],
            jnp.zeros((HALF - 2 * quarter, places.shape[0]), f32),
        ],
        axis=0,
    )
    return jnp.cos(angles), jnp.sin(angles)


def pad_rows(x, count):
    return jnp.pad(x, ((0, count - x.shape[0]), (0, 0)))


def arrange(w):
    qt = HS // 4
    parts = []
    for part in (w[0], w[1]):
        parts += [pad_rows(jnp.concatenate([part[0:qt], part[2 * qt : 3 * qt]]), HALF)]
        parts += [pad_rows(jnp.concatenate([part[qt : 2 * qt], part[3 * qt :]]), HALF)]
    return jnp.concatenate(parts + [pad_rows(w[2], HP)], axis=0)


def disarrange(g):
    qt = HS // 4
    parts = []
    for at in (0, HP):
        a, b = g[at : at + HALF], g[at + HALF : at + HP]
        parts += [a[:qt], b[:qt], a[qt : 2 * qt], b[qt : 2 * qt]]
    return jnp.concatenate(parts + [g[2 * HP : 2 * HP + HS]], axis=0).reshape(3, HS, g.shape[1])


def rope(qa, qb, ka, kb, v, c, s):
    return jnp.concatenate([qa * c - qb * s, qa * s + qb * c, ka * c - kb * s, ka * s + kb * c, v], axis=-2).astype(bf)


def modulated_norm(hidden, shift_vec, scale_vec):
    centre = hidden - jnp.mean(hidden, axis=-1, keepdims=True)
    spread = jnp.mean(centre * centre, axis=-1, keepdims=True)
    return centre * lax.rsqrt(spread + norm_eps) * (1.0 + scale_vec) + shift_vec


def norm_back(hidden, scale_vec, grad):
    centre = hidden - jnp.mean(hidden, axis=-1, keepdims=True)
    inv = lax.rsqrt(jnp.mean(centre * centre, axis=-1, keepdims=True) + norm_eps)
    unit = centre * inv
    grad = grad * (1.0 + scale_vec)
    return inv * (grad - jnp.mean(grad, axis=-1, keepdims=True) - unit * jnp.mean(grad * unit, axis=-1, keepdims=True))


def dp_sum(value, first):
    value = value.astype(bf)
    half = value.shape[0] // 2
    low, high = value[:half], value[half:]
    kept, given = jnp.where(first, low, high), jnp.where(first, high, low)
    both = (kept.astype(f32) + swap(given, "dp", 1).astype(f32)).astype(bf)
    total = (both.astype(f32) + swap(both, "dp", 2).astype(f32)).astype(bf)
    other = swap(total, "dp", 1)
    return jnp.concatenate([jnp.where(first, total, other), jnp.where(first, other, total)], axis=0).astype(f32)


def local(streams, modulation, w_qkv, w_out, w_zero, pairing, positions, cotangent):
    on_main = lax.axis_index("section") == 1
    core = lax.axis_index("dp") % 2
    first = core == 0
    mods = modulation[0]
    pair_row = pairing[0]
    width = streams.shape[-1]
    qkv_w = [arrange(w_qkv[0, k, 0]) for k in range(2)]
    out_w = [pad_rows(w_out[0, k, 0], HP) for k in range(2)]

    def own_half(w):
        rows = w.shape[0] // 2
        return lax.dynamic_slice_in_dim(w, core * rows, rows, axis=0)

    def gather(x):
        return lax.all_gather(x, "seq", axis=0, tiled=False)

    def rows_of(w):
        return w.reshape(-1, width)

    def halves_of(x):
        rows = x.shape[1] // 2
        low, high = x[:, :rows], x[:, rows:]
        mine = jnp.where(first, low, high)
        theirs = jnp.where(first, high, low)
        return mine.reshape(-1, x.shape[2]), theirs.reshape(-1, x.shape[2])

    def to_heads(w_pair, x):
        mine, theirs = [nt(rows_of(w), x).reshape(w.shape[:2] + x.shape[:1]) for w in w_pair]
        return jnp.where(first, mine, theirs), jnp.where(first, theirs, mine)

    def from_heads(w_pair, x):
        mine, theirs = halves_of(x)
        return tn(mine, rows_of(w_pair[0])) + tn(theirs, rows_of(w_pair[1]))

    def with_other(x):
        return (x, swap(x, "dp", 1))

    hidden0 = streams[0, 0].astype(f32)
    normed0 = modulated_norm(hidden0, mods[0, 0], mods[0, 1]).astype(bf)
    row_tokens = jnp.concatenate(around(normed0, False), axis=0)
    row_places = jnp.concatenate([positions] + [move(positions, False, -by) for by in FROM[1:]])
    column_w = with_other(jnp.stack(around(own_half(qkv_w[0]), True)))
    low, high = to_heads(column_w, row_tokens)
    qkv0 = rope(low[:, :HALF], low[:, HALF:HP], low[:, HP:], high[:, :HALF], high[:, HALF:], *angle_tables(row_places))
    pieces = [qkv0[0]] + [move(qkv0[i], True, FROM[i]) for i in range(1, RINGS)]
    at = lax.axis_index("seq")
    at_z, at_y = at // RINGS, at % RINGS
    places = jnp.stack([(at_z - z) % RINGS * RINGS + (at_y + y) % RINGS for z in FROM for y in FROM]).astype(jnp.int32)

    cells = jnp.stack([positions // GRID_W, positions % GRID_W]).astype(bf)
    cells = jnp.pad(cells, ((0, 6), (0, width - cells.shape[1])))
    piece_1 = gather(jnp.concatenate([own_half(out_w[0]), own_half(out_w[1]), own_half(qkv_w[1]), cells], axis=0))
    cuts = (HP // 2, HP, HP + 3 * HP // 2)
    out_full0 = with_other(piece_1[:, : cuts[0]])
    out_full1 = with_other(piece_1[:, cuts[0] : cuts[1]])
    qkv_full1 = with_other(piece_1[:, cuts[1] : cuts[2]])
    cells_all = piece_1[:, cuts[2] : cuts[2] + 2, :TB].astype(jnp.int32)
    cos_all, sin_all = angle_tables((cells_all[:, 0] * GRID_W + cells_all[:, 1]).reshape(-1))
    cos_own, sin_own = angle_tables(positions)

    cot = cotangent[0]
    through = nt(cot, w_zero[1])
    grad2 = jnp.where(on_main, cot.astype(f32), jnp.where(pair_row[1] == 1, through, 0.0))
    d_attn1 = (mods[1, 2] * grad2).astype(bf)
    low, high = to_heads(out_full1, d_attn1)
    d_mixed1 = scatter_heads(jnp.concatenate([low, high], axis=1).astype(bf))

    qkv0, mixed0, log_sums0 = attn_fwd(pieces, places)
    early = jnp.concatenate([own_half(qkv_w[0]), normed0, d_attn1], axis=0)
    early = gather(lax.optimization_barrier((early, log_sums0))[0])
    attn0 = from_heads(out_full0, scatter_heads(mixed0))
    hidden1 = hidden0 + mods[0, 2] * attn0
    zero0 = shifted(nn(hidden1.astype(bf), w_zero[0]).astype(bf), "section", 1).astype(f32)
    hidden1 = hidden1 + jnp.where(pair_row[0] == 0, zero0, 0.0)

    normed1 = modulated_norm(hidden1, mods[1, 0], mods[1, 1]).astype(bf)
    low, high = to_heads(qkv_full1, normed1)
    qkv1 = rope(low[:, :HALF], low[:, HALF:HP], low[:, HP:], high[:, :HALF], high[:, HALF:], cos_own, sin_own)
    mixed1, d_raw1, d_raw1_blocks = attn_both(scatter_heads(qkv1), d_mixed1, cos_all, sin_all)
    d_normed1 = from_heads(qkv_full1, scatter_heads(d_raw1_blocks))
    grad1 = grad2 + norm_back(hidden1, mods[1, 1], d_normed1)

    attn1 = from_heads(out_full1, scatter_heads(mixed1))
    hidden2 = hidden1 + mods[1, 2] * attn1
    zero1 = shifted(nn(hidden2.astype(bf), w_zero[1]).astype(bf), "section", 1).astype(f32)
    hidden2 = hidden2 + jnp.where(pair_row[0] == 1, zero0, 0.0) + jnp.where(pair_row[1] == 1, zero1, 0.0)
    final_out = hidden2.astype(bf)[None, None]

    sent = shifted(grad1.astype(bf), "section", -1)
    picked = jnp.where(pair_row[0] == 0, sent, cot)
    picked = jnp.where(on_main, jnp.zeros_like(picked), picked)
    grad1 = grad1 + nt(picked, w_zero[0])
    d_attn0 = (mods[0, 2] * grad1).astype(bf)
    low, high = to_heads(out_full0, d_attn0)
    d_mixed0 = scatter_heads(jnp.concatenate([low, high], axis=1).astype(bf))
    d_mixed0, early = lax.optimization_barrier((d_mixed0, early))
    d_raw0, d_raw0_blocks = attn_bwd(qkv0, d_mixed0, mixed0, log_sums0, cos_all, sin_all)
    last = gather(jnp.concatenate([normed1, d_attn0], axis=0))
    cut = 3 * HP // 2
    qkv_full0 = with_other(early[:, :cut])
    d_normed0 = from_heads(qkv_full0, scatter_heads(d_raw0_blocks))
    grad0 = grad1 + norm_back(hidden0, mods[0, 1], d_normed0)

    normed0_all = early[:, cut : cut + TB].reshape(-1, width)
    d_attn1_all = early[:, cut + TB :].reshape(-1, width)
    normed1_all = last[:, :TB].reshape(-1, width)
    d_attn0_all = last[:, TB:].reshape(-1, width)

    def tokens_last(x):
        return jnp.moveaxis(x, 0, 1).reshape(x.shape[1], -1)

    first_sums = dp_sum(jnp.concatenate([nn(d_raw0, normed0_all), nn(tokens_last(mixed1), d_attn1_all)], axis=0), first)
    last_sums = dp_sum(jnp.concatenate([nn(d_raw1, normed1_all), nn(tokens_last(mixed0), d_attn0_all)], axis=0), first)
    grad_qkv = jnp.stack([disarrange(first_sums[: 3 * HP]), disarrange(last_sums[: 3 * HP])])[None, :, None]
    grad_out = jnp.stack([last_sums[3 * HP : 3 * HP + HS], first_sums[3 * HP : 3 * HP + HS]])[None, :, None]
    return (final_out, grad0[None, None], grad_qkv, grad_out)


def solution(mesh):
    in_specs = (
        P("section", "dp", "seq", None),
        P("section", None, None, None),
        P("section", None, "seq", None, None, None),
        P("section", None, "seq", None, None),
        P(),
        P("dp", None),
        P("seq"),
        P("dp", "seq", None),
    )
    out_specs = (
        P("section", "dp", "seq", None),
        P("section", "dp", "seq", None),
        P("section", None, "seq", None, None, None),
        P("section", None, "seq", None, None),
    )
    return jax.shard_map(local, mesh=mesh, in_specs=in_specs, out_specs=out_specs, check_vma=False)
```

```python
import math

import jax
import jax.numpy as jnp
from jax import lax
from jax.experimental import pallas as pl
from jax.experimental.pallas import tpu as pltpu
from jax.sharding import PartitionSpec as P

GRID_W = 128
HS = 72
HP = 80
HALF = 40
QB = 256
TB = 128
RINGS = 4
FROM = (0, -1, 1, 2)
SCALE = 1.0 / math.sqrt(HS)
EXP_SCALE = math.log2(math.e) / math.sqrt(HS)

norm_eps = 1e-06
bf = jnp.bfloat16
f32 = jnp.float32


def nn(a, b):
    return lax.dot_general(a, b, (((1,), (0,)), ((), ())), preferred_element_type=f32)


def nt(a, b):
    return lax.dot_general(a, b, (((1,), (1,)), ((), ())), preferred_element_type=f32)


def tn(a, b):
    return lax.dot_general(a, b, (((0,), (0,)), ((), ())), preferred_element_type=f32)


def flat(ref, to_ref):
    for j in range(ref.shape[0]):
        to_ref[:, j * TB : (j + 1) * TB] = ref[j]


def put(ref, i, value):
    for j in range(QB // TB):
        ref[i * (QB // TB) + j] = value[:, j * TB : (j + 1) * TB]


def turn_back(x, c, s):
    a, b = x[:HALF], x[HALF:]
    return jnp.concatenate([a * c + b * s, b * c - a * s], axis=0)


def with_ones(v):
    rows = lax.broadcasted_iota(jnp.int32, v.shape, 0)
    return jnp.where(rows == HS, 1.0, v.astype(f32)).astype(bf)


def whole(x):
    zeros = (0,) * x.ndim
    return pl.BlockSpec(x.shape, lambda i: zeros)


def fwd_kernel(to_ref, p0_ref, p1_ref, p2_ref, p3_ref, x_ref, o_ref, l_ref, kt_ref, vo_ref):
    i = pl.program_id(0)

    @pl.when(i == 0)
    def _():
        for at, piece in enumerate((p0_ref, p1_ref, p2_ref, p3_ref)):
            for j in range(piece.shape[1] // TB):
                place = pl.multiple_of(to_ref[at * (piece.shape[1] // TB) + j] * TB, TB)
                x_ref[:, pl.ds(place, TB)] = piece[:, j * TB : (j + 1) * TB]
        kt_ref[...] = x_ref[HP : 2 * HP].astype(f32).T.astype(bf)
        vo_ref[...] = with_ones(x_ref[2 * HP :])

    s = nn(kt_ref[...], x_ref[:HP, pl.ds(pl.multiple_of(i * QB, QB), QB)])
    m = jnp.max(s, axis=0, keepdims=True)
    e = jnp.exp2((s - m) * EXP_SCALE).astype(bf)
    o = nn(vo_ref[...], e)
    total = o[HS : HS + 1]
    rows = lax.broadcasted_iota(jnp.int32, o.shape, 0)
    put(o_ref, i, jnp.where(rows < HS, o * (1.0 / total), 0.0).astype(bf))
    l_ref[...] = m * EXP_SCALE + jnp.log2(total)


def attn_fwd(pieces, places):
    n = sum(p.shape[1] for p in pieces)
    return pl.pallas_call(
        fwd_kernel,
        grid=(n // QB,),
        in_specs=[pl.BlockSpec(memory_space=pltpu.SMEM)] + [whole(p) for p in pieces],
        out_specs=[
            pl.BlockSpec((3 * HP, n), lambda i: (0, 0)),
            pl.BlockSpec((n // TB, HP, TB), lambda i: (0, 0, 0)),
            pl.BlockSpec((1, QB), lambda i: (0, i)),
        ],
        out_shape=[
            jax.ShapeDtypeStruct((3 * HP, n), bf),
            jax.ShapeDtypeStruct((n // TB, HP, TB), bf),
            jax.ShapeDtypeStruct((1, n), f32),
        ],
        scratch_shapes=[pltpu.VMEM((n, HP), bf), pltpu.VMEM((HP, n), bf)],
        compiler_params=pltpu.CompilerParams(vmem_limit_bytes=40 * 2**20),
        cost_estimate=pl.CostEstimate(flops=4 * n * n * 256, bytes_accessed=2 * 4 * HP * n, transcendentals=n * n),
        name="attn_fwd",
    )(places, *pieces)


def prep(x_ref, kt_ref, vt_ref, dk_ref, dv_ref):
    kt_ref[...] = x_ref[HP : 2 * HP].astype(f32).T.astype(bf)
    vt_ref[...] = x_ref[2 * HP :].astype(f32).T.astype(bf)
    dk_ref[...] = jnp.zeros_like(dk_ref)
    dv_ref[...] = jnp.zeros_like(dv_ref)


def finish(i, dq, c_ref, s_ref, d_ref, dk_ref, dv_ref):
    at = pl.ds(pl.multiple_of(i * QB, QB), QB)
    d_ref[:HP, at] = turn_back(dq * SCALE, c_ref[:, at], s_ref[:, at]).astype(bf)

    @pl.when(i == pl.num_programs(0) - 1)
    def _():
        d_ref[HP : 2 * HP, :] = turn_back(dk_ref[...].T * SCALE, c_ref[...], s_ref[...]).astype(bf)
        d_ref[2 * HP :, :] = dv_ref[...].T.astype(bf)


def bwd_kernel(x_ref, g_ref, o_ref, l_ref, c_ref, s_ref, to_ref, dz_ref, kt_ref, vt_ref, dk_ref, dv_ref, gx_ref, ox_ref, d_ref):
    i = pl.program_id(0)

    @pl.when(i == 0)
    def _():
        prep(x_ref, kt_ref, vt_ref, dk_ref, dv_ref)
        flat(g_ref, gx_ref)
        flat(o_ref, ox_ref)

    at = pl.ds(pl.multiple_of(i * QB, QB), QB)
    q = x_ref[:HP, at]
    g = gx_ref[:, at]
    p = jnp.exp2(nn(kt_ref[...], q) * EXP_SCALE - l_ref[...])
    delta = jnp.sum(g.astype(f32) * ox_ref[:, at].astype(f32), axis=0, keepdims=True)
    ds = (p * (nn(vt_ref[...], g) - delta)).astype(bf)
    dv_ref[...] += nt(p.astype(bf), g)
    dk_ref[...] += nt(ds, q)
    finish(i, nn(x_ref[HP : 2 * HP], ds), c_ref, s_ref, d_ref, dk_ref, dv_ref)

    @pl.when(i == pl.num_programs(0) - 1)
    def _():
        for z in range(dz_ref.shape[0]):
            for y in range(dz_ref.shape[2] // TB):
                place = pl.multiple_of(to_ref[z * (dz_ref.shape[2] // TB) + y] * TB, TB)
                dz_ref[z, :, y * TB : (y + 1) * TB] = d_ref[:, pl.ds(place, TB)]


def both_kernel(xb_ref, gb_ref, c_ref, s_ref, o_ref, d_ref, db_ref, kt_ref, vt_ref, dk_ref, dv_ref, x_ref, g_ref, vo_ref):
    i = pl.program_id(0)

    @pl.when(i == 0)
    def _():
        flat(xb_ref, x_ref)
        flat(gb_ref, g_ref)
        prep(x_ref, kt_ref, vt_ref, dk_ref, dv_ref)
        vo_ref[...] = with_ones(x_ref[2 * HP :])

    at = pl.ds(pl.multiple_of(i * QB, QB), QB)
    q = x_ref[:HP, at]
    s = nn(kt_ref[...], q)
    m = jnp.max(s, axis=0, keepdims=True)
    e = jnp.exp2((s - m) * EXP_SCALE)
    eb = e.astype(bf)
    o = nn(vo_ref[...], eb)
    inv = 1.0 / o[HS : HS + 1]
    rows = lax.broadcasted_iota(jnp.int32, o.shape, 0)
    o = jnp.where(rows < HS, o * inv, 0.0)
    put(o_ref, i, o.astype(bf))
    g = g_ref[:, at].astype(f32) * inv
    delta = jnp.sum(g * o, axis=0, keepdims=True)
    g = g.astype(bf)
    ds = (e * (nn(vt_ref[...], g) - delta)).astype(bf)
    dv_ref[...] += nt(eb, g)
    dk_ref[...] += nt(ds, q)
    finish(i, nn(x_ref[HP : 2 * HP], ds), c_ref, s_ref, d_ref, dk_ref, dv_ref)

    @pl.when(i == pl.num_programs(0) - 1)
    def _():
        for j in range(db_ref.shape[0]):
            db_ref[j] = d_ref[:, j * TB : (j + 1) * TB]


def back_call(kernel, ins, in_specs, n, out_shape, extra_scratch, name):
    scratch = [pltpu.VMEM((n, HP), bf), pltpu.VMEM((n, HP), bf), pltpu.VMEM((n, HP), f32), pltpu.VMEM((n, HP), f32)]
    return pl.pallas_call(
        kernel,
        grid=(n // QB,),
        in_specs=in_specs,
        out_specs=[whole(x) for x in out_shape],
        out_shape=out_shape,
        scratch_shapes=scratch + extra_scratch,
        compiler_params=pltpu.CompilerParams(vmem_limit_bytes=48 * 2**20),
        cost_estimate=pl.CostEstimate(flops=10 * n * n * 256, bytes_accessed=2 * 12 * HP * n, transcendentals=n * n),
        name=name,
    )(*ins)


def attn_bwd(x, g, o, l, c, s, places):
    n = x.shape[1]
    specs = [whole(x), whole(g), whole(o), pl.BlockSpec((1, QB), lambda i: (0, i)), whole(c), whole(s)]
    specs += [pl.BlockSpec(memory_space=pltpu.SMEM)]
    extra = [pltpu.VMEM((HP, n), bf), pltpu.VMEM((HP, n), bf), pltpu.VMEM((3 * HP, n), bf)]
    out = [jax.ShapeDtypeStruct((RINGS, 3 * HP, n // RINGS), bf)]
    return back_call(bwd_kernel, (x, g, o, l, c, s, places), specs, n, out, extra, "attn_bwd")[0]


def attn_both(x, g, c, s):
    n = x.shape[0] * TB
    extra = [pltpu.VMEM((3 * HP, n), bf), pltpu.VMEM((HP, n), bf), pltpu.VMEM((HP, n), bf)]
    out = [
        jax.ShapeDtypeStruct((n // TB, HP, TB), bf),
        jax.ShapeDtypeStruct((3 * HP, n), bf),
        jax.ShapeDtypeStruct((n // TB, 3 * HP, TB), bf),
    ]
    return back_call(both_kernel, (x, g, c, s), [whole(x), whole(g), whole(c), whole(s)], n, out, extra, "attn_both")


def swap(value, axis, bit):
    count = lax.axis_size(axis)
    return lax.ppermute(value, axis, [(i, i ^ bit) for i in range(count)])


def shifted(value, axis, by):
    count = lax.axis_size(axis)
    pairs = [(i, i + by) for i in range(count) if 0 <= i + by < count]
    return lax.ppermute(value, axis, pairs)


def move(value, along_z, by):
    pairs = []
    for i in range(RINGS * RINGS):
        z, y = i // RINGS, i % RINGS
        to = (z + by) % RINGS * RINGS + y if along_z else z * RINGS + (y + by) % RINGS
        pairs.append((i, to))
    return lax.ppermute(value, "seq", pairs)


def around(x, along_z):
    behind, ahead = move(x, along_z, 1), move(x, along_z, -1)
    half = x.shape[0] // 2
    far = [move(behind[:half], along_z, 1), move(ahead[half:], along_z, -1)]
    return [x, behind, ahead, jnp.concatenate(far, axis=0)]


def home(parts, along_z):
    got = [parts[0]] + [move(parts[i], along_z, FROM[i]) for i in range(1, RINGS)]
    return [got[0], got[2], got[1], got[3]]


def home_sum(parts, along_z):
    first, *rest = [x.astype(f32) for x in home(parts, along_z)]
    return first + rest[0] + rest[1] + rest[2]


def scatter_heads(value):
    return lax.all_to_all(value, "seq", split_axis=0, concat_axis=0, tiled=True)


def angle_tables(places):
    quarter = HS // 4
    freqs = jnp.exp(-math.log(10000.0) * jnp.arange(quarter, dtype=f32) / quarter)
    grid_rows = (places // GRID_W).astype(f32)
    grid_cols = (places % GRID_W).astype(f32)
    angles = jnp.concatenate(
        [
            freqs[:, None] * grid_rows[None, :],
            freqs[:, None] * grid_cols[None, :],
            jnp.zeros((HALF - 2 * quarter, places.shape[0]), f32),
        ],
        axis=0,
    )
    return jnp.cos(angles), jnp.sin(angles)


def pad_rows(x, count):
    return jnp.pad(x, ((0, count - x.shape[0]), (0, 0)))


def arrange(w):
    qt = HS // 4
    parts = []
    for part in (w[0], w[1]):
        parts += [pad_rows(jnp.concatenate([part[0:qt], part[2 * qt : 3 * qt]]), HALF)]
        parts += [pad_rows(jnp.concatenate([part[qt : 2 * qt], part[3 * qt :]]), HALF)]
    return jnp.concatenate(parts + [pad_rows(w[2], HP)], axis=0)


def disarrange(g):
    qt = HS // 4
    parts = []
    for at in (0, HP):
        a, b = g[at : at + HALF], g[at + HALF : at + HP]
        parts += [a[:qt], b[:qt], a[qt : 2 * qt], b[qt : 2 * qt]]
    return jnp.concatenate(parts + [g[2 * HP : 2 * HP + HS]], axis=0).reshape(3, HS, g.shape[1])


def rope(qa, qb, ka, kb, v, c, s):
    return jnp.concatenate([qa * c - qb * s, qa * s + qb * c, ka * c - kb * s, ka * s + kb * c, v], axis=-2).astype(bf)


def modulated_norm(hidden, shift_vec, scale_vec):
    centre = hidden - jnp.mean(hidden, axis=-1, keepdims=True)
    spread = jnp.mean(centre * centre, axis=-1, keepdims=True)
    return centre * lax.rsqrt(spread + norm_eps) * (1.0 + scale_vec) + shift_vec


def norm_back(hidden, scale_vec, grad):
    centre = hidden - jnp.mean(hidden, axis=-1, keepdims=True)
    inv = lax.rsqrt(jnp.mean(centre * centre, axis=-1, keepdims=True) + norm_eps)
    unit = centre * inv
    grad = grad * (1.0 + scale_vec)
    return inv * (grad - jnp.mean(grad, axis=-1, keepdims=True) - unit * jnp.mean(grad * unit, axis=-1, keepdims=True))


def core_half(value, first):
    value = value.astype(bf)
    half = value.shape[-2] // 2
    low, high = value[..., :half, :], value[..., half:, :]
    kept, given = jnp.where(first, low, high), jnp.where(first, high, low)
    return (kept.astype(f32) + swap(given, "dp", 1).astype(f32)).astype(bf)


def core_whole(value, first):
    total = (value.astype(f32) + swap(value, "dp", 2).astype(f32)).astype(bf)
    other = swap(total, "dp", 1)
    return jnp.concatenate([jnp.where(first, total, other), jnp.where(first, other, total)], axis=0).astype(f32)


def local(streams, modulation, w_qkv, w_out, w_zero, pairing, positions, cotangent):
    on_main = lax.axis_index("section") == 1
    core = lax.axis_index("dp") % 2
    first = core == 0
    mods = modulation[0]
    pair_row = pairing[0]
    width = streams.shape[-1]
    qkv_w = [arrange(w_qkv[0, k, 0]) for k in range(2)]
    out_w = [pad_rows(w_out[0, k, 0], HP) for k in range(2)]

    def own_half(w):
        rows = w.shape[0] // 2
        return lax.dynamic_slice_in_dim(w, core * rows, rows, axis=0)

    def gather(x):
        return lax.all_gather(x, "seq", axis=0, tiled=False)

    def rows_of(w):
        return w.reshape(-1, width)

    def halves_of(x):
        rows = x.shape[1] // 2
        low, high = x[:, :rows], x[:, rows:]
        mine = jnp.where(first, low, high)
        theirs = jnp.where(first, high, low)
        return mine.reshape(-1, x.shape[2]), theirs.reshape(-1, x.shape[2])

    def to_heads(w_pair, x):
        mine, theirs = [nt(rows_of(w), x).reshape(w.shape[:2] + x.shape[:1]) for w in w_pair]
        return jnp.where(first, mine, theirs), jnp.where(first, theirs, mine)

    def from_heads(w_pair, x):
        mine, theirs = halves_of(x)
        return tn(mine, rows_of(w_pair[0])) + tn(theirs, rows_of(w_pair[1]))

    def with_other(x):
        return (x, swap(x, "dp", 1))

    hidden0 = streams[0, 0].astype(f32)
    normed0 = modulated_norm(hidden0, mods[0, 0], mods[0, 1]).astype(bf)
    row_tokens = jnp.concatenate(around(normed0, False), axis=0)
    row_places = jnp.concatenate([positions] + [move(positions, False, -by) for by in FROM[1:]])
    column_w = with_other(jnp.stack(around(own_half(qkv_w[0]), True)))
    low, high = to_heads(column_w, row_tokens)
    qkv0 = rope(low[:, :HALF], low[:, HALF:HP], low[:, HP:], high[:, :HALF], high[:, HALF:], *angle_tables(row_places))
    pieces = home(qkv0, True)
    at = lax.axis_index("seq")
    at_z, at_y = at // RINGS, at % RINGS
    places = jnp.stack([(at_z + z) % RINGS * RINGS + (at_y + y) % RINGS for z in FROM for y in FROM]).astype(jnp.int32)

    cells = jnp.stack([positions // GRID_W, positions % GRID_W]).astype(bf)
    cells = jnp.pad(cells, ((0, 6), (0, width - cells.shape[1])))
    piece_1 = gather(jnp.concatenate([own_half(out_w[0]), own_half(out_w[1]), own_half(qkv_w[1]), cells], axis=0))
    cuts = (HP // 2, HP, HP + 3 * HP // 2)
    out_full0 = with_other(piece_1[:, : cuts[0]])
    out_full1 = with_other(piece_1[:, cuts[0] : cuts[1]])
    qkv_full1 = with_other(piece_1[:, cuts[1] : cuts[2]])
    cells_all = piece_1[:, cuts[2] : cuts[2] + 2, :TB].astype(jnp.int32)
    cos_all, sin_all = angle_tables((cells_all[:, 0] * GRID_W + cells_all[:, 1]).reshape(-1))
    cos_own, sin_own = angle_tables(positions)

    cot = cotangent[0]
    through = nt(cot, w_zero[1])
    grad2 = jnp.where(on_main, cot.astype(f32), jnp.where(pair_row[1] == 1, through, 0.0))
    d_attn1 = (mods[1, 2] * grad2).astype(bf)
    low, high = to_heads(out_full1, d_attn1)
    d_mixed1 = scatter_heads(jnp.concatenate([low, high], axis=1).astype(bf))

    qkv0, mixed0, log_sums0 = attn_fwd(pieces, places)
    attn0 = from_heads(out_full0, scatter_heads(mixed0))
    hidden1 = hidden0 + mods[0, 2] * attn0
    zero0 = shifted(nn(hidden1.astype(bf), w_zero[0]).astype(bf), "section", 1).astype(f32)
    hidden1 = hidden1 + jnp.where(pair_row[0] == 0, zero0, 0.0)

    normed1 = modulated_norm(hidden1, mods[1, 0], mods[1, 1]).astype(bf)
    both_all = gather(jnp.concatenate([d_attn1, normed1], axis=0))
    low, high = to_heads(qkv_full1, normed1)
    qkv1 = rope(low[:, :HALF], low[:, HALF:HP], low[:, HP:], high[:, :HALF], high[:, HALF:], cos_own, sin_own)
    mixed1, d_raw1, d_raw1_blocks = attn_both(scatter_heads(qkv1), d_mixed1, cos_all, sin_all)
    d_normed1 = from_heads(qkv_full1, scatter_heads(d_raw1_blocks))
    grad1 = grad2 + norm_back(hidden1, mods[1, 1], d_normed1)

    sent = shifted(grad1.astype(bf), "section", -1)
    picked = jnp.where(pair_row[0] == 0, sent, cot)
    picked = jnp.where(on_main, jnp.zeros_like(picked), picked)
    grad1 = grad1 + nt(picked, w_zero[0])
    d_attn0 = (mods[0, 2] * grad1).astype(bf)
    low, high = to_heads(out_full0, d_attn0)
    d_mixed0 = scatter_heads(jnp.concatenate([low, high], axis=1).astype(bf))
    d_mixed0, both_all = lax.optimization_barrier((d_mixed0, both_all))
    d_raw0 = attn_bwd(qkv0, d_mixed0, mixed0, log_sums0, cos_all, sin_all, places)

    mixed1_first = lax.optimization_barrier((mixed1, d_mixed0))[0]
    attn1 = from_heads(out_full1, scatter_heads(mixed1_first))
    hidden2 = hidden1 + mods[1, 2] * attn1
    zero1 = shifted(nn(hidden2.astype(bf), w_zero[1]).astype(bf), "section", 1).astype(f32)
    hidden2 = hidden2 + jnp.where(pair_row[0] == 1, zero0, 0.0) + jnp.where(pair_row[1] == 1, zero1, 0.0)
    final_out = hidden2.astype(bf)[None, None]

    d_raw0 = jnp.stack(home(d_raw0, True))
    d_row0 = from_heads(column_w, d_raw0).astype(bf).reshape(RINGS, -1, width)
    grad0 = grad1 + norm_back(hidden0, mods[0, 1], home_sum(d_row0, False))
    qkv_sums0 = lax.dot_general(d_raw0, row_tokens, (((2,), (0,)), ((), ())), preferred_element_type=f32)
    qkv_sums0 = core_whole(home_sum(core_half(qkv_sums0, first), True).astype(bf), first)

    d_attn1_all = both_all[:, :TB].reshape(-1, width)
    normed1_all = both_all[:, TB:].reshape(-1, width)
    d_attn0_all = gather(d_attn0).reshape(-1, width)

    def tokens_last(x):
        return jnp.moveaxis(x, 0, 1).reshape(x.shape[1], -1)

    sums = [nn(d_raw1, normed1_all), nn(tokens_last(mixed1), d_attn1_all), nn(tokens_last(mixed0), d_attn0_all)]
    sums = core_whole(core_half(jnp.concatenate(sums, axis=0), first), first)
    grad_qkv = jnp.stack([disarrange(qkv_sums0), disarrange(sums[: 3 * HP])])[None, :, None]
    grad_out = jnp.stack([sums[4 * HP : 4 * HP + HS], sums[3 * HP : 3 * HP + HS]])[None, :, None]
    return (final_out, grad0[None, None], grad_qkv, grad_out)


def solution(mesh):
    in_specs = (
        P("section", "dp", "seq", None),
        P("section", None, None, None),
        P("section", None, "seq", None, None, None),
        P("section", None, "seq", None, None),
        P(),
        P("dp", None),
        P("seq"),
        P("dp", "seq", None),
    )
    out_specs = (
        P("section", "dp", "seq", None),
        P("section", "dp", "seq", None),
        P("section", None, "seq", None, None, None),
        P("section", None, "seq", None, None),
    )
    return jax.shard_map(local, mesh=mesh, in_specs=in_specs, out_specs=out_specs, check_vma=False)
```

```python
import math

import jax
import jax.numpy as jnp
from jax import lax
from jax.experimental import pallas as pl
from jax.experimental.pallas import tpu as pltpu
from jax.sharding import PartitionSpec as P

GRID_W = 128
HS = 72
HP = 80
HALF = 40
QB = 256
TB = 128
RINGS = 4
FROM = (0, -1, 1, 2)
SCALE = 1.0 / math.sqrt(HS)
EXP_SCALE = math.log2(math.e) / math.sqrt(HS)

norm_eps = 1e-06
bf = jnp.bfloat16
f32 = jnp.float32


def nn(a, b):
    return lax.dot_general(a, b, (((1,), (0,)), ((), ())), preferred_element_type=f32)


def nt(a, b):
    return lax.dot_general(a, b, (((1,), (1,)), ((), ())), preferred_element_type=f32)


def tn(a, b):
    return lax.dot_general(a, b, (((0,), (0,)), ((), ())), preferred_element_type=f32)


def flat(ref, to_ref):
    for j in range(ref.shape[0]):
        to_ref[:, j * TB : (j + 1) * TB] = ref[j]


def put(ref, i, value):
    for j in range(QB // TB):
        ref[i * (QB // TB) + j] = value[:, j * TB : (j + 1) * TB]


def by_rings(ref, to_ref, block):
    wide = ref.shape[2] // TB
    for z in range(ref.shape[0]):
        for y in range(wide):
            ref[z, :, y * TB : (y + 1) * TB] = block(to_ref[z * wide + y])


def turn_back(x, c, s):
    a, b = x[:HALF], x[HALF:]
    return jnp.concatenate([a * c + b * s, b * c - a * s], axis=0)


def with_ones(v):
    rows = lax.broadcasted_iota(jnp.int32, v.shape, 0)
    return jnp.where(rows == HS, 1.0, v.astype(f32)).astype(bf)


def whole(x):
    zeros = (0,) * x.ndim
    return pl.BlockSpec(x.shape, lambda i: zeros)


def fwd_kernel(to_ref, p0_ref, p1_ref, p2_ref, p3_ref, x_ref, o_ref, oz_ref, l_ref, kt_ref, vo_ref):
    i = pl.program_id(0)

    @pl.when(i == 0)
    def _():
        for at, piece in enumerate((p0_ref, p1_ref, p2_ref, p3_ref)):
            for j in range(piece.shape[1] // TB):
                place = pl.multiple_of(to_ref[at * (piece.shape[1] // TB) + j] * TB, TB)
                x_ref[:, pl.ds(place, TB)] = piece[:, j * TB : (j + 1) * TB]
        kt_ref[...] = x_ref[HP : 2 * HP].astype(f32).T.astype(bf)
        vo_ref[...] = with_ones(x_ref[2 * HP :])

    s = nn(kt_ref[...], x_ref[:HP, pl.ds(pl.multiple_of(i * QB, QB), QB)])
    m = jnp.max(s, axis=0, keepdims=True)
    e = jnp.exp2((s - m) * EXP_SCALE).astype(bf)
    o = nn(vo_ref[...], e)
    total = o[HS : HS + 1]
    rows = lax.broadcasted_iota(jnp.int32, o.shape, 0)
    put(o_ref, i, jnp.where(rows < HS, o * (1.0 / total), 0.0).astype(bf))
    l_ref[...] = m * EXP_SCALE + jnp.log2(total)

    @pl.when(i == pl.num_programs(0) - 1)
    def _():
        by_rings(oz_ref, to_ref, lambda block: o_ref[block])


def attn_fwd(pieces, places):
    n = sum(p.shape[1] for p in pieces)
    return pl.pallas_call(
        fwd_kernel,
        grid=(n // QB,),
        in_specs=[pl.BlockSpec(memory_space=pltpu.SMEM)] + [whole(p) for p in pieces],
        out_specs=[
            pl.BlockSpec((3 * HP, n), lambda i: (0, 0)),
            pl.BlockSpec((n // TB, HP, TB), lambda i: (0, 0, 0)),
            pl.BlockSpec((RINGS, HP, n // RINGS), lambda i: (0, 0, 0)),
            pl.BlockSpec((1, QB), lambda i: (0, i)),
        ],
        out_shape=[
            jax.ShapeDtypeStruct((3 * HP, n), bf),
            jax.ShapeDtypeStruct((n // TB, HP, TB), bf),
            jax.ShapeDtypeStruct((RINGS, HP, n // RINGS), bf),
            jax.ShapeDtypeStruct((1, n), f32),
        ],
        scratch_shapes=[pltpu.VMEM((n, HP), bf), pltpu.VMEM((HP, n), bf)],
        compiler_params=pltpu.CompilerParams(vmem_limit_bytes=40 * 2**20),
        cost_estimate=pl.CostEstimate(flops=4 * n * n * 256, bytes_accessed=2 * 4 * HP * n, transcendentals=n * n),
        name="attn_fwd",
    )(places, *pieces)


def prep(x_ref, kt_ref, vt_ref, dk_ref, dv_ref):
    kt_ref[...] = x_ref[HP : 2 * HP].astype(f32).T.astype(bf)
    vt_ref[...] = x_ref[2 * HP :].astype(f32).T.astype(bf)
    dk_ref[...] = jnp.zeros_like(dk_ref)
    dv_ref[...] = jnp.zeros_like(dv_ref)


def finish(i, dq, c_ref, s_ref, d_ref, dk_ref, dv_ref):
    at = pl.ds(pl.multiple_of(i * QB, QB), QB)
    d_ref[:HP, at] = turn_back(dq * SCALE, c_ref[:, at], s_ref[:, at]).astype(bf)

    @pl.when(i == pl.num_programs(0) - 1)
    def _():
        d_ref[HP : 2 * HP, :] = turn_back(dk_ref[...].T * SCALE, c_ref[...], s_ref[...]).astype(bf)
        d_ref[2 * HP :, :] = dv_ref[...].T.astype(bf)


def bwd_kernel(x_ref, g_ref, o_ref, l_ref, c_ref, s_ref, to_ref, dz_ref, d_ref, kt_ref, vt_ref, dk_ref, dv_ref, gx_ref, ox_ref):
    i = pl.program_id(0)

    @pl.when(i == 0)
    def _():
        prep(x_ref, kt_ref, vt_ref, dk_ref, dv_ref)
        flat(g_ref, gx_ref)
        flat(o_ref, ox_ref)

    at = pl.ds(pl.multiple_of(i * QB, QB), QB)
    q = x_ref[:HP, at]
    g = gx_ref[:, at]
    p = jnp.exp2(nn(kt_ref[...], q) * EXP_SCALE - l_ref[...])
    delta = jnp.sum(g.astype(f32) * ox_ref[:, at].astype(f32), axis=0, keepdims=True)
    ds = (p * (nn(vt_ref[...], g) - delta)).astype(bf)
    dv_ref[...] += nt(p.astype(bf), g)
    dk_ref[...] += nt(ds, q)
    finish(i, nn(x_ref[HP : 2 * HP], ds), c_ref, s_ref, d_ref, dk_ref, dv_ref)

    @pl.when(i == pl.num_programs(0) - 1)
    def _():
        by_rings(dz_ref, to_ref, lambda block: d_ref[:, pl.ds(pl.multiple_of(block * TB, TB), TB)])


def both_kernel(xb_ref, gb_ref, c_ref, s_ref, o_ref, d_ref, db_ref, kt_ref, vt_ref, dk_ref, dv_ref, x_ref, g_ref, vo_ref):
    i = pl.program_id(0)

    @pl.when(i == 0)
    def _():
        flat(xb_ref, x_ref)
        flat(gb_ref, g_ref)
        prep(x_ref, kt_ref, vt_ref, dk_ref, dv_ref)
        vo_ref[...] = with_ones(x_ref[2 * HP :])

    at = pl.ds(pl.multiple_of(i * QB, QB), QB)
    q = x_ref[:HP, at]
    s = nn(kt_ref[...], q)
    m = jnp.max(s, axis=0, keepdims=True)
    e = jnp.exp2((s - m) * EXP_SCALE)
    eb = e.astype(bf)
    o = nn(vo_ref[...], eb)
    inv = 1.0 / o[HS : HS + 1]
    rows = lax.broadcasted_iota(jnp.int32, o.shape, 0)
    o = jnp.where(rows < HS, o * inv, 0.0)
    put(o_ref, i, o.astype(bf))
    g = g_ref[:, at].astype(f32) * inv
    delta = jnp.sum(g * o, axis=0, keepdims=True)
    g = g.astype(bf)
    ds = (e * (nn(vt_ref[...], g) - delta)).astype(bf)
    dv_ref[...] += nt(eb, g)
    dk_ref[...] += nt(ds, q)
    finish(i, nn(x_ref[HP : 2 * HP], ds), c_ref, s_ref, d_ref, dk_ref, dv_ref)

    @pl.when(i == pl.num_programs(0) - 1)
    def _():
        for j in range(db_ref.shape[0]):
            db_ref[j] = d_ref[:, j * TB : (j + 1) * TB]


def back_call(kernel, ins, in_specs, n, out_shape, extra_scratch, name):
    scratch = [pltpu.VMEM((n, HP), bf), pltpu.VMEM((n, HP), bf), pltpu.VMEM((n, HP), f32), pltpu.VMEM((n, HP), f32)]
    return pl.pallas_call(
        kernel,
        grid=(n // QB,),
        in_specs=in_specs,
        out_specs=[whole(x) for x in out_shape],
        out_shape=out_shape,
        scratch_shapes=scratch + extra_scratch,
        compiler_params=pltpu.CompilerParams(vmem_limit_bytes=48 * 2**20),
        cost_estimate=pl.CostEstimate(flops=10 * n * n * 256, bytes_accessed=2 * 12 * HP * n, transcendentals=n * n),
        name=name,
    )(*ins)


def attn_bwd(x, g, o, l, c, s, places):
    n = x.shape[1]
    specs = [whole(x), whole(g), whole(o), pl.BlockSpec((1, QB), lambda i: (0, i)), whole(c), whole(s)]
    specs += [pl.BlockSpec(memory_space=pltpu.SMEM)]
    extra = [pltpu.VMEM((HP, n), bf), pltpu.VMEM((HP, n), bf)]
    out = [jax.ShapeDtypeStruct((RINGS, 3 * HP, n // RINGS), bf), jax.ShapeDtypeStruct((3 * HP, n), bf)]
    return back_call(bwd_kernel, (x, g, o, l, c, s, places), specs, n, out, extra, "attn_bwd")


def attn_both(x, g, c, s):
    n = x.shape[0] * TB
    extra = [pltpu.VMEM((3 * HP, n), bf), pltpu.VMEM((HP, n), bf), pltpu.VMEM((HP, n), bf)]
    out = [
        jax.ShapeDtypeStruct((n // TB, HP, TB), bf),
        jax.ShapeDtypeStruct((3 * HP, n), bf),
        jax.ShapeDtypeStruct((n // TB, 3 * HP, TB), bf),
    ]
    return back_call(both_kernel, (x, g, c, s), [whole(x), whole(g), whole(c), whole(s)], n, out, extra, "attn_both")


def grad_kernel(x_ref, g_ref, out_ref, acc_ref):
    i = pl.program_id(0)

    @pl.when(i == 0)
    def _():
        acc_ref[...] = jnp.zeros_like(acc_ref)

    acc_ref[...] += nn(x_ref[...], g_ref[...].reshape(x_ref.shape[1], -1))

    @pl.when(i == pl.num_programs(0) - 1)
    def _():
        out_ref[...] = acc_ref[...].astype(bf)


def weight_grad(x, gathered, part):
    blocks, _, width = gathered.shape
    step = 4
    return pl.pallas_call(
        grad_kernel,
        grid=(blocks // step,),
        in_specs=[
            pl.BlockSpec((x.shape[0], step * TB), lambda i: (0, i)),
            pl.BlockSpec((step, TB, width), lambda i: (i, part, 0)),
        ],
        out_specs=pl.BlockSpec((x.shape[0], width), lambda i: (0, 0)),
        out_shape=jax.ShapeDtypeStruct((x.shape[0], width), bf),
        scratch_shapes=[pltpu.VMEM((x.shape[0], width), f32)],
        compiler_params=pltpu.CompilerParams(vmem_limit_bytes=32 * 2**20),
        cost_estimate=pl.CostEstimate(
            flops=2 * x.shape[0] * blocks * TB * width, bytes_accessed=2 * blocks * TB * width, transcendentals=0
        ),
        name="weight_grad",
    )(x, gathered)


def swap(value, axis, bit):
    count = lax.axis_size(axis)
    return lax.ppermute(value, axis, [(i, i ^ bit) for i in range(count)])


def shifted(value, axis, by):
    count = lax.axis_size(axis)
    pairs = [(i, i + by) for i in range(count) if 0 <= i + by < count]
    return lax.ppermute(value, axis, pairs)


def move(value, along_z, by):
    pairs = []
    for i in range(RINGS * RINGS):
        z, y = i // RINGS, i % RINGS
        to = (z + by) % RINGS * RINGS + y if along_z else z * RINGS + (y + by) % RINGS
        pairs.append((i, to))
    return lax.ppermute(value, "seq", pairs)


def around(x, along_z):
    return [x] + [move(x, along_z, -by) for by in FROM[1:]]


def home(parts, along_z):
    got = [parts[0]] + [move(parts[i], along_z, FROM[i]) for i in range(1, RINGS)]
    return [got[0], got[2], got[1], got[3]]


def home_sum(parts, along_z):
    first, *rest = [x.astype(f32) for x in home(parts, along_z)]
    return first + rest[0] + rest[1] + rest[2]


def scatter_heads(value):
    return lax.all_to_all(value, "seq", split_axis=0, concat_axis=0, tiled=True)


def angle_tables(places):
    quarter = HS // 4
    freqs = jnp.exp(-math.log(10000.0) * jnp.arange(quarter, dtype=f32) / quarter)
    grid_rows = (places // GRID_W).astype(f32)
    grid_cols = (places % GRID_W).astype(f32)
    angles = jnp.concatenate(
        [
            freqs[:, None] * grid_rows[None, :],
            freqs[:, None] * grid_cols[None, :],
            jnp.zeros((HALF - 2 * quarter, places.shape[0]), f32),
        ],
        axis=0,
    )
    return jnp.cos(angles), jnp.sin(angles)


def pad_rows(x, count):
    return jnp.pad(x, ((0, count - x.shape[0]), (0, 0)))


def arrange(w):
    qt = HS // 4
    parts = []
    for part in (w[0], w[1]):
        parts += [pad_rows(jnp.concatenate([part[0:qt], part[2 * qt : 3 * qt]]), HALF)]
        parts += [pad_rows(jnp.concatenate([part[qt : 2 * qt], part[3 * qt :]]), HALF)]
    return jnp.concatenate(parts + [pad_rows(w[2], HP)], axis=0)


def disarrange(g):
    qt = HS // 4
    parts = []
    for at in (0, HP):
        a, b = g[at : at + HALF], g[at + HALF : at + HP]
        parts += [a[:qt], b[:qt], a[qt : 2 * qt], b[qt : 2 * qt]]
    return jnp.concatenate(parts + [g[2 * HP : 2 * HP + HS]], axis=0).reshape(3, HS, g.shape[1])


def rope(qa, qb, ka, kb, v, c, s):
    return jnp.concatenate([qa * c - qb * s, qa * s + qb * c, ka * c - kb * s, ka * s + kb * c, v], axis=-2).astype(bf)


def modulated_norm(hidden, shift_vec, scale_vec):
    centre = hidden - jnp.mean(hidden, axis=-1, keepdims=True)
    spread = jnp.mean(centre * centre, axis=-1, keepdims=True)
    return centre * lax.rsqrt(spread + norm_eps) * (1.0 + scale_vec) + shift_vec


def norm_back(hidden, scale_vec, grad):
    centre = hidden - jnp.mean(hidden, axis=-1, keepdims=True)
    inv = lax.rsqrt(jnp.mean(centre * centre, axis=-1, keepdims=True) + norm_eps)
    unit = centre * inv
    grad = grad * (1.0 + scale_vec)
    return inv * (grad - jnp.mean(grad, axis=-1, keepdims=True) - unit * jnp.mean(grad * unit, axis=-1, keepdims=True))


def core_half(value, first):
    value = value.astype(bf)
    half = value.shape[-2] // 2
    low, high = value[..., :half, :], value[..., half:, :]
    kept, given = jnp.where(first, low, high), jnp.where(first, high, low)
    return (kept.astype(f32) + swap(given, "dp", 1).astype(f32)).astype(bf)


def core_whole(value, first):
    total = (value.astype(f32) + swap(value, "dp", 2).astype(f32)).astype(bf)
    other = swap(total, "dp", 1)
    return jnp.concatenate([jnp.where(first, total, other), jnp.where(first, other, total)], axis=0).astype(f32)


def local(streams, modulation, w_qkv, w_out, w_zero, pairing, positions, cotangent):
    on_main = lax.axis_index("section") == 1
    core = lax.axis_index("dp") % 2
    first = core == 0
    mods = modulation[0]
    pair_row = pairing[0]
    width = streams.shape[-1]
    qkv_w = [arrange(w_qkv[0, k, 0]) for k in range(2)]
    out_w = [pad_rows(w_out[0, k, 0], HP) for k in range(2)]

    def own_half(w):
        rows = w.shape[0] // 2
        return lax.dynamic_slice_in_dim(w, core * rows, rows, axis=0)

    def gather(x):
        return lax.all_gather(x, "seq", axis=0, tiled=False)

    def rows_of(w):
        return w.reshape(-1, width)

    def halves_of(x):
        rows = x.shape[1] // 2
        low, high = x[:, :rows], x[:, rows:]
        mine = jnp.where(first, low, high)
        theirs = jnp.where(first, high, low)
        return mine.reshape(-1, x.shape[2]), theirs.reshape(-1, x.shape[2])

    def to_heads(w_pair, x):
        mine, theirs = [nt(rows_of(w), x).reshape(w.shape[:2] + x.shape[:1]) for w in w_pair]
        return jnp.where(first, mine, theirs), jnp.where(first, theirs, mine)

    def from_heads(w_pair, x):
        mine, theirs = halves_of(x)
        return tn(mine, rows_of(w_pair[0])) + tn(theirs, rows_of(w_pair[1]))

    def with_other(x):
        return (x, swap(x, "dp", 1))

    hidden0 = streams[0, 0].astype(f32)
    normed0 = modulated_norm(hidden0, mods[0, 0], mods[0, 1]).astype(bf)
    row_tokens = jnp.concatenate(around(normed0, False), axis=0)
    row_places = jnp.concatenate(around(positions, False))
    column_w = with_other(jnp.stack(around(own_half(qkv_w[0]), True)))
    low, high = to_heads(column_w, row_tokens)
    qkv0 = rope(low[:, :HALF], low[:, HALF:HP], low[:, HP:], high[:, :HALF], high[:, HALF:], *angle_tables(row_places))
    pieces = home(qkv0, True)
    at = lax.axis_index("seq")
    at_z, at_y = at // RINGS, at % RINGS
    places = jnp.stack([(at_z + z) % RINGS * RINGS + (at_y + y) % RINGS for z in FROM for y in FROM]).astype(jnp.int32)

    cells = jnp.stack([positions // GRID_W, positions % GRID_W]).astype(bf)
    cells = jnp.pad(cells, ((0, 6), (0, width - cells.shape[1])))
    piece_1 = gather(jnp.concatenate([own_half(out_w[0]), own_half(out_w[1]), own_half(qkv_w[1]), cells], axis=0))
    qkv0, mixed0, mixed0_rings, log_sums0 = attn_fwd(pieces, places)
    piece_1 = lax.optimization_barrier((piece_1, log_sums0))[0]
    cuts = (HP // 2, HP, HP + 3 * HP // 2)
    out_full0 = with_other(piece_1[:, : cuts[0]])
    out_full1 = with_other(piece_1[:, cuts[0] : cuts[1]])
    qkv_full1 = with_other(piece_1[:, cuts[1] : cuts[2]])
    cells_all = piece_1[:, cuts[2] : cuts[2] + 2, :TB].astype(jnp.int32)
    cos_all, sin_all = angle_tables((cells_all[:, 0] * GRID_W + cells_all[:, 1]).reshape(-1))
    cos_own, sin_own = angle_tables(positions)

    cot = cotangent[0]
    through = nt(cot, w_zero[1])
    grad2 = jnp.where(on_main, cot.astype(f32), jnp.where(pair_row[1] == 1, through, 0.0))
    d_attn1 = (mods[1, 2] * grad2).astype(bf)
    early_all = gather(lax.optimization_barrier((jnp.concatenate([normed0, d_attn1], axis=0), log_sums0))[0])

    mixed0_own = scatter_heads(mixed0)
    low, high = to_heads(out_full1, d_attn1)
    d_mixed1 = lax.optimization_barrier((jnp.concatenate([low, high], axis=1).astype(bf), mixed0_own))[0]
    d_mixed1 = scatter_heads(d_mixed1)
    attn0 = from_heads(out_full0, mixed0_own)
    hidden1 = hidden0 + mods[0, 2] * attn0
    zero0 = shifted(nn(hidden1.astype(bf), w_zero[0]).astype(bf), "section", 1).astype(f32)
    hidden1 = hidden1 + jnp.where(pair_row[0] == 0, zero0, 0.0)

    normed1 = modulated_norm(hidden1, mods[1, 0], mods[1, 1]).astype(bf)
    low, high = to_heads(qkv_full1, normed1)
    qkv1 = rope(low[:, :HALF], low[:, HALF:HP], low[:, HP:], high[:, :HALF], high[:, HALF:], cos_own, sin_own)
    mixed1, d_raw1, d_raw1_blocks = attn_both(scatter_heads(qkv1), d_mixed1, cos_all, sin_all)
    normed1_all = gather(lax.optimization_barrier((normed1, d_raw1, early_all))[0])
    d_normed1 = from_heads(qkv_full1, scatter_heads(d_raw1_blocks))
    grad1 = grad2 + norm_back(hidden1, mods[1, 1], d_normed1)

    sent = shifted(grad1.astype(bf), "section", -1)
    picked = jnp.where(pair_row[0] == 0, sent, cot)
    picked = jnp.where(on_main, jnp.zeros_like(picked), picked)
    grad1 = grad1 + nt(picked, w_zero[0])
    d_attn0 = (mods[0, 2] * grad1).astype(bf)
    low, high = to_heads(out_full0, d_attn0)
    d_mixed0 = scatter_heads(jnp.concatenate([low, high], axis=1).astype(bf))
    d_raw0_rings, d_raw0 = attn_bwd(qkv0, d_mixed0, mixed0, log_sums0, cos_all, sin_all, places)

    mixed1_first = lax.optimization_barrier((mixed1, d_mixed0))[0]
    attn1 = from_heads(out_full1, scatter_heads(mixed1_first))
    hidden2 = hidden1 + mods[1, 2] * attn1
    zero1 = shifted(nn(hidden2.astype(bf), w_zero[1]).astype(bf), "section", 1).astype(f32)
    hidden2 = hidden2 + jnp.where(pair_row[0] == 1, zero0, 0.0) + jnp.where(pair_row[1] == 1, zero1, 0.0)
    final_out = hidden2.astype(bf)[None, None]

    d_row0 = from_heads(column_w, jnp.stack(home(d_raw0_rings, True))).astype(bf).reshape(RINGS, -1, width)
    grad0 = grad1 + norm_back(hidden0, mods[0, 1], home_sum(d_row0, False))

    def tokens_last(x):
        return jnp.moveaxis(x, 0, 1).reshape(x.shape[1], -1)

    qkv_sums0 = core_whole(core_half(weight_grad(d_raw0, early_all, 0), first), first)
    block_1 = jnp.concatenate([weight_grad(d_raw1, normed1_all, 0), weight_grad(tokens_last(mixed1), early_all, 1)], axis=0)
    block_1 = core_whole(core_half(block_1, first), first)
    row_d_attn0 = jnp.concatenate(around(d_attn0, False), axis=0)
    mixed0_rings = jnp.stack(home(mixed0_rings, True))
    out_sums0 = lax.dot_general(mixed0_rings, row_d_attn0, (((2,), (0,)), ((), ())), preferred_element_type=f32)
    out_sums0 = core_whole(home_sum(core_half(out_sums0, first), True).astype(bf), first)
    grad_qkv = jnp.stack([disarrange(qkv_sums0), disarrange(block_1[: 3 * HP])])[None, :, None]
    grad_out = jnp.stack([out_sums0[:HS], block_1[3 * HP : 3 * HP + HS]])[None, :, None]
    return (final_out, grad0[None, None], grad_qkv, grad_out)


def solution(mesh):
    in_specs = (
        P("section", "dp", "seq", None),
        P("section", None, None, None),
        P("section", None, "seq", None, None, None),
        P("section", None, "seq", None, None),
        P(),
        P("dp", None),
        P("seq"),
        P("dp", "seq", None),
    )
    out_specs = (
        P("section", "dp", "seq", None),
        P("section", "dp", "seq", None),
        P("section", None, "seq", None, None, None),
        P("section", None, "seq", None, None),
    )
    return jax.shard_map(local, mesh=mesh, in_specs=in_specs, out_specs=out_specs, check_vma=False)
```

```python
import functools
import math

import jax
import jax.numpy as jnp
import numpy as np
from jax import lax
from jax.experimental import pallas as pl
from jax.experimental.pallas import tpu as pltpu
from jax.sharding import PartitionSpec as P

GRID_W = 128
HS = 72
HP = 80
HALF = 40
QB = 256
TB = 128
RINGS = 4
FROM = (0, -1, 1, 2)
SCALE = 1.0 / math.sqrt(HS)
EXP_SCALE = math.log2(math.e) / math.sqrt(HS)

norm_eps = 1e-06
bf = jnp.bfloat16
f32 = jnp.float32


def nn(a, b):
    return lax.dot_general(a, b, (((1,), (0,)), ((), ())), preferred_element_type=f32)


def nt(a, b):
    return lax.dot_general(a, b, (((1,), (1,)), ((), ())), preferred_element_type=f32)


def tn(a, b):
    return lax.dot_general(a, b, (((0,), (0,)), ((), ())), preferred_element_type=f32)


def flat(ref, to_ref):
    for j in range(ref.shape[0]):
        to_ref[:, j * TB : (j + 1) * TB] = ref[j]


def put(ref, i, value):
    for j in range(QB // TB):
        ref[i * (QB // TB) + j] = value[:, j * TB : (j + 1) * TB]


def by_rings(ref, to_ref, block):
    wide = ref.shape[2] // TB
    for z in range(ref.shape[0]):
        for y in range(wide):
            ref[z, :, y * TB : (y + 1) * TB] = block(to_ref[z * wide + y])


def turn_back(x, c, s):
    a, b = x[:HALF], x[HALF:]
    return jnp.concatenate([a * c + b * s, b * c - a * s], axis=0)


def with_ones(v):
    rows = lax.broadcasted_iota(jnp.int32, v.shape, 0)
    return jnp.where(rows == HS, 1.0, v.astype(f32)).astype(bf)


def whole(x):
    zeros = (0,) * x.ndim
    return pl.BlockSpec(x.shape, lambda i: zeros)


def fwd_kernel(to_ref, p0_ref, p1_ref, p2_ref, p3_ref, x_ref, o_ref, oz_ref, l_ref, kt_ref, vo_ref):
    i = pl.program_id(0)

    @pl.when(i == 0)
    def _():
        for at, piece in enumerate((p0_ref, p1_ref, p2_ref, p3_ref)):
            for j in range(piece.shape[1] // TB):
                place = pl.multiple_of(to_ref[at * (piece.shape[1] // TB) + j] * TB, TB)
                x_ref[:, pl.ds(place, TB)] = piece[:, j * TB : (j + 1) * TB]
        kt_ref[...] = x_ref[HP : 2 * HP].astype(f32).T.astype(bf)
        vo_ref[...] = with_ones(x_ref[2 * HP :])

    s = nn(kt_ref[...], x_ref[:HP, pl.ds(pl.multiple_of(i * QB, QB), QB)])
    m = jnp.max(s, axis=0, keepdims=True)
    e = jnp.exp2((s - m) * EXP_SCALE).astype(bf)
    o = nn(vo_ref[...], e)
    total = o[HS : HS + 1]
    rows = lax.broadcasted_iota(jnp.int32, o.shape, 0)
    put(o_ref, i, jnp.where(rows < HS, o * (1.0 / total), 0.0).astype(bf))
    l_ref[...] = m * EXP_SCALE + jnp.log2(total)

    @pl.when(i == pl.num_programs(0) - 1)
    def _():
        by_rings(oz_ref, to_ref, lambda block: o_ref[block])


def attn_fwd(pieces, places):
    n = sum(p.shape[1] for p in pieces)
    return pl.pallas_call(
        fwd_kernel,
        grid=(n // QB,),
        in_specs=[pl.BlockSpec(memory_space=pltpu.SMEM)] + [whole(p) for p in pieces],
        out_specs=[
            pl.BlockSpec((3 * HP, n), lambda i: (0, 0)),
            pl.BlockSpec((n // TB, HP, TB), lambda i: (0, 0, 0)),
            pl.BlockSpec((RINGS, HP, n // RINGS), lambda i: (0, 0, 0)),
            pl.BlockSpec((1, QB), lambda i: (0, i)),
        ],
        out_shape=[
            jax.ShapeDtypeStruct((3 * HP, n), bf),
            jax.ShapeDtypeStruct((n // TB, HP, TB), bf),
            jax.ShapeDtypeStruct((RINGS, HP, n // RINGS), bf),
            jax.ShapeDtypeStruct((1, n), f32),
        ],
        scratch_shapes=[pltpu.VMEM((n, HP), bf), pltpu.VMEM((HP, n), bf)],
        compiler_params=pltpu.CompilerParams(vmem_limit_bytes=40 * 2**20),
        cost_estimate=pl.CostEstimate(flops=4 * n * n * 256, bytes_accessed=2 * 4 * HP * n, transcendentals=n * n),
        name="attn_fwd",
    )(places, *pieces)


def prep(x_ref, kt_ref, vt_ref, dk_ref, dv_ref):
    kt_ref[...] = x_ref[HP : 2 * HP].astype(f32).T.astype(bf)
    vt_ref[...] = x_ref[2 * HP :].astype(f32).T.astype(bf)
    dk_ref[...] = jnp.zeros_like(dk_ref)
    dv_ref[...] = jnp.zeros_like(dv_ref)


def finish(i, dq, c_ref, s_ref, d_ref, dk_ref, dv_ref):
    at = pl.ds(pl.multiple_of(i * QB, QB), QB)
    d_ref[:HP, at] = turn_back(dq * SCALE, c_ref[:, at], s_ref[:, at]).astype(bf)

    @pl.when(i == pl.num_programs(0) - 1)
    def _():
        d_ref[HP : 2 * HP, :] = turn_back(dk_ref[...].T * SCALE, c_ref[...], s_ref[...]).astype(bf)
        d_ref[2 * HP :, :] = dv_ref[...].T.astype(bf)


def bwd_kernel(x_ref, g_ref, o_ref, l_ref, c_ref, s_ref, to_ref, dz_ref, db_ref, kt_ref, vt_ref, dk_ref, dv_ref, gx_ref, ox_ref, d_ref):
    i = pl.program_id(0)

    @pl.when(i == 0)
    def _():
        prep(x_ref, kt_ref, vt_ref, dk_ref, dv_ref)
        flat(g_ref, gx_ref)
        flat(o_ref, ox_ref)

    at = pl.ds(pl.multiple_of(i * QB, QB), QB)
    q = x_ref[:HP, at]
    g = gx_ref[:, at]
    p = jnp.exp2(nn(kt_ref[...], q) * EXP_SCALE - l_ref[...])
    delta = jnp.sum(g.astype(f32) * ox_ref[:, at].astype(f32), axis=0, keepdims=True)
    ds = (p * (nn(vt_ref[...], g) - delta)).astype(bf)
    dv_ref[...] += nt(p.astype(bf), g)
    dk_ref[...] += nt(ds, q)
    finish(i, nn(x_ref[HP : 2 * HP], ds), c_ref, s_ref, d_ref, dk_ref, dv_ref)

    @pl.when(i == pl.num_programs(0) - 1)
    def _():
        for j in range(db_ref.shape[0]):
            db_ref[j] = d_ref[:, j * TB : (j + 1) * TB]
        by_rings(dz_ref, to_ref, lambda block: db_ref[block])


def both_kernel(xb_ref, gb_ref, c_ref, s_ref, o_ref, db_ref, kt_ref, vt_ref, dk_ref, dv_ref, x_ref, g_ref, vo_ref, d_ref):
    i = pl.program_id(0)

    @pl.when(i == 0)
    def _():
        flat(xb_ref, x_ref)
        flat(gb_ref, g_ref)
        prep(x_ref, kt_ref, vt_ref, dk_ref, dv_ref)
        vo_ref[...] = with_ones(x_ref[2 * HP :])

    at = pl.ds(pl.multiple_of(i * QB, QB), QB)
    q = x_ref[:HP, at]
    s = nn(kt_ref[...], q)
    m = jnp.max(s, axis=0, keepdims=True)
    e = jnp.exp2((s - m) * EXP_SCALE)
    eb = e.astype(bf)
    o = nn(vo_ref[...], eb)
    inv = 1.0 / o[HS : HS + 1]
    rows = lax.broadcasted_iota(jnp.int32, o.shape, 0)
    o = jnp.where(rows < HS, o * inv, 0.0)
    put(o_ref, i, o.astype(bf))
    g = g_ref[:, at].astype(f32) * inv
    delta = jnp.sum(g * o, axis=0, keepdims=True)
    g = g.astype(bf)
    ds = (e * (nn(vt_ref[...], g) - delta)).astype(bf)
    dv_ref[...] += nt(eb, g)
    dk_ref[...] += nt(ds, q)
    finish(i, nn(x_ref[HP : 2 * HP], ds), c_ref, s_ref, d_ref, dk_ref, dv_ref)

    @pl.when(i == pl.num_programs(0) - 1)
    def _():
        for j in range(db_ref.shape[0]):
            db_ref[j] = d_ref[:, j * TB : (j + 1) * TB]


def back_call(kernel, ins, in_specs, n, out_shape, extra_scratch, name):
    scratch = [pltpu.VMEM((n, HP), bf), pltpu.VMEM((n, HP), bf), pltpu.VMEM((n, HP), f32), pltpu.VMEM((n, HP), f32)]
    return pl.pallas_call(
        kernel,
        grid=(n // QB,),
        in_specs=in_specs,
        out_specs=[whole(x) for x in out_shape],
        out_shape=out_shape,
        scratch_shapes=scratch + extra_scratch,
        compiler_params=pltpu.CompilerParams(vmem_limit_bytes=48 * 2**20),
        cost_estimate=pl.CostEstimate(flops=10 * n * n * 256, bytes_accessed=2 * 12 * HP * n, transcendentals=n * n),
        name=name,
    )(*ins)


def attn_bwd(x, g, o, l, c, s, places):
    n = x.shape[1]
    specs = [whole(x), whole(g), whole(o), pl.BlockSpec((1, QB), lambda i: (0, i)), whole(c), whole(s)]
    specs += [pl.BlockSpec(memory_space=pltpu.SMEM)]
    extra = [pltpu.VMEM((HP, n), bf), pltpu.VMEM((HP, n), bf), pltpu.VMEM((3 * HP, n), bf)]
    out = [jax.ShapeDtypeStruct((RINGS, 3 * HP, n // RINGS), bf), jax.ShapeDtypeStruct((n // TB, 3 * HP, TB), bf)]
    return back_call(bwd_kernel, (x, g, o, l, c, s, places), specs, n, out, extra, "attn_bwd")


def attn_both(x, g, c, s):
    n = x.shape[0] * TB
    extra = [pltpu.VMEM((3 * HP, n), bf), pltpu.VMEM((HP, n), bf), pltpu.VMEM((HP, n), bf), pltpu.VMEM((3 * HP, n), bf)]
    out = [
        jax.ShapeDtypeStruct((n // TB, HP, TB), bf),
        jax.ShapeDtypeStruct((n // TB, 3 * HP, TB), bf),
    ]
    return back_call(both_kernel, (x, g, c, s), [whole(x), whole(g), whole(c), whole(s)], n, out, extra, "attn_both")


def grad_kernel(p_ref, x_ref, g_ref, out_ref, acc_ref):
    i = pl.program_id(0)

    @pl.when(i == 0)
    def _():
        acc_ref[...] = jnp.zeros_like(acc_ref)

    x = jnp.concatenate([x_ref[j] for j in range(x_ref.shape[0])], axis=1)
    x = nn(p_ref[...], x).astype(bf)
    acc_ref[...] += nn(x, g_ref[...].reshape(x.shape[1], -1))

    @pl.when(i == pl.num_programs(0) - 1)
    def _():
        out_ref[...] = acc_ref[...].astype(bf)


def weight_grad(order, x, gathered, part):
    blocks, _, width = gathered.shape
    step = 4
    pick = np.zeros((len(order), x.shape[1]), np.float32)
    pick[np.arange(len(order)), order] = 1.0
    pick = jnp.asarray(pick, bf)
    return pl.pallas_call(
        grad_kernel,
        grid=(blocks // step,),
        in_specs=[
            whole(pick),
            pl.BlockSpec((step,) + x.shape[1:], lambda i: (i, 0, 0)),
            pl.BlockSpec((step, TB, width), lambda i: (i, part, 0)),
        ],
        out_specs=pl.BlockSpec((len(order), width), lambda i: (0, 0)),
        out_shape=jax.ShapeDtypeStruct((len(order), width), bf),
        scratch_shapes=[pltpu.VMEM((len(order), width), f32)],
        compiler_params=pltpu.CompilerParams(vmem_limit_bytes=60 * 2**20),
        cost_estimate=pl.CostEstimate(
            flops=2 * x.shape[1] * blocks * TB * width, bytes_accessed=2 * blocks * TB * width, transcendentals=0
        ),
        name="weight_grad",
    )(pick, x, gathered)


GROUPS = 4


def fetch(mine_ref, theirs_ref, buf_ref, sems, at):
    heads = buf_ref.shape[0] // GROUPS
    count = buf_ref.shape[1] // 2
    copies = []
    for g in range(GROUPS):
        for k, ref in enumerate((mine_ref, theirs_ref)):
            copies.append(
                pltpu.make_async_copy(
                    ref.at[pl.ds(g * heads, heads), pl.ds(at, count), :],
                    buf_ref.at[pl.ds(g * heads, heads), pl.ds(k * count, count), :],
                    sems.at[g, k],
                )
            )
    for copy in copies:
        copy.start()
    return copies


def qkv_kernel(at, first_ref, x_ref, c_ref, s_ref, mine_ref, theirs_ref, out_ref, buf_ref, sems):
    copies = fetch(mine_ref, theirs_ref, buf_ref, sems, at)
    x, c, s = x_ref[...], c_ref[...], s_ref[...]
    first = first_ref[0] == 1
    count = buf_ref.shape[1] // 2
    heads = buf_ref.shape[0] // GROUPS
    for g in range(GROUPS):
        copies[2 * g].wait()
        copies[2 * g + 1].wait()
        for h in range(g * heads, (g + 1) * heads):
            raw = nt(buf_ref[h], x)
            low = jnp.where(first, raw[:count], raw[count:])
            high = jnp.where(first, raw[count:], raw[:count])
            qa, qb, ka = low[:HALF], low[HALF:HP], low[HP : HP + HALF]
            kb, v = high[:HALF], high[HALF : HALF + HP]
            parts = [qa * c - qb * s, qa * s + qb * c, ka * c - kb * s, ka * s + kb * c, v]
            out_ref[h] = jnp.concatenate(parts, axis=0).astype(bf)


def grad_in_kernel(at, sub, first_ref, x_ref, mine_ref, theirs_ref, out_ref, buf_ref, sems):
    copies = fetch(mine_ref, theirs_ref, buf_ref, sems, at)
    x = x_ref[...]
    first = first_ref[0] == 1
    count = buf_ref.shape[1] // 2
    heads = buf_ref.shape[0] // GROUPS
    for g in range(GROUPS):
        copies[2 * g].wait()
        copies[2 * g + 1].wait()
        for h in range(g * heads, (g + 1) * heads):
            raw = nt(buf_ref[h], x)
            mine, theirs = raw[sub : sub + HALF], raw[count + sub : count + sub + HALF]
            parts = [jnp.where(first, mine, theirs), jnp.where(first, theirs, mine)]
            out_ref[h] = jnp.concatenate(parts, axis=0).astype(bf)


def sum_kernel(at, sub, first_ref, x_ref, mine_ref, theirs_ref, out_ref, buf_ref, sems):
    copies = fetch(mine_ref, theirs_ref, buf_ref, sems, at)
    first = first_ref[0] == 1
    count = buf_ref.shape[1] // 2
    heads = buf_ref.shape[0] // GROUPS
    rows = x_ref.shape[1] // 2
    total = jnp.zeros(out_ref.shape, f32)

    def in_place(x):
        parts = [jnp.zeros((sub, x.shape[1]), f32)] if sub else []
        parts.append(x)
        if sub + rows < count:
            parts.append(jnp.zeros((count - sub - rows, x.shape[1]), f32))
        return parts

    for g in range(GROUPS):
        copies[2 * g].wait()
        copies[2 * g + 1].wait()
        for h in range(g * heads, (g + 1) * heads):
            x = x_ref[h].astype(f32)
            low, high = x[:rows], x[rows:]
            parts = in_place(jnp.where(first, low, high)) + in_place(jnp.where(first, high, low))
            total = total + tn(jnp.concatenate(parts, axis=0).astype(bf), buf_ref[h])
    out_ref[...] = total


def with_weights(kernel, first, ins, w_pair, count, out_shape, name):
    heads, _, width = w_pair[0].shape
    in_hbm = pl.BlockSpec(memory_space=pltpu.HBM)
    flops = 2 * heads * 2 * count * TB * width
    return pl.pallas_call(
        kernel,
        in_specs=[pl.BlockSpec(memory_space=pltpu.SMEM)] + [pl.BlockSpec(memory_space=pltpu.VMEM) for _ in ins] + [in_hbm, in_hbm],
        out_specs=pl.BlockSpec(memory_space=pltpu.VMEM),
        out_shape=out_shape,
        scratch_shapes=[pltpu.VMEM((heads, 2 * count, width), bf), pltpu.SemaphoreType.DMA((GROUPS, 2))],
        compiler_params=pltpu.CompilerParams(vmem_limit_bytes=58 * 2**20),
        cost_estimate=pl.CostEstimate(flops=flops, bytes_accessed=4 * heads * count * width, transcendentals=0),
        name=name,
    )(first, *ins, *w_pair)


def swap(value, axis, bit):
    count = lax.axis_size(axis)
    return lax.ppermute(value, axis, [(i, i ^ bit) for i in range(count)])


def shifted(value, axis, by):
    count = lax.axis_size(axis)
    pairs = [(i, i + by) for i in range(count) if 0 <= i + by < count]
    return lax.ppermute(value, axis, pairs)


def move(value, along_z, by):
    pairs = []
    for i in range(RINGS * RINGS):
        z, y = i // RINGS, i % RINGS
        to = (z + by) % RINGS * RINGS + y if along_z else z * RINGS + (y + by) % RINGS
        pairs.append((i, to))
    return lax.ppermute(value, "seq", pairs)


def around(x, along_z):
    return [x] + [move(x, along_z, -by) for by in FROM[1:]]


def home(parts, along_z):
    got = [parts[0]] + [move(parts[i], along_z, FROM[i]) for i in range(1, RINGS)]
    return [got[0], got[2], got[1], got[3]]


def home_sum(parts, along_z):
    first, *rest = [x.astype(f32) for x in home(parts, along_z)]
    return first + rest[0] + rest[1] + rest[2]


def together(*values):
    return lax.optimization_barrier(values)


def scatter_heads(value):
    return lax.all_to_all(value, "seq", split_axis=0, concat_axis=0, tiled=True)


def angle_tables(places):
    quarter = HS // 4
    freqs = jnp.exp(-math.log(10000.0) * jnp.arange(quarter, dtype=f32) / quarter)
    grid_rows = (places // GRID_W).astype(f32)
    grid_cols = (places % GRID_W).astype(f32)
    angles = jnp.concatenate(
        [
            freqs[:, None] * grid_rows[None, :],
            freqs[:, None] * grid_cols[None, :],
            jnp.zeros((HALF - 2 * quarter, places.shape[0]), f32),
        ],
        axis=0,
    )
    return jnp.cos(angles), jnp.sin(angles)


def pad_rows(x, count):
    return jnp.pad(x, ((0, count - x.shape[0]), (0, 0)))


def arrange(w):
    qt = HS // 4
    parts = []
    for part in (w[0], w[1]):
        parts += [pad_rows(jnp.concatenate([part[0:qt], part[2 * qt : 3 * qt]]), HALF)]
        parts += [pad_rows(jnp.concatenate([part[qt : 2 * qt], part[3 * qt :]]), HALF)]
    return jnp.concatenate(parts + [pad_rows(w[2], HP)], axis=0)


def natural_order():
    qt = HS // 4
    order = []
    for at in (0, HP):
        for start in (at, at + HALF, at + qt, at + HALF + qt):
            order += range(start, start + qt)
    return order + list(range(2 * HP, 2 * HP + HS))


def rope(qa, qb, ka, kb, v, c, s):
    return jnp.concatenate([qa * c - qb * s, qa * s + qb * c, ka * c - kb * s, ka * s + kb * c, v], axis=-2).astype(bf)


def modulated_norm(hidden, shift_vec, scale_vec):
    centre = hidden - jnp.mean(hidden, axis=-1, keepdims=True)
    spread = jnp.mean(centre * centre, axis=-1, keepdims=True)
    return centre * lax.rsqrt(spread + norm_eps) * (1.0 + scale_vec) + shift_vec


def norm_back(hidden, scale_vec, grad):
    centre = hidden - jnp.mean(hidden, axis=-1, keepdims=True)
    inv = lax.rsqrt(jnp.mean(centre * centre, axis=-1, keepdims=True) + norm_eps)
    unit = centre * inv
    grad = grad * (1.0 + scale_vec)
    return inv * (grad - jnp.mean(grad, axis=-1, keepdims=True) - unit * jnp.mean(grad * unit, axis=-1, keepdims=True))


def half_rows(rows):
    return -(-rows // 32) * 16


def core_half(value, first):
    rows = value.shape[-2]
    half = half_rows(rows)
    low, high = value[..., :half, :], value[..., rows - half :, :]
    kept, given = jnp.where(first, low, high), jnp.where(first, high, low)
    return (kept.astype(f32) + swap(given, "dp", 1).astype(f32)).astype(bf)


def core_whole(value, first, rows):
    total = (value.astype(f32) + swap(value, "dp", 2).astype(f32)).astype(bf)
    other = swap(total, "dp", 1)
    low, high = jnp.where(first, total, other), jnp.where(first, other, total)
    return jnp.concatenate([low, high[2 * value.shape[0] - rows :]], axis=0).astype(f32)


def local(streams, modulation, w_qkv, w_out, w_zero, pairing, positions, cotangent):
    on_main = lax.axis_index("section") == 1
    core = lax.axis_index("dp") % 2
    first = core == 0
    mods = modulation[0]
    pair_row = pairing[0]
    width = streams.shape[-1]
    qkv_w = [arrange(w_qkv[0, k, 0]) for k in range(2)]
    out_w = [pad_rows(w_out[0, k, 0], HP) for k in range(2)]

    def own_half(w):
        rows = w.shape[0] // 2
        return lax.dynamic_slice_in_dim(w, core * rows, rows, axis=0)

    def gather(x):
        return lax.all_gather(x, "seq", axis=0, tiled=False)

    def rows_of(w):
        return w.reshape(-1, width)

    def halves_of(x):
        rows = x.shape[1] // 2
        low, high = x[:, :rows], x[:, rows:]
        mine = jnp.where(first, low, high)
        theirs = jnp.where(first, high, low)
        return mine.reshape(-1, x.shape[2]), theirs.reshape(-1, x.shape[2])

    def to_heads(w_pair, x):
        mine, theirs = [nt(rows_of(w), x).reshape(w.shape[:2] + x.shape[:1]) for w in w_pair]
        return jnp.where(first, mine, theirs), jnp.where(first, theirs, mine)

    def from_heads(w_pair, x):
        mine, theirs = halves_of(x)
        return tn(mine, rows_of(w_pair[0])) + tn(theirs, rows_of(w_pair[1]))

    def with_other(x):
        return (x, swap(x, "dp", 1))

    cot = cotangent[0]
    through = nt(cot, w_zero[1])
    grad2 = jnp.where(on_main, cot.astype(f32), jnp.where(pair_row[1] == 1, through, 0.0))
    d_attn1 = (mods[1, 2] * grad2).astype(bf)
    hidden0 = streams[0, 0].astype(f32)
    normed0 = modulated_norm(hidden0, mods[0, 0], mods[0, 1]).astype(bf)
    row_tokens = jnp.concatenate(around(normed0, False), axis=0)
    row_places = jnp.concatenate(around(positions, False))
    column_w = with_other(jnp.stack(around(own_half(qkv_w[0]), True)))
    low, high = to_heads(column_w, row_tokens)
    qkv0 = rope(low[:, :HALF], low[:, HALF:HP], low[:, HP:], high[:, :HALF], high[:, HALF:], *angle_tables(row_places))
    pieces = home(qkv0, True)
    at = lax.axis_index("seq")
    at_z, at_y = at // RINGS, at % RINGS
    places = jnp.stack([(at_z + z) % RINGS * RINGS + (at_y + y) % RINGS for z in FROM for y in FROM]).astype(jnp.int32)

    cells = jnp.stack([positions // GRID_W, positions % GRID_W]).astype(bf)
    cells = jnp.pad(cells, ((0, 6), (0, width - cells.shape[1])))
    piece_1 = gather(jnp.concatenate([own_half(qkv_w[1]), cells, own_half(out_w[0]), own_half(out_w[1])], axis=0))
    pieces, d_attn1 = together(pieces, d_attn1)
    qkv0, mixed0, mixed0_rings, log_sums0 = attn_fwd(pieces, places)
    mixed0_own = scatter_heads(mixed0)
    piece_1, mixed0_own = lax.optimization_barrier((piece_1, mixed0_own))
    cut = 3 * HP // 2 + 8
    full_1 = with_other(piece_1)
    cells_all = piece_1[:, 3 * HP // 2 : 3 * HP // 2 + 2, :TB].astype(jnp.int32)
    cos_all, sin_all = angle_tables((cells_all[:, 0] * GRID_W + cells_all[:, 1]).reshape(-1))
    cos_own, sin_own = angle_tables(positions)

    first_flag = jnp.where(first, 1, 0).astype(jnp.int32).reshape(1)
    heads = lax.axis_size("seq")

    def to_mixed(block, d_attn):
        kernel = functools.partial(grad_in_kernel, cut, block * HALF)
        shape = jax.ShapeDtypeStruct((heads, HP, TB), bf)
        return with_weights(kernel, first_flag, (d_attn,), full_1, HP, shape, "to_mixed")

    def from_mixed(block, mixed):
        kernel = functools.partial(sum_kernel, cut, block * HALF)
        shape = jax.ShapeDtypeStruct((TB, width), f32)
        return with_weights(kernel, first_flag, (mixed,), full_1, HP, shape, "from_mixed")

    early, mixed0_own = together(jnp.concatenate([normed0, d_attn1], axis=0), mixed0_own)
    early_all = gather(early)

    d_mixed1 = scatter_heads(to_mixed(1, d_attn1))
    attn0 = from_mixed(0, mixed0_own)
    hidden1 = hidden0 + mods[0, 2] * attn0
    zero0 = shifted(nn(hidden1.astype(bf), w_zero[0]).astype(bf), "section", 1).astype(f32)
    hidden1 = hidden1 + jnp.where(pair_row[0] == 0, zero0, 0.0)

    normed1 = modulated_norm(hidden1, mods[1, 0], mods[1, 1]).astype(bf)
    shape = jax.ShapeDtypeStruct((heads, 3 * HP, TB), bf)
    ins = (normed1, cos_own, sin_own)
    qkv1 = with_weights(functools.partial(qkv_kernel, 0), first_flag, ins, full_1, cut, shape, "to_qkv")
    qkv1, d_mixed1 = together(qkv1, d_mixed1)
    qkv1 = scatter_heads(qkv1)
    mixed0_rings, qkv1 = together(mixed0_rings, qkv1)
    mixed0_rings = home(mixed0_rings, True)
    mixed1, d_raw1 = attn_both(qkv1, d_mixed1, cos_all, sin_all)
    mixed1, d_raw1, mixed0_rings = together(mixed1, d_raw1, mixed0_rings)
    order = natural_order()
    plain = list(range(HS))
    out_grad1 = weight_grad(plain, mixed1, early_all, 1)
    d_raw1_own, out_grad1, mixed1, normed1, early_all = together(scatter_heads(d_raw1), out_grad1, mixed1, normed1, early_all)
    mixed1_own = scatter_heads(mixed1)
    normed1_all = gather(normed1)
    shape = jax.ShapeDtypeStruct((TB, width), f32)
    ins = (d_raw1_own,)
    d_normed1 = with_weights(functools.partial(sum_kernel, 0, 0), first_flag, ins, full_1, cut, shape, "from_qkv")
    grad1 = grad2 + norm_back(hidden1, mods[1, 1], d_normed1)

    sent = shifted(grad1.astype(bf), "section", -1)
    picked = jnp.where(pair_row[0] == 0, sent, cot)
    picked = jnp.where(on_main, jnp.zeros_like(picked), picked)
    grad1 = grad1 + nt(picked, w_zero[0])
    d_attn0 = (mods[0, 2] * grad1).astype(bf)
    d_mixed0 = to_mixed(0, d_attn0)

    mixed1_own, d_mixed0 = together(mixed1_own, d_mixed0)
    attn1 = from_mixed(1, mixed1_own)
    hidden2 = hidden1 + mods[1, 2] * attn1
    zero1 = nn(hidden2.astype(bf), w_zero[1]).astype(bf)
    d_mixed0, zero1 = together(scatter_heads(d_mixed0), zero1)
    zero1 = shifted(zero1, "section", 1)

    d_raw0_rings, d_raw0 = attn_bwd(qkv0, d_mixed0, mixed0, log_sums0, cos_all, sin_all, places)
    d_raw0_rings, d_attn0 = together(d_raw0_rings, d_attn0)

    homed = home(d_raw0_rings, True)
    grads = [weight_grad(order, d_raw0, early_all, 0), weight_grad(order, d_raw1, normed1_all, 0)]
    row_d_attn0 = around(d_attn0, False)
    homed, grads, zero1, row_d_attn0 = together(homed, grads, zero1, row_d_attn0)

    zero1 = zero1.astype(f32)
    hidden2 = hidden2 + jnp.where(pair_row[0] == 1, zero0, 0.0) + jnp.where(pair_row[1] == 1, zero1, 0.0)
    final_out = hidden2.astype(bf)[None, None]

    d_row0 = from_heads(column_w, jnp.stack(homed)).astype(bf).reshape(RINGS, -1, width)
    grad0 = grad1 + norm_back(hidden0, mods[0, 1], home_sum(d_row0, False))

    grads = jnp.concatenate(grads + [out_grad1], axis=0)
    grads = core_whole(core_half(grads, first), first, grads.shape[0])
    out_grad0 = lax.dot_general(jnp.stack(mixed0_rings), jnp.concatenate(row_d_attn0, axis=0), (((2,), (0,)), ((), ())), preferred_element_type=f32)
    out_grad0 = home_sum(core_half(out_grad0.astype(bf), first), True).astype(bf)
    out_grad0 = core_whole(out_grad0, first, HP)
    rows = len(order)
    grad_qkv = grads[: 2 * rows].reshape(1, 2, 1, 3, HS, width)
    grad_out = jnp.stack([out_grad0[:HS], grads[2 * rows :]])[None, :, None]
    return (final_out, grad0[None, None], grad_qkv, grad_out)


def solution(mesh):
    in_specs = (
        P("section", "dp", "seq", None),
        P("section", None, None, None),
        P("section", None, "seq", None, None, None),
        P("section", None, "seq", None, None),
        P(),
        P("dp", None),
        P("seq"),
        P("dp", "seq", None),
    )
    out_specs = (
        P("section", "dp", "seq", None),
        P("section", "dp", "seq", None),
        P("section", None, "seq", None, None, None),
        P("section", None, "seq", None, None),
    )
    return jax.shard_map(local, mesh=mesh, in_specs=in_specs, out_specs=out_specs, check_vma=False)
```

```python
import functools
import math

import jax
import jax.numpy as jnp
import numpy as np
from jax import lax
from jax.experimental import pallas as pl
from jax.experimental.pallas import tpu as pltpu
from jax.sharding import PartitionSpec as P

GRID_W = 128
HS = 72
HP = 80
HALF = 40
QB = 1024
TB = 128
RINGS = 4
FROM = (0, -1, 1, 2)
SCALE = 1.0 / math.sqrt(HS)
EXP_SCALE = math.log2(math.e) / math.sqrt(HS)

norm_eps = 1e-06
bf = jnp.bfloat16
f32 = jnp.float32


def nn(a, b):
    return lax.dot_general(a, b, (((1,), (0,)), ((), ())), preferred_element_type=f32)


def nt(a, b):
    return lax.dot_general(a, b, (((1,), (1,)), ((), ())), preferred_element_type=f32)


def tn(a, b):
    return lax.dot_general(a, b, (((0,), (0,)), ((), ())), preferred_element_type=f32)


def flat(ref, to_ref):
    for j in range(ref.shape[0]):
        to_ref[:, j * TB : (j + 1) * TB] = ref[j]


def put(ref, i, value):
    for j in range(QB // TB):
        ref[i * (QB // TB) + j] = value[:, j * TB : (j + 1) * TB]


def by_rings(ref, to_ref, block):
    wide = ref.shape[2] // TB
    for z in range(ref.shape[0]):
        for y in range(wide):
            ref[z, :, y * TB : (y + 1) * TB] = block(to_ref[z * wide + y])


def turn_back(x, c, s):
    a, b = x[:HALF], x[HALF:]
    return jnp.concatenate([a * c + b * s, b * c - a * s], axis=0)


def with_ones(v):
    rows = lax.broadcasted_iota(jnp.int32, v.shape, 0)
    return jnp.where(rows == HS, 1.0, v.astype(f32)).astype(bf)


def whole(x):
    zeros = (0,) * x.ndim
    return pl.BlockSpec(x.shape, lambda i: zeros)


def fwd_kernel(to_ref, p0_ref, p1_ref, p2_ref, p3_ref, x_ref, o_ref, l_ref, kt_ref, vo_ref):
    i = pl.program_id(0)

    @pl.when(i == 0)
    def _():
        for at, piece in enumerate((p0_ref, p1_ref, p2_ref, p3_ref)):
            for j in range(piece.shape[1] // TB):
                place = pl.multiple_of(to_ref[at * (piece.shape[1] // TB) + j] * TB, TB)
                x_ref[:, pl.ds(place, TB)] = piece[:, j * TB : (j + 1) * TB]
        kt_ref[...] = x_ref[HP : 2 * HP].astype(f32).T.astype(bf)
        vo_ref[...] = with_ones(x_ref[2 * HP :])

    s = nn(kt_ref[...], x_ref[:HP, pl.ds(pl.multiple_of(i * QB, QB), QB)])
    m = jnp.max(s, axis=0, keepdims=True)
    e = jnp.exp2((s - m) * EXP_SCALE).astype(bf)
    o = nn(vo_ref[...], e)
    total = o[HS : HS + 1]
    rows = lax.broadcasted_iota(jnp.int32, o.shape, 0)
    put(o_ref, i, jnp.where(rows < HS, o * (1.0 / total), 0.0).astype(bf))
    l_ref[...] = m * EXP_SCALE + jnp.log2(total)


def attn_fwd(pieces, places):
    n = sum(p.shape[1] for p in pieces)
    return pl.pallas_call(
        fwd_kernel,
        grid=(n // QB,),
        in_specs=[pl.BlockSpec(memory_space=pltpu.SMEM)] + [whole(p) for p in pieces],
        out_specs=[
            pl.BlockSpec((3 * HP, n), lambda i: (0, 0)),
            pl.BlockSpec((n // TB, HP, TB), lambda i: (0, 0, 0)),
            pl.BlockSpec((1, QB), lambda i: (0, i)),
        ],
        out_shape=[
            jax.ShapeDtypeStruct((3 * HP, n), bf),
            jax.ShapeDtypeStruct((n // TB, HP, TB), bf),
            jax.ShapeDtypeStruct((1, n), f32),
        ],
        scratch_shapes=[pltpu.VMEM((n, HP), bf), pltpu.VMEM((HP, n), bf)],
        compiler_params=pltpu.CompilerParams(vmem_limit_bytes=40 * 2**20),
        cost_estimate=pl.CostEstimate(flops=4 * n * n * 256, bytes_accessed=2 * 4 * HP * n, transcendentals=n * n),
        name="attn_fwd",
    )(places, *pieces)


def prep(x_ref, kt_ref, vt_ref, dk_ref, dv_ref):
    kt_ref[...] = x_ref[HP : 2 * HP].astype(f32).T.astype(bf)
    vt_ref[...] = x_ref[2 * HP :].astype(f32).T.astype(bf)
    dk_ref[...] = jnp.zeros_like(dk_ref)
    dv_ref[...] = jnp.zeros_like(dv_ref)


def finish(i, dq, c_ref, s_ref, d_ref, dk_ref, dv_ref):
    at = pl.ds(pl.multiple_of(i * QB, QB), QB)
    d_ref[:HP, at] = turn_back(dq * SCALE, c_ref[:, at], s_ref[:, at]).astype(bf)

    @pl.when(i == pl.num_programs(0) - 1)
    def _():
        d_ref[HP : 2 * HP, :] = turn_back(dk_ref[...].T * SCALE, c_ref[...], s_ref[...]).astype(bf)
        d_ref[2 * HP :, :] = dv_ref[...].T.astype(bf)


def bwd_kernel(x_ref, g_ref, o_ref, l_ref, c_ref, s_ref, to_ref, dz_ref, db_ref, kt_ref, vt_ref, dk_ref, dv_ref, gx_ref, ox_ref, d_ref):
    i = pl.program_id(0)

    @pl.when(i == 0)
    def _():
        prep(x_ref, kt_ref, vt_ref, dk_ref, dv_ref)
        flat(g_ref, gx_ref)
        flat(o_ref, ox_ref)

    at = pl.ds(pl.multiple_of(i * QB, QB), QB)
    q = x_ref[:HP, at]
    g = gx_ref[:, at]
    p = jnp.exp2(nn(kt_ref[...], q) * EXP_SCALE - l_ref[...])
    delta = jnp.sum(g.astype(f32) * ox_ref[:, at].astype(f32), axis=0, keepdims=True)
    ds = (p * (nn(vt_ref[...], g) - delta)).astype(bf)
    dv_ref[...] += nt(p.astype(bf), g)
    dk_ref[...] += nt(ds, q)
    finish(i, nn(x_ref[HP : 2 * HP], ds), c_ref, s_ref, d_ref, dk_ref, dv_ref)

    @pl.when(i == pl.num_programs(0) - 1)
    def _():
        for j in range(db_ref.shape[0]):
            db_ref[j] = d_ref[:, j * TB : (j + 1) * TB]
        by_rings(dz_ref, to_ref, lambda block: db_ref[block])


def both_kernel(xb_ref, gb_ref, c_ref, s_ref, o_ref, db_ref, kt_ref, vt_ref, dk_ref, dv_ref, x_ref, g_ref, vo_ref, d_ref):
    i = pl.program_id(0)

    @pl.when(i == 0)
    def _():
        flat(xb_ref, x_ref)
        flat(gb_ref, g_ref)
        prep(x_ref, kt_ref, vt_ref, dk_ref, dv_ref)
        vo_ref[...] = with_ones(x_ref[2 * HP :])

    at = pl.ds(pl.multiple_of(i * QB, QB), QB)
    q = x_ref[:HP, at]
    s = nn(kt_ref[...], q)
    m = jnp.max(s, axis=0, keepdims=True)
    e = jnp.exp2((s - m) * EXP_SCALE)
    eb = e.astype(bf)
    o = nn(vo_ref[...], eb)
    inv = 1.0 / o[HS : HS + 1]
    rows = lax.broadcasted_iota(jnp.int32, o.shape, 0)
    o = jnp.where(rows < HS, o * inv, 0.0)
    put(o_ref, i, o.astype(bf))
    g = g_ref[:, at].astype(f32) * inv
    delta = jnp.sum(g * o, axis=0, keepdims=True)
    g = g.astype(bf)
    ds = (e * (nn(vt_ref[...], g) - delta)).astype(bf)
    dv_ref[...] += nt(eb, g)
    dk_ref[...] += nt(ds, q)
    finish(i, nn(x_ref[HP : 2 * HP], ds), c_ref, s_ref, d_ref, dk_ref, dv_ref)

    @pl.when(i == pl.num_programs(0) - 1)
    def _():
        for j in range(db_ref.shape[0]):
            db_ref[j] = d_ref[:, j * TB : (j + 1) * TB]


def back_call(kernel, ins, in_specs, n, out_shape, extra_scratch, name):
    scratch = [pltpu.VMEM((n, HP), bf), pltpu.VMEM((n, HP), bf), pltpu.VMEM((n, HP), f32), pltpu.VMEM((n, HP), f32)]
    return pl.pallas_call(
        kernel,
        grid=(n // QB,),
        in_specs=in_specs,
        out_specs=[whole(x) for x in out_shape],
        out_shape=out_shape,
        scratch_shapes=scratch + extra_scratch,
        compiler_params=pltpu.CompilerParams(vmem_limit_bytes=48 * 2**20),
        cost_estimate=pl.CostEstimate(flops=10 * n * n * 256, bytes_accessed=2 * 12 * HP * n, transcendentals=n * n),
        name=name,
    )(*ins)


def attn_bwd(x, g, o, l, c, s, places):
    n = x.shape[1]
    specs = [whole(x), whole(g), whole(o), pl.BlockSpec((1, QB), lambda i: (0, i)), whole(c), whole(s)]
    specs += [pl.BlockSpec(memory_space=pltpu.SMEM)]
    extra = [pltpu.VMEM((HP, n), bf), pltpu.VMEM((HP, n), bf), pltpu.VMEM((3 * HP, n), bf)]
    out = [jax.ShapeDtypeStruct((RINGS, 3 * HP, n // RINGS), bf), jax.ShapeDtypeStruct((n // TB, 3 * HP, TB), bf)]
    return back_call(bwd_kernel, (x, g, o, l, c, s, places), specs, n, out, extra, "attn_bwd")


def attn_both(x, g, c, s):
    n = x.shape[0] * TB
    extra = [pltpu.VMEM((3 * HP, n), bf), pltpu.VMEM((HP, n), bf), pltpu.VMEM((HP, n), bf), pltpu.VMEM((3 * HP, n), bf)]
    out = [
        jax.ShapeDtypeStruct((n // TB, HP, TB), bf),
        jax.ShapeDtypeStruct((n // TB, 3 * HP, TB), bf),
    ]
    return back_call(both_kernel, (x, g, c, s), [whole(x), whole(g), whole(c), whole(s)], n, out, extra, "attn_both")


PIECES = 4
STEP = 2


def grad_kernel(p_ref, x_ref, *refs):
    *pieces, out_ref, acc_ref = refs
    i = pl.program_id(0)

    @pl.when(i == 0)
    def _():
        acc_ref[...] = jnp.zeros_like(acc_ref)

    x = jnp.concatenate([x_ref[j] for j in range(x_ref.shape[0])], axis=1)
    x = nn(p_ref[...], x).astype(bf)
    wide = STEP * TB
    total = acc_ref[...]
    for j, piece in enumerate(pieces):
        total = total + nn(x[:, j * wide : (j + 1) * wide], piece[...].reshape(wide, -1))
    acc_ref[...] = total

    @pl.when(i == pl.num_programs(0) - 1)
    def _():
        out_ref[...] = acc_ref[...].astype(bf)


def weight_grad(order, x, gathered, part):
    blocks, _, width = gathered.shape
    pick = np.zeros((len(order), x.shape[1]), np.float32)
    pick[np.arange(len(order)), order] = 1.0
    pick = jnp.asarray(pick, bf)

    def piece(j):
        return pl.BlockSpec((STEP, TB, width), lambda i: (PIECES * i + j, part, 0))

    return pl.pallas_call(
        grad_kernel,
        grid=(blocks // (PIECES * STEP),),
        in_specs=[whole(pick), pl.BlockSpec((PIECES * STEP,) + x.shape[1:], lambda i: (i, 0, 0))]
        + [piece(j) for j in range(PIECES)],
        out_specs=pl.BlockSpec((len(order), width), lambda i: (0, 0)),
        out_shape=jax.ShapeDtypeStruct((len(order), width), bf),
        scratch_shapes=[pltpu.VMEM((len(order), width), f32)],
        compiler_params=pltpu.CompilerParams(vmem_limit_bytes=60 * 2**20),
        cost_estimate=pl.CostEstimate(flops=1, bytes_accessed=1, transcendentals=0),
        name="weight_grad",
    )(pick, x, *([gathered] * PIECES))


GROUPS = 4


def fetch(mine_ref, theirs_ref, buf_ref, sems, at):
    heads = buf_ref.shape[0] // GROUPS
    count = buf_ref.shape[1] // 2
    copies = []
    for g in range(GROUPS):
        for k, ref in enumerate((mine_ref, theirs_ref)):
            copies.append(
                pltpu.make_async_copy(
                    ref.at[pl.ds(g * heads, heads), pl.ds(at, count), :],
                    buf_ref.at[pl.ds(g * heads, heads), pl.ds(k * count, count), :],
                    sems.at[g, k],
                )
            )
    for copy in copies:
        copy.start()
    return copies


def qkv_kernel(at, first_ref, x_ref, c_ref, s_ref, mine_ref, theirs_ref, out_ref, buf_ref, sems):
    copies = fetch(mine_ref, theirs_ref, buf_ref, sems, at)
    x, c, s = x_ref[...], c_ref[...], s_ref[...]
    first = first_ref[0] == 1
    count = buf_ref.shape[1] // 2
    heads = buf_ref.shape[0] // GROUPS
    for g in range(GROUPS):
        copies[2 * g].wait()
        copies[2 * g + 1].wait()
        for h in range(g * heads, (g + 1) * heads):
            raw = nt(buf_ref[h], x)
            low = jnp.where(first, raw[:count], raw[count:])
            high = jnp.where(first, raw[count:], raw[:count])
            qa, qb, ka = low[:HALF], low[HALF:HP], low[HP : HP + HALF]
            kb, v = high[:HALF], high[HALF : HALF + HP]
            parts = [qa * c - qb * s, qa * s + qb * c, ka * c - kb * s, ka * s + kb * c, v]
            out_ref[h] = jnp.concatenate(parts, axis=0).astype(bf)


def grad_in_kernel(at, sub, first_ref, x_ref, mine_ref, theirs_ref, out_ref, buf_ref, sems):
    copies = fetch(mine_ref, theirs_ref, buf_ref, sems, at)
    x = x_ref[...]
    first = first_ref[0] == 1
    count = buf_ref.shape[1] // 2
    heads = buf_ref.shape[0] // GROUPS
    for g in range(GROUPS):
        copies[2 * g].wait()
        copies[2 * g + 1].wait()
        for h in range(g * heads, (g + 1) * heads):
            raw = nt(buf_ref[h], x)
            mine, theirs = raw[sub : sub + HALF], raw[count + sub : count + sub + HALF]
            parts = [jnp.where(first, mine, theirs), jnp.where(first, theirs, mine)]
            out_ref[h] = jnp.concatenate(parts, axis=0).astype(bf)


def sum_kernel(at, sub, first_ref, x_ref, mine_ref, theirs_ref, out_ref, buf_ref, sems):
    copies = fetch(mine_ref, theirs_ref, buf_ref, sems, at)
    first = first_ref[0] == 1
    count = buf_ref.shape[1] // 2
    heads = buf_ref.shape[0] // GROUPS
    rows = x_ref.shape[1] // 2
    total = jnp.zeros(out_ref.shape, f32)

    def in_place(x):
        parts = [jnp.zeros((sub, x.shape[1]), f32)] if sub else []
        parts.append(x)
        if sub + rows < count:
            parts.append(jnp.zeros((count - sub - rows, x.shape[1]), f32))
        return parts

    for g in range(GROUPS):
        copies[2 * g].wait()
        copies[2 * g + 1].wait()
        for h in range(g * heads, (g + 1) * heads):
            x = x_ref[h].astype(f32)
            low, high = x[:rows], x[rows:]
            parts = in_place(jnp.where(first, low, high)) + in_place(jnp.where(first, high, low))
            total = total + tn(jnp.concatenate(parts, axis=0).astype(bf), buf_ref[h])
    out_ref[...] = total


def with_weights(kernel, first, ins, w_pair, count, out_shape, name):
    heads, _, width = w_pair[0].shape
    in_hbm = pl.BlockSpec(memory_space=pltpu.HBM)
    flops = 2 * heads * 2 * count * TB * width
    return pl.pallas_call(
        kernel,
        in_specs=[pl.BlockSpec(memory_space=pltpu.SMEM)] + [pl.BlockSpec(memory_space=pltpu.VMEM) for _ in ins] + [in_hbm, in_hbm],
        out_specs=pl.BlockSpec(memory_space=pltpu.VMEM),
        out_shape=out_shape,
        scratch_shapes=[pltpu.VMEM((heads, 2 * count, width), bf), pltpu.SemaphoreType.DMA((GROUPS, 2))],
        compiler_params=pltpu.CompilerParams(vmem_limit_bytes=58 * 2**20),
        cost_estimate=pl.CostEstimate(flops=flops, bytes_accessed=4 * heads * count * width, transcendentals=0),
        name=name,
    )(first, *ins, *w_pair)


def swap(value, axis, bit):
    count = lax.axis_size(axis)
    return lax.ppermute(value, axis, [(i, i ^ bit) for i in range(count)])


def shifted(value, axis, by):
    count = lax.axis_size(axis)
    pairs = [(i, i + by) for i in range(count) if 0 <= i + by < count]
    return lax.ppermute(value, axis, pairs)


def move(value, along_z, by):
    pairs = []
    for i in range(RINGS * RINGS):
        z, y = i // RINGS, i % RINGS
        to = (z + by) % RINGS * RINGS + y if along_z else z * RINGS + (y + by) % RINGS
        pairs.append((i, to))
    return lax.ppermute(value, "seq", pairs)


def around(x, along_z):
    return [x] + [move(x, along_z, -by) for by in FROM[1:]]


def home(parts, along_z):
    got = [parts[0]] + [move(parts[i], along_z, FROM[i]) for i in range(1, RINGS)]
    return [got[0], got[2], got[1], got[3]]


def float_sum(parts):
    first, *rest = [x.astype(f32) for x in parts]
    return first + rest[0] + rest[1] + rest[2]


def together(*values):
    return lax.optimization_barrier(values)


def scatter_heads(value):
    return lax.all_to_all(value, "seq", split_axis=0, concat_axis=0, tiled=True)


def angle_tables(places):
    quarter = HS // 4
    freqs = jnp.exp(-math.log(10000.0) * jnp.arange(quarter, dtype=f32) / quarter)
    grid_rows = (places // GRID_W).astype(f32)
    grid_cols = (places % GRID_W).astype(f32)
    angles = jnp.concatenate(
        [
            freqs[:, None] * grid_rows[None, :],
            freqs[:, None] * grid_cols[None, :],
            jnp.zeros((HALF - 2 * quarter, places.shape[0]), f32),
        ],
        axis=0,
    )
    return jnp.cos(angles), jnp.sin(angles)


def pad_rows(x, count):
    return jnp.pad(x, ((0, count - x.shape[0]), (0, 0)))


def arrange(w):
    qt = HS // 4
    parts = []
    for part in (w[0], w[1]):
        parts += [pad_rows(jnp.concatenate([part[0:qt], part[2 * qt : 3 * qt]]), HALF)]
        parts += [pad_rows(jnp.concatenate([part[qt : 2 * qt], part[3 * qt :]]), HALF)]
    return jnp.concatenate(parts + [pad_rows(w[2], HP)], axis=0)


def natural_order():
    qt = HS // 4
    order = []
    for at in (0, HP):
        for start in (at, at + HALF, at + qt, at + HALF + qt):
            order += range(start, start + qt)
    return order + list(range(2 * HP, 2 * HP + HS))


def rope(qa, qb, ka, kb, v, c, s):
    return jnp.concatenate([qa * c - qb * s, qa * s + qb * c, ka * c - kb * s, ka * s + kb * c, v], axis=-2).astype(bf)


def modulated_norm(hidden, shift_vec, scale_vec):
    centre = hidden - jnp.mean(hidden, axis=-1, keepdims=True)
    spread = jnp.mean(centre * centre, axis=-1, keepdims=True)
    return centre * lax.rsqrt(spread + norm_eps) * (1.0 + scale_vec) + shift_vec


def norm_back(hidden, scale_vec, grad):
    centre = hidden - jnp.mean(hidden, axis=-1, keepdims=True)
    inv = lax.rsqrt(jnp.mean(centre * centre, axis=-1, keepdims=True) + norm_eps)
    unit = centre * inv
    grad = grad * (1.0 + scale_vec)
    return inv * (grad - jnp.mean(grad, axis=-1, keepdims=True) - unit * jnp.mean(grad * unit, axis=-1, keepdims=True))


def half_rows(rows):
    return -(-rows // 16) * 8


def core_half(value, first):
    rows = value.shape[-2]
    half = half_rows(rows)
    low, high = value[..., :half, :], value[..., rows - half :, :]
    kept, given = jnp.where(first, low, high), jnp.where(first, high, low)
    return (kept.astype(f32) + swap(given, "dp", 1).astype(f32)).astype(bf)


def chip_sum(value):
    return (value.astype(f32) + swap(value, "dp", 2).astype(f32)).astype(bf)


def core_whole(total, other, first, rows):
    low, high = jnp.where(first, total, other), jnp.where(first, other, total)
    return jnp.concatenate([low, high[2 * total.shape[0] - rows :]], axis=0).astype(f32)


def local(streams, modulation, w_qkv, w_out, w_zero, pairing, positions, cotangent):
    on_main = lax.axis_index("section") == 1
    core = lax.axis_index("dp") % 2
    first = core == 0
    mods = modulation[0]
    pair_row = pairing[0]
    width = streams.shape[-1]
    qkv_w = [arrange(w_qkv[0, k, 0]) for k in range(2)]
    out_w = [pad_rows(w_out[0, k, 0], HP) for k in range(2)]

    def own_half(w):
        rows = w.shape[0] // 2
        return lax.dynamic_slice_in_dim(w, core * rows, rows, axis=0)

    def gather(x):
        return lax.all_gather(x, "seq", axis=0, tiled=False)

    def rows_of(w):
        return w.reshape(-1, width)

    def halves_of(x):
        rows = x.shape[1] // 2
        low, high = x[:, :rows], x[:, rows:]
        mine = jnp.where(first, low, high)
        theirs = jnp.where(first, high, low)
        return mine.reshape(-1, x.shape[2]), theirs.reshape(-1, x.shape[2])

    def to_heads(w_pair, x):
        mine, theirs = [nt(rows_of(w), x).reshape(w.shape[:2] + x.shape[:1]) for w in w_pair]
        return jnp.where(first, mine, theirs), jnp.where(first, theirs, mine)

    def from_heads(w_pair, x):
        mine, theirs = halves_of(x)
        return tn(mine, rows_of(w_pair[0])) + tn(theirs, rows_of(w_pair[1]))

    def with_other(x):
        return (x, swap(x, "dp", 1))

    cot = cotangent[0]
    through = nt(cot, w_zero[1])
    grad2 = jnp.where(on_main, cot.astype(f32), jnp.where(pair_row[1] == 1, through, 0.0))
    d_attn1 = (mods[1, 2] * grad2).astype(bf)
    hidden0 = streams[0, 0].astype(f32)
    normed0 = modulated_norm(hidden0, mods[0, 0], mods[0, 1]).astype(bf)
    cells = jnp.stack([positions // GRID_W, positions % GRID_W]).astype(bf)
    message = jnp.concatenate([normed0, jnp.pad(cells.T, ((0, 0), (0, TB - 2)))], axis=1)
    message = jnp.concatenate(around(message, False), axis=0)
    row_tokens = message[:, :width]
    row_cells = message[:, width : width + 2].astype(jnp.int32)
    row_places = row_cells[:, 0] * GRID_W + row_cells[:, 1]
    column_w = with_other(jnp.stack(around(own_half(qkv_w[0]), True)))
    low, high = to_heads(column_w, row_tokens)
    qkv0 = rope(low[:, :HALF], low[:, HALF:HP], low[:, HP:], high[:, :HALF], high[:, HALF:], *angle_tables(row_places))
    pieces = home(qkv0, True)
    at = lax.axis_index("seq")
    at_z, at_y = at // RINGS, at % RINGS
    places = jnp.stack([(at_z + z) % RINGS * RINGS + (at_y + y) % RINGS for z in FROM for y in FROM]).astype(jnp.int32)

    cells = jnp.pad(cells, ((0, 6), (0, width - cells.shape[1])))
    piece_1 = gather(jnp.concatenate([own_half(qkv_w[1]), cells, own_half(out_w[0]), own_half(out_w[1])], axis=0))
    pieces, d_attn1 = together(pieces, d_attn1)
    qkv0, mixed0, log_sums0 = attn_fwd(pieces, places)
    mixed0_own = scatter_heads(mixed0)
    piece_1, mixed0_own = lax.optimization_barrier((piece_1, mixed0_own))
    cut = 3 * HP // 2 + 8
    full_1 = with_other(piece_1)
    cells_all = piece_1[:, 3 * HP // 2 : 3 * HP // 2 + 2, :TB].astype(jnp.int32)
    cos_all, sin_all = angle_tables((cells_all[:, 0] * GRID_W + cells_all[:, 1]).reshape(-1))
    cos_own, sin_own = angle_tables(positions)

    first_flag = jnp.where(first, 1, 0).astype(jnp.int32).reshape(1)
    heads = lax.axis_size("seq")

    def to_mixed(block, d_attn):
        kernel = functools.partial(grad_in_kernel, cut, block * HALF)
        shape = jax.ShapeDtypeStruct((heads, HP, TB), bf)
        return with_weights(kernel, first_flag, (d_attn,), full_1, HP, shape, "to_mixed")

    def from_mixed(block, mixed):
        kernel = functools.partial(sum_kernel, cut, block * HALF)
        shape = jax.ShapeDtypeStruct((TB, width), f32)
        return with_weights(kernel, first_flag, (mixed,), full_1, HP, shape, "from_mixed")

    normed0, mixed0_own = together(normed0, mixed0_own)
    normed0_all = gather(normed0)

    d_mixed1 = scatter_heads(to_mixed(1, d_attn1))
    attn0 = from_mixed(0, mixed0_own)
    hidden1 = hidden0 + mods[0, 2] * attn0
    zero0 = shifted(nn(hidden1.astype(bf), w_zero[0]).astype(bf), "section", 1).astype(f32)
    hidden1 = hidden1 + jnp.where(pair_row[0] == 0, zero0, 0.0)

    normed1 = modulated_norm(hidden1, mods[1, 0], mods[1, 1]).astype(bf)
    shape = jax.ShapeDtypeStruct((heads, 3 * HP, TB), bf)
    ins = (normed1, cos_own, sin_own)
    qkv1 = with_weights(functools.partial(qkv_kernel, 0), first_flag, ins, full_1, cut, shape, "to_qkv")
    qkv1, d_mixed1, second = together(qkv1, d_mixed1, jnp.concatenate([normed1, d_attn1], axis=0))
    qkv1 = scatter_heads(qkv1)
    second_all = gather(second)
    mixed1, d_raw1 = attn_both(qkv1, d_mixed1, cos_all, sin_all)
    order = natural_order()
    plain = list(range(HS))
    d_raw1_own, mixed1_out = together(scatter_heads(d_raw1), mixed1)
    mixed1_own = scatter_heads(mixed1_out)
    shape = jax.ShapeDtypeStruct((TB, width), f32)
    ins = (d_raw1_own,)
    d_normed1 = with_weights(functools.partial(sum_kernel, 0, 0), first_flag, ins, full_1, cut, shape, "from_qkv")
    grad1 = grad2 + norm_back(hidden1, mods[1, 1], d_normed1)

    sent = shifted(grad1.astype(bf), "section", -1)
    sent, mixed1_own = together(sent, mixed1_own)
    picked = jnp.where(pair_row[0] == 0, sent, cot)
    picked = jnp.where(on_main, jnp.zeros_like(picked), picked)
    grad1 = grad1 + nt(picked, w_zero[0])
    d_attn0 = (mods[0, 2] * grad1).astype(bf)
    d_mixed0 = to_mixed(0, d_attn0)
    d_attn0_all = gather(d_attn0)

    mixed1_own, d_mixed0 = together(mixed1_own, d_mixed0)
    attn1 = from_mixed(1, mixed1_own)
    hidden2 = hidden1 + mods[1, 2] * attn1
    zero1 = nn(hidden2.astype(bf), w_zero[1]).astype(bf)
    d_mixed0, zero1 = together(scatter_heads(d_mixed0), zero1)
    zero1 = shifted(zero1, "section", 1)

    d_raw0_rings, d_raw0 = attn_bwd(qkv0, d_mixed0, mixed0, log_sums0, cos_all, sin_all, places)
    d_raw0_rings, d_raw1, mixed1 = together(d_raw0_rings, d_raw1, mixed1)

    homed = home(d_raw0_rings, True)
    grads = [
        weight_grad(order, d_raw0, normed0_all, 0),
        weight_grad(order, d_raw1, second_all, 0),
        weight_grad(plain, mixed1, second_all, 1),
    ]
    homed, grads, zero1 = together(homed, grads, zero1)

    zero1 = zero1.astype(f32)
    hidden2 = hidden2 + jnp.where(pair_row[0] == 1, zero0, 0.0) + jnp.where(pair_row[1] == 1, zero1, 0.0)
    final_out = hidden2.astype(bf)[None, None]

    d_row0 = from_heads(column_w, jnp.stack(homed)).astype(bf).reshape(RINGS, -1, width)
    grads, d_row0 = together(core_half(jnp.concatenate(grads, axis=0), first), d_row0)
    d_row0, grads, mixed0 = together(home(d_row0, False), chip_sum(grads), mixed0)
    grad0 = grad1 + norm_back(hidden0, mods[0, 1], float_sum(d_row0))
    rows = len(order)
    grads = core_whole(grads, swap(grads, "dp", 1), first, 2 * rows + HS)
    out_grad0 = weight_grad(plain, mixed0, d_attn0_all, 0)
    out_grad0 = (out_grad0.astype(f32) + swap(out_grad0, "dp", 1).astype(f32)).astype(bf)
    out_grad0 = chip_sum(out_grad0).astype(f32)
    grad_qkv = grads[: 2 * rows].reshape(1, 2, 1, 3, HS, width)
    grad_out = jnp.stack([out_grad0, grads[2 * rows :]])[None, :, None]
    return (final_out, grad0[None, None], grad_qkv, grad_out)


def solution(mesh):
    in_specs = (
        P("section", "dp", "seq", None),
        P("section", None, None, None),
        P("section", None, "seq", None, None, None),
        P("section", None, "seq", None, None),
        P(),
        P("dp", None),
        P("seq"),
        P("dp", "seq", None),
    )
    out_specs = (
        P("section", "dp", "seq", None),
        P("section", "dp", "seq", None),
        P("section", None, "seq", None, None, None),
        P("section", None, "seq", None, None),
    )
    return jax.shard_map(local, mesh=mesh, in_specs=in_specs, out_specs=out_specs, check_vma=False)
```

```python
import functools
import math

import jax
import jax.numpy as jnp
import numpy as np
from jax import lax
from jax.experimental import pallas as pl
from jax.experimental.pallas import tpu as pltpu
from jax.sharding import PartitionSpec as P

GRID_W = 128
HS = 72
HP = 80
HALF = 40
QB = 1024
TB = 128
RINGS = 4
FROM = (0, -1, 1, 2)
SCALE = 1.0 / math.sqrt(HS)
EXP_SCALE = math.log2(math.e) / math.sqrt(HS)

norm_eps = 1e-06
bf = jnp.bfloat16
f32 = jnp.float32


def nn(a, b):
    return lax.dot_general(a, b, (((1,), (0,)), ((), ())), preferred_element_type=f32)


def nt(a, b):
    return lax.dot_general(a, b, (((1,), (1,)), ((), ())), preferred_element_type=f32)


def tn(a, b):
    return lax.dot_general(a, b, (((0,), (0,)), ((), ())), preferred_element_type=f32)


def flat(ref, to_ref):
    for j in range(ref.shape[0]):
        to_ref[:, j * TB : (j + 1) * TB] = ref[j]


def put(ref, i, value):
    for j in range(QB // TB):
        ref[i * (QB // TB) + j] = value[:, j * TB : (j + 1) * TB]


def by_rings(ref, to_ref, block):
    wide = ref.shape[2] // TB
    for z in range(ref.shape[0]):
        for y in range(wide):
            ref[z, :, y * TB : (y + 1) * TB] = block(to_ref[z * wide + y])


def turn_back(x, c, s):
    a, b = x[:HALF], x[HALF:]
    return jnp.concatenate([a * c + b * s, b * c - a * s], axis=0)


def with_ones(v):
    rows = lax.broadcasted_iota(jnp.int32, v.shape, 0)
    return jnp.where(rows == HS, 1.0, v.astype(f32)).astype(bf)


def whole(x):
    zeros = (0,) * x.ndim
    return pl.BlockSpec(x.shape, lambda i: zeros)


def fwd_kernel(to_ref, p0_ref, p1_ref, p2_ref, p3_ref, x_ref, o_ref, l_ref, kt_ref, vo_ref):
    i = pl.program_id(0)

    @pl.when(i == 0)
    def _():
        for at, piece in enumerate((p0_ref, p1_ref, p2_ref, p3_ref)):
            for j in range(piece.shape[1] // TB):
                place = pl.multiple_of(to_ref[at * (piece.shape[1] // TB) + j] * TB, TB)
                x_ref[:, pl.ds(place, TB)] = piece[:, j * TB : (j + 1) * TB]
        kt_ref[...] = x_ref[HP : 2 * HP].astype(f32).T.astype(bf)
        vo_ref[...] = with_ones(x_ref[2 * HP :])

    s = nn(kt_ref[...], x_ref[:HP, pl.ds(pl.multiple_of(i * QB, QB), QB)])
    m = jnp.max(s, axis=0, keepdims=True)
    e = jnp.exp2((s - m) * EXP_SCALE).astype(bf)
    o = nn(vo_ref[...], e)
    total = o[HS : HS + 1]
    rows = lax.broadcasted_iota(jnp.int32, o.shape, 0)
    put(o_ref, i, jnp.where(rows < HS, o * (1.0 / total), 0.0).astype(bf))
    l_ref[...] = m * EXP_SCALE + jnp.log2(total)


def attn_fwd(pieces, places):
    n = sum(p.shape[1] for p in pieces)
    return pl.pallas_call(
        fwd_kernel,
        grid=(n // QB,),
        in_specs=[pl.BlockSpec(memory_space=pltpu.SMEM)] + [whole(p) for p in pieces],
        out_specs=[
            pl.BlockSpec((3 * HP, n), lambda i: (0, 0)),
            pl.BlockSpec((n // TB, HP, TB), lambda i: (0, 0, 0)),
            pl.BlockSpec((1, QB), lambda i: (0, i)),
        ],
        out_shape=[
            jax.ShapeDtypeStruct((3 * HP, n), bf),
            jax.ShapeDtypeStruct((n // TB, HP, TB), bf),
            jax.ShapeDtypeStruct((1, n), f32),
        ],
        scratch_shapes=[pltpu.VMEM((n, HP), bf), pltpu.VMEM((HP, n), bf)],
        compiler_params=pltpu.CompilerParams(vmem_limit_bytes=40 * 2**20),
        cost_estimate=pl.CostEstimate(flops=4 * n * n * 256, bytes_accessed=2 * 4 * HP * n, transcendentals=n * n),
        name="attn_fwd",
    )(places, *pieces)


def prep(x_ref, kt_ref, vt_ref, dk_ref, dv_ref):
    kt_ref[...] = x_ref[HP : 2 * HP].astype(f32).T.astype(bf)
    vt_ref[...] = x_ref[2 * HP :].astype(f32).T.astype(bf)
    dk_ref[...] = jnp.zeros_like(dk_ref)
    dv_ref[...] = jnp.zeros_like(dv_ref)


def finish(i, dq, c_ref, s_ref, d_ref, dk_ref, dv_ref):
    at = pl.ds(pl.multiple_of(i * QB, QB), QB)
    d_ref[:HP, at] = turn_back(dq * SCALE, c_ref[:, at], s_ref[:, at]).astype(bf)

    @pl.when(i == pl.num_programs(0) - 1)
    def _():
        d_ref[HP : 2 * HP, :] = turn_back(dk_ref[...].T * SCALE, c_ref[...], s_ref[...]).astype(bf)
        d_ref[2 * HP :, :] = dv_ref[...].T.astype(bf)


def bwd_kernel(x_ref, g_ref, o_ref, l_ref, c_ref, s_ref, to_ref, dz_ref, db_ref, kt_ref, vt_ref, dk_ref, dv_ref, gx_ref, ox_ref, d_ref):
    i = pl.program_id(0)

    @pl.when(i == 0)
    def _():
        prep(x_ref, kt_ref, vt_ref, dk_ref, dv_ref)
        flat(g_ref, gx_ref)
        flat(o_ref, ox_ref)

    at = pl.ds(pl.multiple_of(i * QB, QB), QB)
    q = x_ref[:HP, at]
    g = gx_ref[:, at]
    p = jnp.exp2(nn(kt_ref[...], q) * EXP_SCALE - l_ref[...])
    delta = jnp.sum(g.astype(f32) * ox_ref[:, at].astype(f32), axis=0, keepdims=True)
    ds = (p * (nn(vt_ref[...], g) - delta)).astype(bf)
    dv_ref[...] += nt(p.astype(bf), g)
    dk_ref[...] += nt(ds, q)
    finish(i, nn(x_ref[HP : 2 * HP], ds), c_ref, s_ref, d_ref, dk_ref, dv_ref)

    @pl.when(i == pl.num_programs(0) - 1)
    def _():
        for j in range(db_ref.shape[0]):
            db_ref[j] = d_ref[:, j * TB : (j + 1) * TB]
        by_rings(dz_ref, to_ref, lambda block: db_ref[block])


def both_kernel(xb_ref, gb_ref, c_ref, s_ref, o_ref, db_ref, kt_ref, vt_ref, dk_ref, dv_ref, x_ref, g_ref, vo_ref, d_ref):
    i = pl.program_id(0)

    @pl.when(i == 0)
    def _():
        flat(xb_ref, x_ref)
        flat(gb_ref, g_ref)
        prep(x_ref, kt_ref, vt_ref, dk_ref, dv_ref)
        vo_ref[...] = with_ones(x_ref[2 * HP :])

    at = pl.ds(pl.multiple_of(i * QB, QB), QB)
    q = x_ref[:HP, at]
    s = nn(kt_ref[...], q)
    m = jnp.max(s, axis=0, keepdims=True)
    e = jnp.exp2((s - m) * EXP_SCALE)
    eb = e.astype(bf)
    o = nn(vo_ref[...], eb)
    inv = 1.0 / o[HS : HS + 1]
    rows = lax.broadcasted_iota(jnp.int32, o.shape, 0)
    o = jnp.where(rows < HS, o * inv, 0.0)
    put(o_ref, i, o.astype(bf))
    g = g_ref[:, at].astype(f32) * inv
    delta = jnp.sum(g * o, axis=0, keepdims=True)
    g = g.astype(bf)
    ds = (e * (nn(vt_ref[...], g) - delta)).astype(bf)
    dv_ref[...] += nt(eb, g)
    dk_ref[...] += nt(ds, q)
    finish(i, nn(x_ref[HP : 2 * HP], ds), c_ref, s_ref, d_ref, dk_ref, dv_ref)

    @pl.when(i == pl.num_programs(0) - 1)
    def _():
        for j in range(db_ref.shape[0]):
            db_ref[j] = d_ref[:, j * TB : (j + 1) * TB]


def back_call(kernel, ins, in_specs, n, out_shape, extra_scratch, name):
    scratch = [pltpu.VMEM((n, HP), bf), pltpu.VMEM((n, HP), bf), pltpu.VMEM((n, HP), f32), pltpu.VMEM((n, HP), f32)]
    return pl.pallas_call(
        kernel,
        grid=(n // QB,),
        in_specs=in_specs,
        out_specs=[whole(x) for x in out_shape],
        out_shape=out_shape,
        scratch_shapes=scratch + extra_scratch,
        compiler_params=pltpu.CompilerParams(vmem_limit_bytes=48 * 2**20),
        cost_estimate=pl.CostEstimate(flops=10 * n * n * 256, bytes_accessed=2 * 12 * HP * n, transcendentals=n * n),
        name=name,
    )(*ins)


def attn_bwd(x, g, o, l, c, s, places):
    n = x.shape[1]
    specs = [whole(x), whole(g), whole(o), pl.BlockSpec((1, QB), lambda i: (0, i)), whole(c), whole(s)]
    specs += [pl.BlockSpec(memory_space=pltpu.SMEM)]
    extra = [pltpu.VMEM((HP, n), bf), pltpu.VMEM((HP, n), bf), pltpu.VMEM((3 * HP, n), bf)]
    out = [jax.ShapeDtypeStruct((RINGS, 3 * HP, n // RINGS), bf), jax.ShapeDtypeStruct((n // TB, 3 * HP, TB), bf)]
    return back_call(bwd_kernel, (x, g, o, l, c, s, places), specs, n, out, extra, "attn_bwd")


def attn_both(x, g, c, s):
    n = x.shape[0] * TB
    extra = [pltpu.VMEM((3 * HP, n), bf), pltpu.VMEM((HP, n), bf), pltpu.VMEM((HP, n), bf), pltpu.VMEM((3 * HP, n), bf)]
    out = [
        jax.ShapeDtypeStruct((n // TB, HP, TB), bf),
        jax.ShapeDtypeStruct((n // TB, 3 * HP, TB), bf),
    ]
    return back_call(both_kernel, (x, g, c, s), [whole(x), whole(g), whole(c), whole(s)], n, out, extra, "attn_both")


PIECES = 4
STEP = 2


def grad_kernel(p_ref, x_ref, *refs):
    *pieces, out_ref, acc_ref = refs
    i = pl.program_id(0)

    @pl.when(i == 0)
    def _():
        acc_ref[...] = jnp.zeros_like(acc_ref)

    x = jnp.concatenate([x_ref[j] for j in range(x_ref.shape[0])], axis=1)
    x = nn(p_ref[...], x).astype(bf)
    wide = STEP * TB
    total = acc_ref[...]
    for j, piece in enumerate(pieces):
        total = total + nn(x[:, j * wide : (j + 1) * wide], piece[...].reshape(wide, -1))
    acc_ref[...] = total

    @pl.when(i == pl.num_programs(0) - 1)
    def _():
        out_ref[...] = acc_ref[...].astype(bf)


def weight_grad(order, x, gathered, part):
    blocks, _, width = gathered.shape
    pick = np.zeros((len(order), x.shape[1]), np.float32)
    pick[np.arange(len(order)), order] = 1.0
    pick = jnp.asarray(pick, bf)

    def piece(j):
        return pl.BlockSpec((STEP, TB, width), lambda i: (PIECES * i + j, part, 0))

    return pl.pallas_call(
        grad_kernel,
        grid=(blocks // (PIECES * STEP),),
        in_specs=[whole(pick), pl.BlockSpec((PIECES * STEP,) + x.shape[1:], lambda i: (i, 0, 0))]
        + [piece(j) for j in range(PIECES)],
        out_specs=pl.BlockSpec((len(order), width), lambda i: (0, 0)),
        out_shape=jax.ShapeDtypeStruct((len(order), width), bf),
        scratch_shapes=[pltpu.VMEM((len(order), width), f32)],
        compiler_params=pltpu.CompilerParams(vmem_limit_bytes=60 * 2**20),
        cost_estimate=pl.CostEstimate(flops=1, bytes_accessed=1, transcendentals=0),
        name="weight_grad",
    )(pick, x, *([gathered] * PIECES))


GROUPS = 4


def fetch(mine_ref, theirs_ref, buf_ref, sems, at):
    heads = buf_ref.shape[0] // GROUPS
    count = buf_ref.shape[1] // 2
    copies = []
    for g in range(GROUPS):
        for k, ref in enumerate((mine_ref, theirs_ref)):
            copies.append(
                pltpu.make_async_copy(
                    ref.at[pl.ds(g * heads, heads), pl.ds(at, count), :],
                    buf_ref.at[pl.ds(g * heads, heads), pl.ds(k * count, count), :],
                    sems.at[g, k],
                )
            )
    for copy in copies:
        copy.start()
    return copies


def group_rows(buf_ref, g):
    heads = buf_ref.shape[0] // GROUPS
    return buf_ref[g * heads : (g + 1) * heads].reshape(heads * buf_ref.shape[1], buf_ref.shape[2])


def qkv_kernel(at, first_ref, x_ref, c_ref, s_ref, mine_ref, theirs_ref, out_ref, buf_ref, sems):
    copies = fetch(mine_ref, theirs_ref, buf_ref, sems, at)
    x, c, s = x_ref[...], c_ref[...], s_ref[...]
    first = first_ref[0] == 1
    count = buf_ref.shape[1] // 2
    heads = buf_ref.shape[0] // GROUPS
    for g in range(GROUPS):
        copies[2 * g].wait()
        copies[2 * g + 1].wait()
        products = nt(group_rows(buf_ref, g), x)
        for h in range(g * heads, (g + 1) * heads):
            raw = products[2 * count * (h - g * heads) : 2 * count * (h - g * heads + 1)]
            low = jnp.where(first, raw[:count], raw[count:])
            high = jnp.where(first, raw[count:], raw[:count])
            qa, qb, ka = low[:HALF], low[HALF:HP], low[HP : HP + HALF]
            kb, v = high[:HALF], high[HALF : HALF + HP]
            parts = [qa * c - qb * s, qa * s + qb * c, ka * c - kb * s, ka * s + kb * c, v]
            out_ref[h] = jnp.concatenate(parts, axis=0).astype(bf)


def grad_in_kernel(at, sub, first_ref, x_ref, mine_ref, theirs_ref, out_ref, buf_ref, sems):
    copies = fetch(mine_ref, theirs_ref, buf_ref, sems, at)
    x = x_ref[...]
    first = first_ref[0] == 1
    count = buf_ref.shape[1] // 2
    heads = buf_ref.shape[0] // GROUPS
    for g in range(GROUPS):
        copies[2 * g].wait()
        copies[2 * g + 1].wait()
        products = nt(group_rows(buf_ref, g), x)
        for h in range(g * heads, (g + 1) * heads):
            raw = products[2 * count * (h - g * heads) : 2 * count * (h - g * heads + 1)]
            mine, theirs = raw[sub : sub + HALF], raw[count + sub : count + sub + HALF]
            parts = [jnp.where(first, mine, theirs), jnp.where(first, theirs, mine)]
            out_ref[h] = jnp.concatenate(parts, axis=0).astype(bf)


def sum_kernel(at, sub, first_ref, x_ref, mine_ref, theirs_ref, out_ref, buf_ref, sems):
    copies = fetch(mine_ref, theirs_ref, buf_ref, sems, at)
    first = first_ref[0] == 1
    count = buf_ref.shape[1] // 2
    heads = buf_ref.shape[0] // GROUPS
    rows = x_ref.shape[1] // 2
    total = jnp.zeros(out_ref.shape, f32)

    def in_place(x):
        parts = [jnp.zeros((sub, x.shape[1]), f32)] if sub else []
        parts.append(x)
        if sub + rows < count:
            parts.append(jnp.zeros((count - sub - rows, x.shape[1]), f32))
        return parts

    for g in range(GROUPS):
        copies[2 * g].wait()
        copies[2 * g + 1].wait()
        parts = []
        for h in range(g * heads, (g + 1) * heads):
            x = x_ref[h].astype(f32)
            low, high = x[:rows], x[rows:]
            parts += in_place(jnp.where(first, low, high)) + in_place(jnp.where(first, high, low))
        total = total + tn(jnp.concatenate(parts, axis=0).astype(bf), group_rows(buf_ref, g))
    out_ref[...] = total


def with_weights(kernel, first, ins, w_pair, count, out_shape, name):
    heads, _, width = w_pair[0].shape
    in_hbm = pl.BlockSpec(memory_space=pltpu.HBM)
    flops = 2 * heads * 2 * count * TB * width
    return pl.pallas_call(
        kernel,
        in_specs=[pl.BlockSpec(memory_space=pltpu.SMEM)] + [pl.BlockSpec(memory_space=pltpu.VMEM) for _ in ins] + [in_hbm, in_hbm],
        out_specs=pl.BlockSpec(memory_space=pltpu.VMEM),
        out_shape=out_shape,
        scratch_shapes=[pltpu.VMEM((heads, 2 * count, width), bf), pltpu.SemaphoreType.DMA((GROUPS, 2))],
        compiler_params=pltpu.CompilerParams(vmem_limit_bytes=58 * 2**20),
        cost_estimate=pl.CostEstimate(flops=flops, bytes_accessed=4 * heads * count * width, transcendentals=0),
        name=name,
    )(first, *ins, *w_pair)


def swap(value, axis, bit):
    count = lax.axis_size(axis)
    return lax.ppermute(value, axis, [(i, i ^ bit) for i in range(count)])


def shifted(value, axis, by):
    count = lax.axis_size(axis)
    pairs = [(i, i + by) for i in range(count) if 0 <= i + by < count]
    return lax.ppermute(value, axis, pairs)


def move(value, along_z, by):
    pairs = []
    for i in range(RINGS * RINGS):
        z, y = i // RINGS, i % RINGS
        to = (z + by) % RINGS * RINGS + y if along_z else z * RINGS + (y + by) % RINGS
        pairs.append((i, to))
    return lax.ppermute(value, "seq", pairs)


def around(x, along_z):
    return [x] + [move(x, along_z, -by) for by in FROM[1:]]


def home(parts, along_z):
    got = [parts[0]] + [move(parts[i], along_z, FROM[i]) for i in range(1, RINGS)]
    return [got[0], got[2], got[1], got[3]]


def float_sum(parts):
    first, *rest = [x.astype(f32) for x in parts]
    return first + rest[0] + rest[1] + rest[2]


def together(*values):
    return lax.optimization_barrier(values)


def scatter_heads(value):
    return lax.all_to_all(value, "seq", split_axis=0, concat_axis=0, tiled=True)


def angle_tables(places):
    quarter = HS // 4
    freqs = jnp.exp(-math.log(10000.0) * jnp.arange(quarter, dtype=f32) / quarter)
    grid_rows = (places // GRID_W).astype(f32)
    grid_cols = (places % GRID_W).astype(f32)
    angles = jnp.concatenate(
        [
            freqs[:, None] * grid_rows[None, :],
            freqs[:, None] * grid_cols[None, :],
            jnp.zeros((HALF - 2 * quarter, places.shape[0]), f32),
        ],
        axis=0,
    )
    return jnp.cos(angles), jnp.sin(angles)


def pad_rows(x, count):
    return jnp.pad(x, ((0, count - x.shape[0]), (0, 0)))


def arrange(w):
    qt = HS // 4
    parts = []
    for part in (w[0], w[1]):
        parts += [pad_rows(jnp.concatenate([part[0:qt], part[2 * qt : 3 * qt]]), HALF)]
        parts += [pad_rows(jnp.concatenate([part[qt : 2 * qt], part[3 * qt :]]), HALF)]
    return jnp.concatenate(parts + [pad_rows(w[2], HP)], axis=0)


def natural_order():
    qt = HS // 4
    order = []
    for at in (0, HP):
        for start in (at, at + HALF, at + qt, at + HALF + qt):
            order += range(start, start + qt)
    return order + list(range(2 * HP, 2 * HP + HS))


def rope(qa, qb, ka, kb, v, c, s):
    return jnp.concatenate([qa * c - qb * s, qa * s + qb * c, ka * c - kb * s, ka * s + kb * c, v], axis=-2).astype(bf)


def modulated_norm(hidden, shift_vec, scale_vec):
    centre = hidden - jnp.mean(hidden, axis=-1, keepdims=True)
    spread = jnp.mean(centre * centre, axis=-1, keepdims=True)
    return centre * lax.rsqrt(spread + norm_eps) * (1.0 + scale_vec) + shift_vec


def norm_back(hidden, scale_vec, grad):
    centre = hidden - jnp.mean(hidden, axis=-1, keepdims=True)
    inv = lax.rsqrt(jnp.mean(centre * centre, axis=-1, keepdims=True) + norm_eps)
    unit = centre * inv
    grad = grad * (1.0 + scale_vec)
    return inv * (grad - jnp.mean(grad, axis=-1, keepdims=True) - unit * jnp.mean(grad * unit, axis=-1, keepdims=True))


def half_rows(rows):
    return -(-rows // 16) * 8


def core_half(value, first):
    rows = value.shape[-2]
    half = half_rows(rows)
    low, high = value[..., :half, :], value[..., rows - half :, :]
    kept, given = jnp.where(first, low, high), jnp.where(first, high, low)
    return (kept.astype(f32) + swap(given, "dp", 1).astype(f32)).astype(bf)


def chip_sum(value):
    return (value.astype(f32) + swap(value, "dp", 2).astype(f32)).astype(bf)


def core_whole(total, other, first, rows):
    low, high = jnp.where(first, total, other), jnp.where(first, other, total)
    return jnp.concatenate([low, high[2 * total.shape[0] - rows :]], axis=0).astype(f32)


def local(streams, modulation, w_qkv, w_out, w_zero, pairing, positions, cotangent):
    on_main = lax.axis_index("section") == 1
    core = lax.axis_index("dp") % 2
    first = core == 0
    mods = modulation[0]
    pair_row = pairing[0]
    width = streams.shape[-1]
    qkv_w = [arrange(w_qkv[0, k, 0]) for k in range(2)]
    out_w = [pad_rows(w_out[0, k, 0], HP) for k in range(2)]

    def own_half(w):
        rows = w.shape[0] // 2
        return lax.dynamic_slice_in_dim(w, core * rows, rows, axis=0)

    def gather(x):
        return lax.all_gather(x, "seq", axis=0, tiled=False)

    def rows_of(w):
        return w.reshape(-1, width)

    def halves_of(x):
        rows = x.shape[1] // 2
        low, high = x[:, :rows], x[:, rows:]
        mine = jnp.where(first, low, high)
        theirs = jnp.where(first, high, low)
        return mine.reshape(-1, x.shape[2]), theirs.reshape(-1, x.shape[2])

    def to_heads(w_pair, x):
        mine, theirs = [nt(rows_of(w), x).reshape(w.shape[:2] + x.shape[:1]) for w in w_pair]
        return jnp.where(first, mine, theirs), jnp.where(first, theirs, mine)

    def from_heads(w_pair, x):
        mine, theirs = halves_of(x)
        return tn(mine, rows_of(w_pair[0])) + tn(theirs, rows_of(w_pair[1]))

    def with_other(x):
        return (x, swap(x, "dp", 1))

    cot = cotangent[0]
    through = nt(cot, w_zero[1])
    grad2 = jnp.where(on_main, cot.astype(f32), jnp.where(pair_row[1] == 1, through, 0.0))
    d_attn1 = (mods[1, 2] * grad2).astype(bf)
    hidden0 = streams[0, 0].astype(f32)
    normed0 = modulated_norm(hidden0, mods[0, 0], mods[0, 1]).astype(bf)
    cells = jnp.stack([positions // GRID_W, positions % GRID_W]).astype(bf)
    message = jnp.concatenate([normed0, jnp.pad(cells.T, ((0, 0), (0, TB - 2)))], axis=1)
    message = jnp.concatenate(around(message, False), axis=0)
    row_tokens = message[:, :width]
    row_cells = message[:, width : width + 2].astype(jnp.int32)
    row_places = row_cells[:, 0] * GRID_W + row_cells[:, 1]
    column_w = with_other(jnp.stack(around(own_half(qkv_w[0]), True)))
    low, high = to_heads(column_w, row_tokens)
    qkv0 = rope(low[:, :HALF], low[:, HALF:HP], low[:, HP:], high[:, :HALF], high[:, HALF:], *angle_tables(row_places))
    pieces = home(qkv0, True)
    at = lax.axis_index("seq")
    at_z, at_y = at // RINGS, at % RINGS
    places = jnp.stack([(at_z + z) % RINGS * RINGS + (at_y + y) % RINGS for z in FROM for y in FROM]).astype(jnp.int32)

    cells = jnp.pad(cells, ((0, 6), (0, width - cells.shape[1])))
    piece_1 = gather(jnp.concatenate([own_half(qkv_w[1]), cells, own_half(out_w[0]), own_half(out_w[1])], axis=0))
    pieces, d_attn1 = together(pieces, d_attn1)
    qkv0, mixed0, log_sums0 = attn_fwd(pieces, places)
    mixed0_own = scatter_heads(mixed0)
    piece_1, mixed0_own = lax.optimization_barrier((piece_1, mixed0_own))
    cut = 3 * HP // 2 + 8
    full_1 = with_other(piece_1)
    cells_all = piece_1[:, 3 * HP // 2 : 3 * HP // 2 + 2, :TB].astype(jnp.int32)
    cos_all, sin_all = angle_tables((cells_all[:, 0] * GRID_W + cells_all[:, 1]).reshape(-1))
    cos_own, sin_own = angle_tables(positions)

    first_flag = jnp.where(first, 1, 0).astype(jnp.int32).reshape(1)
    heads = lax.axis_size("seq")

    def to_mixed(block, d_attn):
        kernel = functools.partial(grad_in_kernel, cut, block * HALF)
        shape = jax.ShapeDtypeStruct((heads, HP, TB), bf)
        return with_weights(kernel, first_flag, (d_attn,), full_1, HP, shape, "to_mixed")

    def from_mixed(block, mixed):
        kernel = functools.partial(sum_kernel, cut, block * HALF)
        shape = jax.ShapeDtypeStruct((TB, width), f32)
        return with_weights(kernel, first_flag, (mixed,), full_1, HP, shape, "from_mixed")

    normed0, mixed0_own = together(normed0, mixed0_own)
    normed0_all = gather(normed0)

    d_mixed1 = scatter_heads(to_mixed(1, d_attn1))
    attn0 = from_mixed(0, mixed0_own)
    hidden1 = hidden0 + mods[0, 2] * attn0
    zero0 = shifted(nn(hidden1.astype(bf), w_zero[0]).astype(bf), "section", 1).astype(f32)
    hidden1 = hidden1 + jnp.where(pair_row[0] == 0, zero0, 0.0)

    normed1 = modulated_norm(hidden1, mods[1, 0], mods[1, 1]).astype(bf)
    shape = jax.ShapeDtypeStruct((heads, 3 * HP, TB), bf)
    ins = (normed1, cos_own, sin_own)
    qkv1 = with_weights(functools.partial(qkv_kernel, 0), first_flag, ins, full_1, cut, shape, "to_qkv")
    qkv1, d_mixed1, second = together(qkv1, d_mixed1, jnp.concatenate([normed1, d_attn1], axis=0))
    qkv1 = scatter_heads(qkv1)
    second_all = gather(second)
    mixed1, d_raw1 = attn_both(qkv1, d_mixed1, cos_all, sin_all)
    order = natural_order()
    plain = list(range(HS))
    d_raw1_own, mixed1_out = together(scatter_heads(d_raw1), mixed1)
    mixed1_own = scatter_heads(mixed1_out)
    shape = jax.ShapeDtypeStruct((TB, width), f32)
    ins = (d_raw1_own,)
    d_normed1 = with_weights(functools.partial(sum_kernel, 0, 0), first_flag, ins, full_1, cut, shape, "from_qkv")
    grad1 = grad2 + norm_back(hidden1, mods[1, 1], d_normed1)

    sent = shifted(grad1.astype(bf), "section", -1)
    sent, mixed1_own = together(sent, mixed1_own)
    picked = jnp.where(pair_row[0] == 0, sent, cot)
    picked = jnp.where(on_main, jnp.zeros_like(picked), picked)
    grad1 = grad1 + nt(picked, w_zero[0])
    d_attn0 = (mods[0, 2] * grad1).astype(bf)
    d_mixed0 = to_mixed(0, d_attn0)
    d_attn0_all = gather(d_attn0)

    mixed1_own, d_mixed0 = together(mixed1_own, d_mixed0)
    attn1 = from_mixed(1, mixed1_own)
    hidden2 = hidden1 + mods[1, 2] * attn1
    zero1 = nn(hidden2.astype(bf), w_zero[1]).astype(bf)
    d_mixed0, zero1 = together(scatter_heads(d_mixed0), zero1)
    zero1 = shifted(zero1, "section", 1)

    d_raw0_rings, d_raw0 = attn_bwd(qkv0, d_mixed0, mixed0, log_sums0, cos_all, sin_all, places)
    d_raw0_rings, d_raw1, mixed1 = together(d_raw0_rings, d_raw1, mixed1)

    homed = home(d_raw0_rings, True)
    grads = [
        weight_grad(order, d_raw0, normed0_all, 0),
        weight_grad(order, d_raw1, second_all, 0),
        weight_grad(plain, mixed1, second_all, 1),
    ]
    homed, grads, zero1 = together(homed, grads, zero1)

    zero1 = zero1.astype(f32)
    hidden2 = hidden2 + jnp.where(pair_row[0] == 1, zero0, 0.0) + jnp.where(pair_row[1] == 1, zero1, 0.0)
    final_out = hidden2.astype(bf)[None, None]

    d_row0 = from_heads(column_w, jnp.stack(homed)).astype(bf).reshape(RINGS, -1, width)
    grads, d_row0 = together(core_half(jnp.concatenate(grads, axis=0), first), d_row0)
    d_row0, grads, mixed0 = together(home(d_row0, False), chip_sum(grads), mixed0)
    grad0 = grad1 + norm_back(hidden0, mods[0, 1], float_sum(d_row0))
    rows = len(order)
    grads = core_whole(grads, swap(grads, "dp", 1), first, 2 * rows + HS)
    out_grad0 = weight_grad(plain, mixed0, d_attn0_all, 0)
    out_grad0 = (out_grad0.astype(f32) + swap(out_grad0, "dp", 1).astype(f32)).astype(bf)
    out_grad0 = chip_sum(out_grad0).astype(f32)
    grad_qkv = grads[: 2 * rows].reshape(1, 2, 1, 3, HS, width)
    grad_out = jnp.stack([out_grad0, grads[2 * rows :]])[None, :, None]
    return (final_out, grad0[None, None], grad_qkv, grad_out)


def solution(mesh):
    in_specs = (
        P("section", "dp", "seq", None),
        P("section", None, None, None),
        P("section", None, "seq", None, None, None),
        P("section", None, "seq", None, None),
        P(),
        P("dp", None),
        P("seq"),
        P("dp", "seq", None),
    )
    out_specs = (
        P("section", "dp", "seq", None),
        P("section", "dp", "seq", None),
        P("section", None, "seq", None, None, None),
        P("section", None, "seq", None, None),
    )
    return jax.shard_map(local, mesh=mesh, in_specs=in_specs, out_specs=out_specs, check_vma=False)
```

```python
import functools
import math

import jax
import jax.numpy as jnp
import numpy as np
from jax import lax
from jax.experimental import pallas as pl
from jax.experimental.pallas import tpu as pltpu
from jax.sharding import PartitionSpec as P

GRID_W = 128
HS = 72
HP = 80
HALF = 40
QB = 1024
TB = 128
RINGS = 4
FROM = (0, -1, 1, 2)
SCALE = 1.0 / math.sqrt(HS)
EXP_SCALE = math.log2(math.e) / math.sqrt(HS)

norm_eps = 1e-06
bf = jnp.bfloat16
f32 = jnp.float32


def nn(a, b):
    return lax.dot_general(a, b, (((1,), (0,)), ((), ())), preferred_element_type=f32)


def nt(a, b):
    return lax.dot_general(a, b, (((1,), (1,)), ((), ())), preferred_element_type=f32)


def tn(a, b):
    return lax.dot_general(a, b, (((0,), (0,)), ((), ())), preferred_element_type=f32)


def flat(ref, to_ref):
    for j in range(ref.shape[0]):
        to_ref[:, j * TB : (j + 1) * TB] = ref[j]


def put(ref, i, value):
    for j in range(QB // TB):
        ref[i * (QB // TB) + j] = value[:, j * TB : (j + 1) * TB]


def by_rings(ref, to_ref, block):
    wide = ref.shape[2] // TB
    for z in range(ref.shape[0]):
        for y in range(wide):
            ref[z, :, y * TB : (y + 1) * TB] = block(to_ref[z * wide + y])


def turn_back(x, c, s):
    a, b = x[:HALF], x[HALF:]
    return jnp.concatenate([a * c + b * s, b * c - a * s], axis=0)


def with_ones(v):
    rows = lax.broadcasted_iota(jnp.int32, v.shape, 0)
    return jnp.where(rows == HS, 1.0, v.astype(f32)).astype(bf)


def whole(x):
    zeros = (0,) * x.ndim
    return pl.BlockSpec(x.shape, lambda i: zeros)


def fwd_kernel(to_ref, p0_ref, p1_ref, p2_ref, p3_ref, x_ref, o_ref, l_ref, kt_ref, vo_ref):
    i = pl.program_id(0)

    @pl.when(i == 0)
    def _():
        for at, piece in enumerate((p0_ref, p1_ref, p2_ref, p3_ref)):
            for j in range(piece.shape[1] // TB):
                place = pl.multiple_of(to_ref[at * (piece.shape[1] // TB) + j] * TB, TB)
                x_ref[:, pl.ds(place, TB)] = piece[:, j * TB : (j + 1) * TB]
        kt_ref[...] = x_ref[HP : 2 * HP].astype(f32).T.astype(bf)
        vo_ref[...] = with_ones(x_ref[2 * HP :])

    s = nn(kt_ref[...], x_ref[:HP, pl.ds(pl.multiple_of(i * QB, QB), QB)])
    m = jnp.max(s, axis=0, keepdims=True)
    e = jnp.exp2((s - m) * EXP_SCALE).astype(bf)
    o = nn(vo_ref[...], e)
    total = o[HS : HS + 1]
    rows = lax.broadcasted_iota(jnp.int32, o.shape, 0)
    put(o_ref, i, jnp.where(rows < HS, o * (1.0 / total), 0.0).astype(bf))
    l_ref[...] = m * EXP_SCALE + jnp.log2(total)


def attn_fwd(pieces, places):
    n = sum(p.shape[1] for p in pieces)
    return pl.pallas_call(
        fwd_kernel,
        grid=(n // QB,),
        in_specs=[pl.BlockSpec(memory_space=pltpu.SMEM)] + [whole(p) for p in pieces],
        out_specs=[
            pl.BlockSpec((3 * HP, n), lambda i: (0, 0)),
            pl.BlockSpec((n // TB, HP, TB), lambda i: (0, 0, 0)),
            pl.BlockSpec((1, QB), lambda i: (0, i)),
        ],
        out_shape=[
            jax.ShapeDtypeStruct((3 * HP, n), bf),
            jax.ShapeDtypeStruct((n // TB, HP, TB), bf),
            jax.ShapeDtypeStruct((1, n), f32),
        ],
        scratch_shapes=[pltpu.VMEM((n, HP), bf), pltpu.VMEM((HP, n), bf)],
        compiler_params=pltpu.CompilerParams(vmem_limit_bytes=40 * 2**20),
        cost_estimate=pl.CostEstimate(flops=4 * n * n * 256, bytes_accessed=2 * 4 * HP * n, transcendentals=n * n),
        name="attn_fwd",
    )(places, *pieces)


def prep(x_ref, kt_ref, vt_ref, dk_ref, dv_ref):
    kt_ref[...] = x_ref[HP : 2 * HP].astype(f32).T.astype(bf)
    vt_ref[...] = x_ref[2 * HP :].astype(f32).T.astype(bf)
    dk_ref[...] = jnp.zeros_like(dk_ref)
    dv_ref[...] = jnp.zeros_like(dv_ref)


def finish(i, dq, c_ref, s_ref, d_ref, dk_ref, dv_ref):
    at = pl.ds(pl.multiple_of(i * QB, QB), QB)
    d_ref[:HP, at] = turn_back(dq * SCALE, c_ref[:, at], s_ref[:, at]).astype(bf)

    @pl.when(i == pl.num_programs(0) - 1)
    def _():
        d_ref[HP : 2 * HP, :] = turn_back(dk_ref[...].T * SCALE, c_ref[...], s_ref[...]).astype(bf)
        d_ref[2 * HP :, :] = dv_ref[...].T.astype(bf)


def bwd_kernel(x_ref, g_ref, o_ref, l_ref, c_ref, s_ref, to_ref, dz_ref, db_ref, kt_ref, vt_ref, dk_ref, dv_ref, gx_ref, ox_ref, d_ref):
    i = pl.program_id(0)

    @pl.when(i == 0)
    def _():
        prep(x_ref, kt_ref, vt_ref, dk_ref, dv_ref)
        flat(g_ref, gx_ref)
        flat(o_ref, ox_ref)

    at = pl.ds(pl.multiple_of(i * QB, QB), QB)
    q = x_ref[:HP, at]
    g = gx_ref[:, at]
    p = jnp.exp2(nn(kt_ref[...], q) * EXP_SCALE - l_ref[...])
    delta = jnp.sum(g.astype(f32) * ox_ref[:, at].astype(f32), axis=0, keepdims=True)
    ds = (p * (nn(vt_ref[...], g) - delta)).astype(bf)
    dv_ref[...] += nt(p.astype(bf), g)
    dk_ref[...] += nt(ds, q)
    finish(i, nn(x_ref[HP : 2 * HP], ds), c_ref, s_ref, d_ref, dk_ref, dv_ref)

    @pl.when(i == pl.num_programs(0) - 1)
    def _():
        for j in range(db_ref.shape[0]):
            db_ref[j] = d_ref[:, j * TB : (j + 1) * TB]
        by_rings(dz_ref, to_ref, lambda block: db_ref[block])


def both_kernel(xb_ref, gb_ref, c_ref, s_ref, o_ref, db_ref, kt_ref, vt_ref, dk_ref, dv_ref, x_ref, g_ref, vo_ref, d_ref):
    i = pl.program_id(0)

    @pl.when(i == 0)
    def _():
        flat(xb_ref, x_ref)
        flat(gb_ref, g_ref)
        prep(x_ref, kt_ref, vt_ref, dk_ref, dv_ref)
        vo_ref[...] = with_ones(x_ref[2 * HP :])

    at = pl.ds(pl.multiple_of(i * QB, QB), QB)
    q = x_ref[:HP, at]
    s = nn(kt_ref[...], q)
    m = jnp.max(s, axis=0, keepdims=True)
    e = jnp.exp2((s - m) * EXP_SCALE)
    eb = e.astype(bf)
    o = nn(vo_ref[...], eb)
    inv = 1.0 / o[HS : HS + 1]
    rows = lax.broadcasted_iota(jnp.int32, o.shape, 0)
    o = jnp.where(rows < HS, o * inv, 0.0)
    put(o_ref, i, o.astype(bf))
    g = g_ref[:, at].astype(f32) * inv
    delta = jnp.sum(g * o, axis=0, keepdims=True)
    g = g.astype(bf)
    ds = (e * (nn(vt_ref[...], g) - delta)).astype(bf)
    dv_ref[...] += nt(eb, g)
    dk_ref[...] += nt(ds, q)
    finish(i, nn(x_ref[HP : 2 * HP], ds), c_ref, s_ref, d_ref, dk_ref, dv_ref)

    @pl.when(i == pl.num_programs(0) - 1)
    def _():
        for j in range(db_ref.shape[0]):
            db_ref[j] = d_ref[:, j * TB : (j + 1) * TB]


def back_call(kernel, ins, in_specs, n, out_shape, extra_scratch, name):
    scratch = [pltpu.VMEM((n, HP), bf), pltpu.VMEM((n, HP), bf), pltpu.VMEM((n, HP), f32), pltpu.VMEM((n, HP), f32)]
    return pl.pallas_call(
        kernel,
        grid=(n // QB,),
        in_specs=in_specs,
        out_specs=[whole(x) for x in out_shape],
        out_shape=out_shape,
        scratch_shapes=scratch + extra_scratch,
        compiler_params=pltpu.CompilerParams(vmem_limit_bytes=48 * 2**20),
        cost_estimate=pl.CostEstimate(flops=10 * n * n * 256, bytes_accessed=2 * 12 * HP * n, transcendentals=n * n),
        name=name,
    )(*ins)


def attn_bwd(x, g, o, l, c, s, places):
    n = x.shape[1]
    specs = [whole(x), whole(g), whole(o), pl.BlockSpec((1, QB), lambda i: (0, i)), whole(c), whole(s)]
    specs += [pl.BlockSpec(memory_space=pltpu.SMEM)]
    extra = [pltpu.VMEM((HP, n), bf), pltpu.VMEM((HP, n), bf), pltpu.VMEM((3 * HP, n), bf)]
    out = [jax.ShapeDtypeStruct((RINGS, 3 * HP, n // RINGS), bf), jax.ShapeDtypeStruct((n // TB, 3 * HP, TB), bf)]
    return back_call(bwd_kernel, (x, g, o, l, c, s, places), specs, n, out, extra, "attn_bwd")


def attn_both(x, g, c, s):
    n = x.shape[0] * TB
    extra = [pltpu.VMEM((3 * HP, n), bf), pltpu.VMEM((HP, n), bf), pltpu.VMEM((HP, n), bf), pltpu.VMEM((3 * HP, n), bf)]
    out = [
        jax.ShapeDtypeStruct((n // TB, HP, TB), bf),
        jax.ShapeDtypeStruct((n // TB, 3 * HP, TB), bf),
    ]
    return back_call(both_kernel, (x, g, c, s), [whole(x), whole(g), whole(c), whole(s)], n, out, extra, "attn_both")


PIECES = 4
STEP = 2


def grad_kernel(p_ref, x_ref, *refs):
    *pieces, out_ref, acc_ref = refs
    i = pl.program_id(0)

    @pl.when(i == 0)
    def _():
        acc_ref[...] = jnp.zeros_like(acc_ref)

    x = jnp.concatenate([x_ref[j] for j in range(x_ref.shape[0])], axis=1)
    x = nn(p_ref[...], x).astype(bf)
    wide = STEP * TB
    total = acc_ref[...]
    for j, piece in enumerate(pieces):
        total = total + nn(x[:, j * wide : (j + 1) * wide], piece[...].reshape(wide, -1))
    acc_ref[...] = total

    @pl.when(i == pl.num_programs(0) - 1)
    def _():
        out_ref[...] = acc_ref[...].astype(bf)


def weight_grad(order, x, gathered, part):
    blocks, _, width = gathered.shape
    pick = np.zeros((len(order), x.shape[1]), np.float32)
    pick[np.arange(len(order)), order] = 1.0
    pick = jnp.asarray(pick, bf)

    def piece(j):
        return pl.BlockSpec((STEP, TB, width), lambda i: (PIECES * i + j, part, 0))

    return pl.pallas_call(
        grad_kernel,
        grid=(blocks // (PIECES * STEP),),
        in_specs=[whole(pick), pl.BlockSpec((PIECES * STEP,) + x.shape[1:], lambda i: (i, 0, 0))]
        + [piece(j) for j in range(PIECES)],
        out_specs=pl.BlockSpec((len(order), width), lambda i: (0, 0)),
        out_shape=jax.ShapeDtypeStruct((len(order), width), bf),
        scratch_shapes=[pltpu.VMEM((len(order), width), f32)],
        compiler_params=pltpu.CompilerParams(vmem_limit_bytes=60 * 2**20),
        cost_estimate=pl.CostEstimate(flops=1, bytes_accessed=1, transcendentals=0),
        name="weight_grad",
    )(pick, x, *([gathered] * PIECES))


GROUPS = 4


def fetch(mine_ref, theirs_ref, buf_ref, sems, at):
    heads = buf_ref.shape[0] // GROUPS
    count = buf_ref.shape[1] // 2
    copies = []
    for g in range(GROUPS):
        for k, ref in enumerate((mine_ref, theirs_ref)):
            copies.append(
                pltpu.make_async_copy(
                    ref.at[pl.ds(g * heads, heads), pl.ds(at, count), :],
                    buf_ref.at[pl.ds(g * heads, heads), pl.ds(k * count, count), :],
                    sems.at[g, k],
                )
            )
    for copy in copies:
        copy.start()
    return copies


def group_rows(buf_ref, g):
    heads = buf_ref.shape[0] // GROUPS
    return buf_ref[g * heads : (g + 1) * heads].reshape(heads * buf_ref.shape[1], buf_ref.shape[2])


def qkv_kernel(at, first_ref, x_ref, c_ref, s_ref, mine_ref, theirs_ref, out_ref, buf_ref, sems):
    copies = fetch(mine_ref, theirs_ref, buf_ref, sems, at)
    x, c, s = x_ref[...], c_ref[...], s_ref[...]
    first = first_ref[0] == 1
    count = buf_ref.shape[1] // 2
    heads = buf_ref.shape[0] // GROUPS
    for g in range(GROUPS):
        copies[2 * g].wait()
        copies[2 * g + 1].wait()
        products = nt(group_rows(buf_ref, g), x)
        for h in range(g * heads, (g + 1) * heads):
            raw = products[2 * count * (h - g * heads) : 2 * count * (h - g * heads + 1)]
            low = jnp.where(first, raw[:count], raw[count:])
            high = jnp.where(first, raw[count:], raw[:count])
            qa, qb, ka = low[:HALF], low[HALF:HP], low[HP : HP + HALF]
            kb, v = high[:HALF], high[HALF : HALF + HP]
            parts = [qa * c - qb * s, qa * s + qb * c, ka * c - kb * s, ka * s + kb * c, v]
            out_ref[h] = jnp.concatenate(parts, axis=0).astype(bf)


def grad_in_kernel(at, sub, first_ref, x_ref, mine_ref, theirs_ref, out_ref, buf_ref, sems):
    copies = fetch(mine_ref, theirs_ref, buf_ref, sems, at)
    x = x_ref[...]
    first = first_ref[0] == 1
    count = buf_ref.shape[1] // 2
    heads = buf_ref.shape[0] // GROUPS
    for g in range(GROUPS):
        copies[2 * g].wait()
        copies[2 * g + 1].wait()
        products = nt(group_rows(buf_ref, g), x)
        for h in range(g * heads, (g + 1) * heads):
            raw = products[2 * count * (h - g * heads) : 2 * count * (h - g * heads + 1)]
            mine, theirs = raw[sub : sub + HALF], raw[count + sub : count + sub + HALF]
            parts = [jnp.where(first, mine, theirs), jnp.where(first, theirs, mine)]
            out_ref[h] = jnp.concatenate(parts, axis=0).astype(bf)


def sum_kernel(at, sub, first_ref, x_ref, mine_ref, theirs_ref, out_ref, buf_ref, sems):
    copies = fetch(mine_ref, theirs_ref, buf_ref, sems, at)
    first = first_ref[0] == 1
    count = buf_ref.shape[1] // 2
    heads = buf_ref.shape[0] // GROUPS
    rows = x_ref.shape[1] // 2
    total = jnp.zeros(out_ref.shape, f32)

    def in_place(x):
        parts = [jnp.zeros((sub, x.shape[1]), f32)] if sub else []
        parts.append(x)
        if sub + rows < count:
            parts.append(jnp.zeros((count - sub - rows, x.shape[1]), f32))
        return parts

    for g in range(GROUPS):
        copies[2 * g].wait()
        copies[2 * g + 1].wait()
        parts = []
        for h in range(g * heads, (g + 1) * heads):
            x = x_ref[h].astype(f32)
            low, high = x[:rows], x[rows:]
            parts += in_place(jnp.where(first, low, high)) + in_place(jnp.where(first, high, low))
        total = total + tn(jnp.concatenate(parts, axis=0).astype(bf), group_rows(buf_ref, g))
    out_ref[...] = total


def with_weights(kernel, first, ins, w_pair, count, out_shape, name):
    heads, _, width = w_pair[0].shape
    in_hbm = pl.BlockSpec(memory_space=pltpu.HBM)
    flops = 2 * heads * 2 * count * TB * width
    return pl.pallas_call(
        kernel,
        in_specs=[pl.BlockSpec(memory_space=pltpu.SMEM)] + [pl.BlockSpec(memory_space=pltpu.VMEM) for _ in ins] + [in_hbm, in_hbm],
        out_specs=pl.BlockSpec(memory_space=pltpu.VMEM),
        out_shape=out_shape,
        scratch_shapes=[pltpu.VMEM((heads, 2 * count, width), bf), pltpu.SemaphoreType.DMA((GROUPS, 2))],
        compiler_params=pltpu.CompilerParams(vmem_limit_bytes=58 * 2**20),
        cost_estimate=pl.CostEstimate(flops=flops, bytes_accessed=4 * heads * count * width, transcendentals=0),
        name=name,
    )(first, *ins, *w_pair)


def swap(value, axis, bit):
    count = lax.axis_size(axis)
    return lax.ppermute(value, axis, [(i, i ^ bit) for i in range(count)])


def shifted(value, axis, by):
    count = lax.axis_size(axis)
    pairs = [(i, i + by) for i in range(count) if 0 <= i + by < count]
    return lax.ppermute(value, axis, pairs)


def move(value, along_z, by):
    pairs = []
    for i in range(RINGS * RINGS):
        z, y = i // RINGS, i % RINGS
        to = (z + by) % RINGS * RINGS + y if along_z else z * RINGS + (y + by) % RINGS
        pairs.append((i, to))
    return lax.ppermute(value, "seq", pairs)


def around(x, along_z):
    return [x] + [move(x, along_z, -by) for by in FROM[1:]]


def home(parts, along_z):
    got = [parts[0]] + [move(parts[i], along_z, FROM[i]) for i in range(1, RINGS)]
    return [got[0], got[2], got[1], got[3]]


def float_sum(parts):
    first, *rest = [x.astype(f32) for x in parts]
    return first + rest[0] + rest[1] + rest[2]


def together(*values):
    return lax.optimization_barrier(values)


def scatter_heads(value):
    return lax.all_to_all(value, "seq", split_axis=0, concat_axis=0, tiled=True)


def angle_tables(places):
    quarter = HS // 4
    freqs = jnp.exp(-math.log(10000.0) * jnp.arange(quarter, dtype=f32) / quarter)
    grid_rows = (places // GRID_W).astype(f32)
    grid_cols = (places % GRID_W).astype(f32)
    angles = jnp.concatenate(
        [
            freqs[:, None] * grid_rows[None, :],
            freqs[:, None] * grid_cols[None, :],
            jnp.zeros((HALF - 2 * quarter, places.shape[0]), f32),
        ],
        axis=0,
    )
    return jnp.cos(angles), jnp.sin(angles)


def pad_rows(x, count):
    return jnp.pad(x, ((0, count - x.shape[0]), (0, 0)))


def arrange(w):
    qt = HS // 4
    parts = []
    for part in (w[0], w[1]):
        parts += [pad_rows(jnp.concatenate([part[0:qt], part[2 * qt : 3 * qt]]), HALF)]
        parts += [pad_rows(jnp.concatenate([part[qt : 2 * qt], part[3 * qt :]]), HALF)]
    return jnp.concatenate(parts + [pad_rows(w[2], HP)], axis=0)


def natural_order():
    qt = HS // 4
    order = []
    for at in (0, HP):
        for start in (at, at + HALF, at + qt, at + HALF + qt):
            order += range(start, start + qt)
    return order + list(range(2 * HP, 2 * HP + HS))


def rope(qa, qb, ka, kb, v, c, s):
    return jnp.concatenate([qa * c - qb * s, qa * s + qb * c, ka * c - kb * s, ka * s + kb * c, v], axis=-2).astype(bf)


def modulated_norm(hidden, shift_vec, scale_vec):
    centre = hidden - jnp.mean(hidden, axis=-1, keepdims=True)
    spread = jnp.mean(centre * centre, axis=-1, keepdims=True)
    return centre * lax.rsqrt(spread + norm_eps) * (1.0 + scale_vec) + shift_vec


def norm_back(hidden, scale_vec, grad):
    centre = hidden - jnp.mean(hidden, axis=-1, keepdims=True)
    inv = lax.rsqrt(jnp.mean(centre * centre, axis=-1, keepdims=True) + norm_eps)
    unit = centre * inv
    grad = grad * (1.0 + scale_vec)
    return inv * (grad - jnp.mean(grad, axis=-1, keepdims=True) - unit * jnp.mean(grad * unit, axis=-1, keepdims=True))


def half_rows(rows):
    return -(-rows // 16) * 8


def core_half(value, first):
    rows = value.shape[-2]
    half = half_rows(rows)
    low, high = value[..., :half, :], value[..., rows - half :, :]
    kept, given = jnp.where(first, low, high), jnp.where(first, high, low)
    return (kept.astype(f32) + swap(given, "dp", 1).astype(f32)).astype(bf)


def chip_sum(value):
    return (value.astype(f32) + swap(value, "dp", 2).astype(f32)).astype(bf)


def core_whole(total, other, first, rows):
    low, high = jnp.where(first, total, other), jnp.where(first, other, total)
    return jnp.concatenate([low, high[2 * total.shape[0] - rows :]], axis=0).astype(f32)


def local(streams, modulation, w_qkv, w_out, w_zero, pairing, positions, cotangent):
    on_main = lax.axis_index("section") == 1
    core = lax.axis_index("dp") % 2
    first = core == 0
    mods = modulation[0]
    pair_row = pairing[0]
    width = streams.shape[-1]
    qkv_w = [arrange(w_qkv[0, k, 0]) for k in range(2)]
    out_w = [pad_rows(w_out[0, k, 0], HP) for k in range(2)]

    def own_half(w):
        rows = w.shape[0] // 2
        return lax.dynamic_slice_in_dim(w, core * rows, rows, axis=0)

    def gather(x):
        return lax.all_gather(x, "seq", axis=0, tiled=False)

    def rows_of(w):
        return w.reshape(-1, width)

    def halves_of(x):
        rows = x.shape[1] // 2
        low, high = x[:, :rows], x[:, rows:]
        mine = jnp.where(first, low, high)
        theirs = jnp.where(first, high, low)
        return mine.reshape(-1, x.shape[2]), theirs.reshape(-1, x.shape[2])

    def to_heads(w_pair, x):
        mine, theirs = [nt(rows_of(w), x).reshape(w.shape[:2] + x.shape[:1]) for w in w_pair]
        return jnp.where(first, mine, theirs), jnp.where(first, theirs, mine)

    def from_heads(w_pair, x):
        mine, theirs = halves_of(x)
        return tn(mine, rows_of(w_pair[0])) + tn(theirs, rows_of(w_pair[1]))

    def with_other(x):
        return (x, swap(x, "dp", 1))

    cot = cotangent[0]
    through = nt(cot, w_zero[1])
    grad2 = jnp.where(on_main, cot.astype(f32), jnp.where(pair_row[1] == 1, through, 0.0))
    d_attn1 = (mods[1, 2] * grad2).astype(bf)
    hidden0 = streams[0, 0].astype(f32)
    normed0 = modulated_norm(hidden0, mods[0, 0], mods[0, 1]).astype(bf)
    cells = jnp.stack([positions // GRID_W, positions % GRID_W]).astype(bf)
    message = jnp.concatenate([normed0, jnp.pad(cells.T, ((0, 0), (0, TB - 2)))], axis=1)
    message = jnp.concatenate(around(message, False), axis=0)
    row_tokens = message[:, :width]
    row_cells = message[:, width : width + 2].astype(jnp.int32)
    row_places = row_cells[:, 0] * GRID_W + row_cells[:, 1]
    column_w = with_other(jnp.stack(around(own_half(qkv_w[0]), True)))
    low, high = to_heads(column_w, row_tokens)
    qkv0 = rope(low[:, :HALF], low[:, HALF:HP], low[:, HP:], high[:, :HALF], high[:, HALF:], *angle_tables(row_places))
    pieces = home(qkv0, True)
    at = lax.axis_index("seq")
    at_z, at_y = at // RINGS, at % RINGS
    places = jnp.stack([(at_z + z) % RINGS * RINGS + (at_y + y) % RINGS for z in FROM for y in FROM]).astype(jnp.int32)

    cells = jnp.pad(cells, ((0, 6), (0, width - cells.shape[1])))
    piece_1 = gather(jnp.concatenate([own_half(qkv_w[1]), cells, own_half(out_w[0]), own_half(out_w[1])], axis=0))
    pieces, d_attn1 = together(pieces, d_attn1)
    qkv0, mixed0, log_sums0 = attn_fwd(pieces, places)
    mixed0_own = scatter_heads(mixed0)
    piece_1, mixed0_own = lax.optimization_barrier((piece_1, mixed0_own))
    cut = 3 * HP // 2 + 8
    full_1 = with_other(piece_1)
    cells_all = piece_1[:, 3 * HP // 2 : 3 * HP // 2 + 2, :TB].astype(jnp.int32)
    cos_all, sin_all = angle_tables((cells_all[:, 0] * GRID_W + cells_all[:, 1]).reshape(-1))
    cos_own, sin_own = angle_tables(positions)

    first_flag = jnp.where(first, 1, 0).astype(jnp.int32).reshape(1)
    heads = lax.axis_size("seq")

    def to_mixed(block, d_attn):
        kernel = functools.partial(grad_in_kernel, cut, block * HALF)
        shape = jax.ShapeDtypeStruct((heads, HP, TB), bf)
        return with_weights(kernel, first_flag, (d_attn,), full_1, HP, shape, "to_mixed")

    def from_mixed(block, mixed):
        kernel = functools.partial(sum_kernel, cut, block * HALF)
        shape = jax.ShapeDtypeStruct((TB, width), f32)
        return with_weights(kernel, first_flag, (mixed,), full_1, HP, shape, "from_mixed")

    normed0, mixed0_own = together(normed0, mixed0_own)
    normed0_all = gather(normed0)

    d_mixed1 = scatter_heads(to_mixed(1, d_attn1))
    attn0 = from_mixed(0, mixed0_own)
    hidden1 = hidden0 + mods[0, 2] * attn0
    zero0 = shifted(nn(hidden1.astype(bf), w_zero[0]).astype(bf), "section", 1).astype(f32)
    hidden1 = hidden1 + jnp.where(pair_row[0] == 0, zero0, 0.0)

    normed1 = modulated_norm(hidden1, mods[1, 0], mods[1, 1]).astype(bf)
    shape = jax.ShapeDtypeStruct((heads, 3 * HP, TB), bf)
    ins = (normed1, cos_own, sin_own)
    qkv1 = with_weights(functools.partial(qkv_kernel, 0), first_flag, ins, full_1, cut, shape, "to_qkv")
    qkv1, d_mixed1, second = together(qkv1, d_mixed1, jnp.concatenate([normed1, d_attn1], axis=0))
    qkv1 = scatter_heads(qkv1)
    second_all = gather(second)
    mixed1, d_raw1 = attn_both(qkv1, d_mixed1, cos_all, sin_all)
    order = natural_order()
    plain = list(range(HS))
    d_raw1_own, mixed1_out = together(scatter_heads(d_raw1), mixed1)
    mixed1_own = scatter_heads(mixed1_out)
    shape = jax.ShapeDtypeStruct((TB, width), f32)
    ins = (d_raw1_own,)
    d_normed1 = with_weights(functools.partial(sum_kernel, 0, 0), first_flag, ins, full_1, cut, shape, "from_qkv")
    grad1 = grad2 + norm_back(hidden1, mods[1, 1], d_normed1)

    sent = shifted(grad1.astype(bf), "section", -1)
    sent, mixed1_own = together(sent, mixed1_own)
    picked = jnp.where(pair_row[0] == 0, sent, cot)
    picked = jnp.where(on_main, jnp.zeros_like(picked), picked)
    grad1 = grad1 + nt(picked, w_zero[0])
    d_attn0 = (mods[0, 2] * grad1).astype(bf)
    d_mixed0 = to_mixed(0, d_attn0)
    d_attn0_all = gather(d_attn0)

    mixed1_own, d_mixed0 = together(mixed1_own, d_mixed0)
    attn1 = from_mixed(1, mixed1_own)
    hidden2 = hidden1 + mods[1, 2] * attn1
    zero1 = nn(hidden2.astype(bf), w_zero[1]).astype(bf)
    d_mixed0, zero1 = together(scatter_heads(d_mixed0), zero1)
    zero1 = shifted(zero1, "section", 1)

    d_raw0_rings, d_raw0 = attn_bwd(qkv0, d_mixed0, mixed0, log_sums0, cos_all, sin_all, places)
    d_raw0_rings, d_raw1, mixed1 = together(d_raw0_rings, d_raw1, mixed1)

    homed = home(d_raw0_rings, True)
    grads = [
        weight_grad(order, d_raw0, normed0_all, 0),
        weight_grad(order, d_raw1, second_all, 0),
        weight_grad(plain, mixed1, second_all, 1),
    ]
    homed, grads, zero1 = together(homed, grads, zero1)

    zero1 = zero1.astype(f32)
    hidden2 = hidden2 + jnp.where(pair_row[0] == 1, zero0, 0.0) + jnp.where(pair_row[1] == 1, zero1, 0.0)
    final_out = hidden2.astype(bf)[None, None]

    d_row0 = from_heads(column_w, jnp.stack(homed)).astype(bf).reshape(RINGS, -1, width)
    grads, d_row0, mixed0 = together(core_half(jnp.concatenate(grads, axis=0), first), d_row0, mixed0)
    d_row0, grads = together(home(d_row0, False), chip_sum(grads))
    grad0 = grad1 + norm_back(hidden0, mods[0, 1], float_sum(d_row0))
    rows = len(order)
    grads = core_whole(grads, swap(grads, "dp", 1), first, 2 * rows + HS)
    out_grad0 = weight_grad(plain, mixed0, d_attn0_all, 0)
    out_grad0 = (out_grad0.astype(f32) + swap(out_grad0, "dp", 1).astype(f32)).astype(bf)
    out_grad0 = chip_sum(out_grad0).astype(f32)
    grad_qkv = grads[: 2 * rows].reshape(1, 2, 1, 3, HS, width)
    grad_out = jnp.stack([out_grad0, grads[2 * rows :]])[None, :, None]
    return (final_out, grad0[None, None], grad_qkv, grad_out)


def solution(mesh):
    in_specs = (
        P("section", "dp", "seq", None),
        P("section", None, None, None),
        P("section", None, "seq", None, None, None),
        P("section", None, "seq", None, None),
        P(),
        P("dp", None),
        P("seq"),
        P("dp", "seq", None),
    )
    out_specs = (
        P("section", "dp", "seq", None),
        P("section", "dp", "seq", None),
        P("section", None, "seq", None, None, None),
        P("section", None, "seq", None, None),
    )
    return jax.shard_map(local, mesh=mesh, in_specs=in_specs, out_specs=out_specs, check_vma=False)
```
